512 devices in a mesh: frame: 32 (over x_lo, z), atom: 16 (over y, x_hi, core).
Axes of the slice: x: 4 (x_hi: 2, x_lo: 2; x = x_hi * 2 + x_lo), y: 4, z: 16, core: 2. Of those that a mesh axis runs over, the one named last changes fastest.
Arguments:
- coords: float32 [3, 1536, 8192], P(None, 'frame', 'atom'), may hold values from -45 to 45
- weights: int32 [8192], P('atom'), may hold values from 1 to 32
Outputs:
- msd: float32 [1536, 1536], P('frame', 'atom')
The draws below stay inside these ranges and needn't reach their ends.
All inputs are finite; a program needn't handle non-finite values.
Results may differ from the reference program's by a relative error of at most 0.0003.
Values sent between devices are 32-bit elements; how exact they have to be, the bound alone decides.
No kernel may reach another device: no remote copies, remote signals or barrier semaphores. Data moves between devices by JAX's collectives and lax.ppermute only.
A program may use at most 64 MiB of HBM per device.

```python
import math
import jax
import jax.numpy as jnp
from jax import lax

NEWTON = 3
FRAMES = 1536
ATOMS = 8192


def draw_coords(key, part):
    key = jax.random.fold_in(key, 11)
    keys = jax.random.split(key, 6)
    base = jax.random.truncated_normal(keys[0], -3.0, 3.0, (3, 1, ATOMS), jnp.float32) * 4.0
    frame_scale = jnp.exp(jax.random.uniform(keys[1], (1, FRAMES, 1), jnp.float32, math.log(0.3), math.log(1.2)))
    atom_scale = jnp.exp(jax.random.uniform(keys[2], (1, 1, ATOMS), jnp.float32, math.log(0.5), math.log(2.0)))
    noise = jax.random.truncated_normal(keys[3], -3.0, 3.0, (3, FRAMES, ATOMS), jnp.float32)
    posed = base + noise * frame_scale * atom_scale
    quat = jax.random.normal(keys[4], (4, FRAMES), jnp.float32)
    quat = quat / jnp.sqrt(jnp.sum(quat * quat, axis=0) + 1e-06)
    qw, qx, qy, qz = (quat[0], quat[1], quat[2], quat[3])
    rot = [[1.0 - 2.0 * (qy * qy + qz * qz), 2.0 * (qx * qy - qw * qz), 2.0 * (qx * qz + qw * qy)], [2.0 * (qx * qy + qw * qz), 1.0 - 2.0 * (qx * qx + qz * qz), 2.0 * (qy * qz - qw * qx)], [2.0 * (qx * qz - qw * qy), 2.0 * (qy * qz + qw * qx), 1.0 - 2.0 * (qx * qx + qy * qy)]]
    offset = jax.random.truncated_normal(keys[5], -3.0, 3.0, (3, FRAMES), jnp.float32) * 3.0
    moved = [rot[k][0][:, None] * posed[0] + rot[k][1][:, None] * posed[1] + rot[k][2][:, None] * posed[2] + offset[k][:, None] for k in range(3)]
    return jnp.stack(moved, axis=0).astype(jnp.float32)


def set_ends(drawn, stream_key, smallest, top_value):
    extent = drawn.shape
    spot = [jax.random.randint(jax.random.fold_in(stream_key, axis), (), 0, extent[axis]) for axis in range(len(extent))]
    drawn = drawn.at[tuple(spot)].set(smallest)
    longest = extent.index(max(extent))
    spot[longest] = (spot[longest] + 1) % extent[longest]
    return drawn.at[tuple(spot)].set(top_value)


def setup_inputs(seed: int = 0) -> dict:
    key_of = jax.random.split(jax.random.key(seed), 3)
    return {
        "coords": draw_coords(jax.random.fold_in(key_of[2], 71), 0),
        "weights": set_ends(jax.random.randint(key_of[1], (ATOMS,), 1, 33), jax.random.fold_in(key_of[1], 1), 1, 32).astype(jnp.int32),
    }


def det_four(rows):
    a00, a01, a02, a03 = rows[0]
    a10, a11, a12, a13 = rows[1]
    a20, a21, a22, a23 = rows[2]
    a30, a31, a32, a33 = rows[3]
    s0 = a00 * a11 - a10 * a01
    s1 = a00 * a12 - a10 * a02
    s2 = a00 * a13 - a10 * a03
    s3 = a01 * a12 - a11 * a02
    s4 = a01 * a13 - a11 * a03
    s5 = a02 * a13 - a12 * a03
    t5 = a22 * a33 - a32 * a23
    t4 = a21 * a33 - a31 * a23
    t3 = a21 * a32 - a31 * a22
    t2 = a20 * a33 - a30 * a23
    t1 = a20 * a32 - a30 * a22
    t0 = a20 * a31 - a30 * a21
    return s0 * t5 - s1 * t4 + s2 * t3 + s3 * t2 - s4 * t1 + s5 * t0


def quaternion_fit(moment, spread_rows, spread_cols):
    sxx, sxy, sxz, syx, syy, syz, szx, szy, szz = [moment[k] for k in range(9)]
    coef_two = -2.0 * jnp.sum(moment * moment, axis=0)
    det_three = sxx * (syy * szz - syz * szy) - sxy * (syx * szz - syz * szx) + sxz * (syx * szy - syy * szx)
    coef_one = -8.0 * det_three
    rows = [[sxx + syy + szz, syz - szy, szx - sxz, sxy - syx],
            [syz - szy, sxx - syy - szz, sxy + syx, szx + sxz],
            [szx - sxz, sxy + syx, -sxx + syy - szz, syz + szy],
            [sxy - syx, szx + sxz, syz + szy, -sxx - syy + szz]]
    coef_zero = det_four(rows)
    lam = 0.5 * (spread_rows + spread_cols)
    for turn in range(NEWTON):
        square = lam * lam
        value = (square + coef_two) * square + coef_one * lam + coef_zero
        slope = 4.0 * square * lam + 2.0 * coef_two * lam + coef_one
        lam = lam - value / slope
    return spread_rows + spread_cols - 2.0 * lam


def reference(coords, weights):
    mass = weights.astype(jnp.float32)
    total = jnp.sum(mass)
    centroid = jnp.sum(coords * mass, axis=2) / total
    centered = coords - centroid[:, :, None]
    spread = jnp.sum(mass * centered * centered, axis=(0, 2)) / total
    moment = jnp.einsum("cia,dja->cdij", centered * mass, centered, precision=lax.Precision.HIGHEST)
    moment = moment.reshape(9, FRAMES, FRAMES) / total
    return quaternion_fit(moment, spread[:, None], spread[None, :])
```

```python
import functools

import jax
import jax.numpy as jnp
import numpy as np
from jax import lax
from jax.experimental import pallas as pl
from jax.experimental.pallas import tpu as pltpu
from jax.sharding import PartitionSpec as P

NEWTON = 3
ROWS = 48
SIDE = 16
EXACT = lax.Precision.HIGHEST
VMEM_LIMIT = 40 * 1024 * 1024

OWN = (0, -2, -3, 4, 5)
OTHER = (0, -2, -3)
EARLY = (
    (2, 1), (1, 0), (2, 0), (0, 3), (1, 3), (2, 3),
    (1, 7), (0, 6), (0, 7), (3, 5), (3, 6), (3, 7),
)
LATE = ((0, 4), (4, 5), (2, 7), (2, 4))


def frame_block(column, z, index):
    if index < len(OWN):
        return column * SIDE + (z + OWN[index]) % SIDE
    return (1 - column) * SIDE + (z + OTHER[index - len(OWN)]) % SIDE


def routes():
    ends = []
    for column in range(2):
        for z in range(SIDE):
            for slot, (p, q) in enumerate(EARLY + LATE):
                if slot == len(EARLY) + 2 and column == 1:
                    p = 4
                a, b = frame_block(column, z, p), frame_block(column, z, q)
                if slot == len(EARLY) + 3 and z >= SIDE // 2:
                    ends.append(((a, a), (b, b)))
                else:
                    ends.append(((a, b), (b, a)))
    place = lambda end: end[0] * SIDE + end[1] // 2
    at = {}
    for device, pair in enumerate(ends):
        for which, end in enumerate(pair):
            at.setdefault(place(end), []).append((device, which))
    assert len(at) == len(ends) and all(len(v) == 2 for v in at.values())
    swapped = [None] * len(ends)
    for seed in range(len(ends)):
        device, enter = seed, 0
        while swapped[device] is None:
            swapped[device] = enter
            node = place(ends[device][1 - enter])
            device, enter = [e for e in at[node] if e != (device, 1 - enter)][0]
    first = [place(ends[d][swapped[d]]) for d in range(len(ends))]
    second = [place(ends[d][1 - swapped[d]]) for d in range(len(ends))]
    assert len(set(first)) == len(set(second)) == len(ends)
    half = [0] * len(ends)
    for d in range(len(ends)):
        half[first[d]] = ends[d][swapped[d]][1] % 2
        assert ends[d][1 - swapped[d]][1] % 2 == 1 - half[first[d]] or second[d] != first[d]
    return first, second, swapped, half


def lookup(step, values):
    out = jnp.int32(values[0])
    for k, value in enumerate(values):
        out = jnp.where(step == k, jnp.int32(value), out)
    return out


def iota(shape, axis):
    return lax.broadcasted_iota(jnp.int32, shape, axis)


def dot_t(a, b):
    return lax.dot_general(a, b, (((1,), (1,)), ((), ())), precision=EXACT, preferred_element_type=jnp.float32)


def stage(block, mass, slot, centered, weighted, feature):
    x = block[...]
    local = jnp.sum(mass)
    mean = jnp.sum(x * mass, axis=1, keepdims=True) / local
    x = x - mean
    wx = x * mass
    square = jnp.sum(wx * x, axis=1, keepdims=True)
    centered[slot, : 3 * ROWS] = x
    centered[slot, 3 * ROWS :] = jnp.zeros((256 - 3 * ROWS, x.shape[1]), jnp.float32)
    weighted[slot] = wx
    lane = iota((ROWS, 128), 1)
    square = square[:ROWS] + square[ROWS : 2 * ROWS] + square[2 * ROWS :]
    row, column = jnp.zeros((ROWS, 128), jnp.float32), jnp.zeros((ROWS, 128), jnp.float32)
    for c in range(3):
        part = mean[c * ROWS : (c + 1) * ROWS]
        row = jnp.where(lane == 48 + c, part, row)
        column = jnp.where(lane == 52 + c, part, column)
    row = jnp.where(lane == 51, local, row)
    row = jnp.where(lane == 56, square, row)
    column = jnp.where(lane == 57, square, column)
    feature[slot, 0] = row
    feature[slot, 1] = column


def rest_of(tail):
    return tail[:ROWS] + pltpu.roll(tail[ROWS : 2 * ROWS], 16, 1) + pltpu.roll(tail[2 * ROWS :], 32, 1)


def put_pair(out, slot, product, feature, p, q):
    out[slot, : 3 * ROWS] = product[:, :128]
    out[slot, 3 * ROWS :] = rest_of(product[:, 128:]) + feature[p, 0] + feature[q, 1]


def early_kernel(mass_ref, *refs):
    blocks, (out, centered, weighted, feature) = refs[:7], refs[7:]
    mass = mass_ref[...]
    index = (0, 1, 2, 3, 5, 6, 7)
    for k, block in enumerate(blocks):
        stage(block, mass, k, centered, weighted, feature)
    rows = [index.index(p) for p, _ in EARLY]
    columns = [index.index(q) for _, q in EARLY]

    def body(step, carry):
        p, q = lookup(step, rows), lookup(step, columns)
        put_pair(out, step, dot_t(weighted[p], centered[q]), feature, p, q)
        return carry

    lax.fori_loop(0, len(EARLY), body, 0)


def late_kernel(flags, mass_ref, *refs):
    blocks, (_, out, centered, weighted, feature) = refs[:5], refs[5:]
    mass = mass_ref[...]
    index = (0, 2, 4, 5, 7)
    for k, block in enumerate(blocks):
        stage(block, mass, k, centered, weighted, feature)
    column, diagonal = flags[0], flags[1]
    rows = [index.index(p) for p, _ in LATE]
    columns = [index.index(q) for _, q in LATE]

    def body(step, carry):
        p, q = lookup(step, rows), lookup(step, columns)
        p = jnp.where((step == 2) & (column == 1), jnp.int32(index.index(4)), p)
        put_pair(out, step, dot_t(weighted[p], centered[q]), feature, p, q)
        return carry

    lax.fori_loop(0, len(LATE), body, 0)

    @pl.when(diagonal == 1)
    def _():
        p, q = rows[3], columns[3]
        upper, lower = dot_t(weighted[p], centered[p]), dot_t(weighted[q], centered[q])
        i, j = iota((3 * ROWS, 256), 0) % ROWS, iota((3 * ROWS, 256), 1) % ROWS
        product = jnp.where(i <= j, upper, lower)
        put_pair(out, 3, product, feature, p, q)
        lane = iota((ROWS, 128), 1)
        on = jnp.where(i == j, lower, 0.0)
        ends = jnp.zeros((ROWS, 128), jnp.float32)
        at = iota((ROWS, 256), 1)
        for c in range(3):
            mine = on[c * ROWS : (c + 1) * ROWS]
            for d in range(3):
                inside = (at >= d * ROWS) & (at < (d + 1) * ROWS)
                value = jnp.sum(jnp.where(inside, mine, 0.0), axis=1, keepdims=True)
                ends = jnp.where(lane == 64 + 3 * c + d, value, ends)
        out[3, 3 * ROWS :] += ends


def det_four(rows):
    a00, a01, a02, a03 = rows[0]
    a10, a11, a12, a13 = rows[1]
    a20, a21, a22, a23 = rows[2]
    a30, a31, a32, a33 = rows[3]
    s0 = a00 * a11 - a10 * a01
    s1 = a00 * a12 - a10 * a02
    s2 = a00 * a13 - a10 * a03
    s3 = a01 * a12 - a11 * a02
    s4 = a01 * a13 - a11 * a03
    s5 = a02 * a13 - a12 * a03
    t5 = a22 * a33 - a32 * a23
    t4 = a21 * a33 - a31 * a23
    t3 = a21 * a32 - a31 * a22
    t2 = a20 * a33 - a30 * a23
    t1 = a20 * a32 - a30 * a22
    t0 = a20 * a31 - a30 * a21
    return s0 * t5 - s1 * t4 + s2 * t3 + s3 * t2 - s4 * t1 + s5 * t0


def quaternion_fit(moment, spread_rows, spread_cols):
    sxx, sxy, sxz, syx, syy, syz, szx, szy, szz = moment
    coef_two = -2.0 * sum(m * m for m in moment)
    det_three = (
        sxx * (syy * szz - syz * szy)
        - sxy * (syx * szz - syz * szx)
        + sxz * (syx * szy - syy * szx)
    )
    coef_one = -8.0 * det_three
    rows = [
        [sxx + syy + szz, syz - szy, szx - sxz, sxy - syx],
        [syz - szy, sxx - syy - szz, sxy + syx, szx + sxz],
        [szx - sxz, sxy + syx, -sxx + syy - szz, syz + szy],
        [sxy - syx, szx + sxz, syz + szy, -sxx - syy + szz],
    ]
    coef_zero = det_four(rows)
    lam = 0.5 * (spread_rows + spread_cols)
    for turn in range(NEWTON):
        square = lam * lam
        value = (square + coef_two) * square + coef_one * lam + coef_zero
        slope = 4.0 * square * lam + 2.0 * coef_two * lam + coef_one
        lam = lam - value / slope
    return spread_rows + spread_cols - 2.0 * lam


def square_tile(x):
    return jnp.concatenate([x, jnp.zeros((128 - x.shape[0], 128), jnp.float32)], axis=0)


def fit_kernel(flags, parts, first, second):
    diagonal, swap = flags[1] == 1, flags[2] == 1
    total = parts[0]
    for a in range(1, SIDE):
        total = total + parts[a]
    lane, row = iota((ROWS, 128), 1), iota((ROWS, 128), 0)
    rest = total[3 * ROWS :]

    gathered = jnp.zeros((ROWS, 128), jnp.float32)
    for a in range(SIDE):
        tile = jnp.where((lane >= 48) & (lane < 56), parts[a, 3 * ROWS :], 0.0)
        gathered = gathered + pltpu.roll(tile, (8 * a - 48) % 128, 1)

    def per_sender(which):
        pick = (iota((128, 128), 0) == 8 * iota((128, 128), 1) + which).astype(jnp.float32)
        return jnp.dot(gathered, pick, precision=EXACT, preferred_element_type=jnp.float32)

    mass = per_sender(3)
    whole = jnp.sum(mass, axis=1, keepdims=True)

    def offsets(base):
        out = []
        for c in range(3):
            mean = per_sender(base + c)
            centroid = jnp.sum(mass * mean, axis=1, keepdims=True) / whole
            out.append(jnp.where(lane < SIDE, mean - centroid, 0.0))
        return out

    off_p, off_q = offsets(0), offsets(4)

    def spread(off, at):
        within = jnp.sum(jnp.where(lane == at, rest, 0.0), axis=1, keepdims=True)
        between = jnp.sum(mass * sum(o * o for o in off), axis=1, keepdims=True)
        return (within + between) / whole

    spread_p, spread_q = spread(off_p, 56), spread(off_q, 57)

    def as_row(column):
        return jnp.sum(jnp.where(row == lane, column, 0.0), axis=0, keepdims=True)

    upper = row <= lane
    corner = lane == ROWS
    row_p, row_q = as_row(spread_p), as_row(spread_q)
    spread_rows = jnp.where(upper, spread_p, jnp.where(diagonal, spread_q, spread_p))
    spread_cols = jnp.where(upper, jnp.where(diagonal, row_p, row_q), row_q)
    spread_rows = jnp.where(corner, spread_q, spread_rows)
    spread_cols = jnp.where(corner, spread_q, spread_cols)

    low_rows = jnp.concatenate([mass * jnp.where(diagonal, q, p) for p, q in zip(off_p, off_q)], axis=0)
    up_rows = jnp.concatenate([mass * p for p in off_p], axis=0)
    moment = []
    between = []
    for d in range(3):
        up = dot_t(up_rows, square_tile(jnp.where(diagonal, off_p[d], off_q[d])))
        low = dot_t(low_rows, square_tile(off_q[d]))
        between.append((up, low))
    for c in range(3):
        main = total[c * ROWS : (c + 1) * ROWS]
        tail = pltpu.roll(rest, (32 - 16 * c) % 128, 1)
        shifted = [main, pltpu.roll(main, 128 - 48, 1), jnp.where(lane < 32, pltpu.roll(main, 128 - 96, 1), tail)]
        for d in range(3):
            up, low = (b[c * ROWS : (c + 1) * ROWS] for b in between[d])
            value = shifted[d] + jnp.where(upper, up, low)
            end = jnp.sum(jnp.where(lane == 64 + 3 * c + d, rest, 0.0), axis=1, keepdims=True)
            end = end + jnp.sum(mass * off_q[c] * off_q[d], axis=1, keepdims=True)
            moment.append(jnp.where(corner, end, value) / whole)
    msd = quaternion_fit(moment, spread_rows, spread_cols)
    corner_value = jnp.sum(jnp.where(corner, msd, 0.0), axis=1, keepdims=True)
    msd = jnp.where(lane < ROWS, msd, 0.0)
    turned = square_tile(msd).T[:ROWS]
    plain_a = jnp.where(diagonal, jnp.where(upper, msd, turned), msd)
    mirrored = jnp.where(row > lane, msd, jnp.where(row == lane, corner_value, turned))
    plain_b = jnp.where(diagonal, mirrored, turned)
    first[...] = jnp.where(swap, plain_b, plain_a)
    second[...] = jnp.where(swap, plain_a, plain_b)


def join_kernel(flags, first, second, out):
    lane = iota((ROWS, 128), 1)
    a, b = first[...], second[...]
    left = jnp.where(flags[3] == 1, b, a)
    right = jnp.where(flags[3] == 1, a, b)
    out[...] = jnp.where(lane < ROWS, left, pltpu.roll(right, ROWS, 1))[:, : 2 * ROWS]


def on_device(coords, weights):
    first, second, swapped, half = routes()
    frame, atom = lax.axis_index("frame"), lax.axis_index("atom")
    place = frame * SIDE + atom
    last = (atom == SIDE - 1).astype(jnp.int32)
    column, z = frame // SIDE, frame % SIDE
    late_diagonal = (z >= SIDE // 2).astype(jnp.int32)
    table = jnp.asarray(np.array(swapped) + 2 * np.array(half), jnp.int32)[place]
    build_flags = jnp.stack([column, late_diagonal]).astype(jnp.int32)
    fit_flags = jnp.stack([column, late_diagonal * last, table % 2, table // 2]).astype(jnp.int32)
    mass = weights.astype(jnp.float32)[None, :]

    def along(block, distance):
        route = [
            (c * SIDE + (k + distance) % SIDE, c * SIDE + k) for c in range(2) for k in range(SIDE)
        ]
        return lax.ppermute(block, "frame", route)

    def across(block):
        return lax.ppermute(block, "frame", [((f + SIDE) % (2 * SIDE), f) for f in range(2 * SIDE)])

    own = coords.reshape(3 * ROWS, coords.shape[2])
    plus4 = along(own, 4)
    minus2 = along(own, -2)
    other0 = across(own)
    minus3 = along(minus2, -1)
    other2 = across(minus2)
    other3 = across(minus3)
    plus5 = along(plus4, 1)

    atoms = own.shape[1]
    slots = len(EARLY) + len(LATE)
    result = jax.ShapeDtypeStruct((slots, 4 * ROWS, 128), jnp.float32)

    def scratch(n):
        return [
            pltpu.VMEM((n, 256, atoms), jnp.float32),
            pltpu.VMEM((n, 3 * ROWS, atoms), jnp.float32),
            pltpu.VMEM((n, 2, ROWS, 128), jnp.float32),
        ]

    smem = pl.BlockSpec(memory_space=pltpu.SMEM)
    params = pltpu.CompilerParams(vmem_limit_bytes=VMEM_LIMIT)
    whole = lambda *shape: pl.BlockSpec(shape, lambda i: (0,) * len(shape))
    block_spec = whole(3 * ROWS, atoms)
    pair_flops = 2 * 3 * ROWS * 256 * atoms * 6
    partial = pl.pallas_call(
        early_kernel,
        grid=(1,),
        out_shape=result,
        in_specs=[whole(1, atoms)] + [block_spec] * 7,
        out_specs=whole(len(EARLY), 4 * ROWS, 128),
        scratch_shapes=scratch(7),
        compiler_params=params,
        cost_estimate=pl.CostEstimate(flops=12 * pair_flops, bytes_accessed=4_000_000, transcendentals=0),
    )(mass, own, minus2, minus3, plus4, other0, other2, other3)
    partial = pl.pallas_call(
        late_kernel,
        grid=(1,),
        out_shape=result,
        in_specs=[smem, whole(1, atoms)] + [block_spec] * 5 + [pl.BlockSpec(memory_space=pl.ANY)],
        out_specs=pl.BlockSpec((len(LATE), 4 * ROWS, 128), lambda i: (len(EARLY) // len(LATE), 0, 0)),
        scratch_shapes=scratch(5),
        input_output_aliases={7: 0},
        compiler_params=params,
        cost_estimate=pl.CostEstimate(flops=6 * pair_flops, bytes_accessed=2_000_000, transcendentals=0),
    )(build_flags, mass, own, minus3, plus5, other0, other3, partial)

    parts = lax.all_to_all(partial, "atom", 0, 0, tiled=True)

    block = jax.ShapeDtypeStruct((ROWS, 128), jnp.float32)
    vmem = pl.BlockSpec(memory_space=pltpu.VMEM)
    one, two = pl.pallas_call(
        fit_kernel,
        out_shape=(block, block),
        in_specs=[smem, vmem],
        out_specs=(vmem, vmem),
        compiler_params=params,
    )(fit_flags, parts)
    one = lax.ppermute(one, ("frame", "atom"), list(enumerate(first)))
    two = lax.ppermute(two, ("frame", "atom"), list(enumerate(second)))
    return pl.pallas_call(
        join_kernel,
        out_shape=jax.ShapeDtypeStruct((ROWS, 2 * ROWS), jnp.float32),
        in_specs=[smem, vmem, vmem],
        out_specs=vmem,
        compiler_params=params,
    )(fit_flags, one, two)


def solution(mesh):
    placed = (P(None, "frame", "atom"), P("atom"))
    return jax.shard_map(
        on_device, mesh=mesh, in_specs=placed, out_specs=P("frame", "atom"), check_vma=False
    )
```

```python
import functools

import jax
import jax.numpy as jnp
import numpy as np
from jax import lax
from jax.experimental import pallas as pl
from jax.experimental.pallas import tpu as pltpu
from jax.sharding import PartitionSpec as P

NEWTON = 3
ROWS = 48
SIDE = 16
EXACT = lax.Precision.HIGHEST
VMEM_LIMIT = 40 * 1024 * 1024

OWN = (0, -1, -3, 4, 5)
OTHER = (0, -1, -3)
EARLY = (
    (1, 0), (2, 1), (2, 0), (0, 3), (1, 3), (2, 3),
    (0, 6), (1, 7), (0, 7), (3, 5), (3, 6), (3, 7),
)
LATE = ((1, 4), (4, 6), (2, 7), (2, 4))


def frame_block(column, z, index):
    if index < len(OWN):
        return column * SIDE + (z + OWN[index]) % SIDE
    return (1 - column) * SIDE + (z + OTHER[index - len(OWN)]) % SIDE


def routes():
    ends = []
    for column in range(2):
        for z in range(SIDE):
            for slot, (p, q) in enumerate(EARLY + LATE):
                if slot == len(EARLY) + 2 and column == 1:
                    p = 4
                a, b = frame_block(column, z, p), frame_block(column, z, q)
                if slot == len(EARLY) + 3 and z >= SIDE // 2:
                    ends.append(((a, a), (b, b)))
                else:
                    ends.append(((a, b), (b, a)))
    place = lambda end: end[0] * SIDE + end[1] // 2
    at = {}
    for device, pair in enumerate(ends):
        for which, end in enumerate(pair):
            at.setdefault(place(end), []).append((device, which))
    assert len(at) == len(ends) and all(len(v) == 2 for v in at.values())
    swapped = [None] * len(ends)
    for seed in range(len(ends)):
        device, enter = seed, 0
        while swapped[device] is None:
            swapped[device] = enter
            node = place(ends[device][1 - enter])
            device, enter = [e for e in at[node] if e != (device, 1 - enter)][0]
    first = [place(ends[d][swapped[d]]) for d in range(len(ends))]
    second = [place(ends[d][1 - swapped[d]]) for d in range(len(ends))]
    assert len(set(first)) == len(set(second)) == len(ends)
    half = [0] * len(ends)
    for d in range(len(ends)):
        half[first[d]] = ends[d][swapped[d]][1] % 2
        assert ends[d][1 - swapped[d]][1] % 2 == 1 - half[first[d]] or second[d] != first[d]
    return first, second, swapped, half


def lookup(step, values):
    out = jnp.int32(values[0])
    for k, value in enumerate(values):
        out = jnp.where(step == k, jnp.int32(value), out)
    return out


def iota(shape, axis):
    return lax.broadcasted_iota(jnp.int32, shape, axis)


def dot_t(a, b):
    return lax.dot_general(a, b, (((1,), (1,)), ((), ())), precision=EXACT, preferred_element_type=jnp.float32)


def product(a, b):
    return lax.dot_general(a, b, (((1,), (1,)), ((), ())), preferred_element_type=jnp.float32)


def halves(x):
    high = x.astype(jnp.bfloat16)
    return high, (x - high.astype(jnp.float32)).astype(jnp.bfloat16)


def stage(block, mass, slot, centered, weighted, feature):
    x = block[...]
    atoms = x.shape[1]
    local = jnp.sum(mass)
    mean = jnp.sum(x * mass, axis=1, keepdims=True) / local
    x = x - mean
    wx = x * mass
    square = jnp.sum(wx * x, axis=1, keepdims=True)
    high, low = halves(x)
    for k, part in enumerate((high, low, high)):
        centered[slot, : 3 * ROWS, k * atoms : (k + 1) * atoms] = part
    centered[slot, 3 * ROWS :] = jnp.zeros((256 - 3 * ROWS, 3 * atoms), jnp.bfloat16)
    high, low = halves(wx)
    for k, part in enumerate((high, high, low)):
        weighted[slot, :, k * atoms : (k + 1) * atoms] = part
    lane = iota((ROWS, 128), 1)
    square = square[:ROWS] + square[ROWS : 2 * ROWS] + square[2 * ROWS :]
    row, column = jnp.zeros((ROWS, 128), jnp.float32), jnp.zeros((ROWS, 128), jnp.float32)
    for c in range(3):
        part = mean[c * ROWS : (c + 1) * ROWS]
        row = jnp.where(lane == 48 + c, part, row)
        column = jnp.where(lane == 52 + c, part, column)
    row = jnp.where(lane == 51, local, row)
    row = jnp.where(lane == 56, square, row)
    column = jnp.where(lane == 57, square, column)
    feature[slot, 0] = row
    feature[slot, 1] = column


def rest_of(tail):
    return tail[:ROWS] + pltpu.roll(tail[ROWS : 2 * ROWS], 16, 1) + pltpu.roll(tail[2 * ROWS :], 32, 1)


def put_pair(out, slot, value, feature, p, q):
    out[slot, : 3 * ROWS] = value[:, :128]
    out[slot, 3 * ROWS :] = rest_of(value[:, 128:]) + feature[p, 0] + feature[q, 1]


def early_kernel(mass_ref, *refs):
    blocks, (out, centered, weighted, feature) = refs[:7], refs[7:]
    mass = mass_ref[...].astype(jnp.float32)
    index = (0, 1, 2, 3, 5, 6, 7)
    for k, block in enumerate(blocks):
        stage(block, mass, k, centered, weighted, feature)
    rows = [index.index(p) for p, _ in EARLY]
    columns = [index.index(q) for _, q in EARLY]

    def body(step, carry):
        p, q = lookup(step, rows), lookup(step, columns)
        put_pair(out, step, product(weighted[p], centered[q]), feature, p, q)
        return carry

    lax.fori_loop(0, len(EARLY), body, 0)


def late_kernel(flags, mass_ref, *refs):
    blocks, (_, out, centered, weighted, feature) = refs[:5], refs[5:]
    mass = mass_ref[...].astype(jnp.float32)
    index = (1, 2, 4, 6, 7)
    for k, block in enumerate(blocks):
        stage(block, mass, k, centered, weighted, feature)
    column, diagonal = flags[0], flags[1]
    rows = [index.index(p) for p, _ in LATE]
    columns = [index.index(q) for _, q in LATE]

    def body(step, carry):
        p, q = lookup(step, rows), lookup(step, columns)
        p = jnp.where((step == 2) & (column == 1), jnp.int32(index.index(4)), p)
        put_pair(out, step, product(weighted[p], centered[q]), feature, p, q)
        return carry

    lax.fori_loop(0, len(LATE), body, 0)

    @pl.when(diagonal == 1)
    def _():
        p, q = rows[3], columns[3]
        upper, lower = product(weighted[p], centered[p]), product(weighted[q], centered[q])
        i, j = iota((3 * ROWS, 256), 0) % ROWS, iota((3 * ROWS, 256), 1) % ROWS
        put_pair(out, 3, jnp.where(i <= j, upper, lower), feature, p, q)
        lane = iota((ROWS, 128), 1)
        on = jnp.where(i == j, lower, 0.0)
        ends = jnp.zeros((ROWS, 128), jnp.float32)
        at = iota((ROWS, 256), 1)
        for c in range(3):
            mine = on[c * ROWS : (c + 1) * ROWS]
            for d in range(3):
                inside = (at >= d * ROWS) & (at < (d + 1) * ROWS)
                value = jnp.sum(jnp.where(inside, mine, 0.0), axis=1, keepdims=True)
                ends = jnp.where(lane == 64 + 3 * c + d, value, ends)
        out[3, 3 * ROWS :] += ends


def det_four(rows):
    a00, a01, a02, a03 = rows[0]
    a10, a11, a12, a13 = rows[1]
    a20, a21, a22, a23 = rows[2]
    a30, a31, a32, a33 = rows[3]
    s0 = a00 * a11 - a10 * a01
    s1 = a00 * a12 - a10 * a02
    s2 = a00 * a13 - a10 * a03
    s3 = a01 * a12 - a11 * a02
    s4 = a01 * a13 - a11 * a03
    s5 = a02 * a13 - a12 * a03
    t5 = a22 * a33 - a32 * a23
    t4 = a21 * a33 - a31 * a23
    t3 = a21 * a32 - a31 * a22
    t2 = a20 * a33 - a30 * a23
    t1 = a20 * a32 - a30 * a22
    t0 = a20 * a31 - a30 * a21
    return s0 * t5 - s1 * t4 + s2 * t3 + s3 * t2 - s4 * t1 + s5 * t0


def quaternion_fit(moment, spread_rows, spread_cols):
    sxx, sxy, sxz, syx, syy, syz, szx, szy, szz = moment
    coef_two = -2.0 * sum(m * m for m in moment)
    det_three = (
        sxx * (syy * szz - syz * szy)
        - sxy * (syx * szz - syz * szx)
        + sxz * (syx * szy - syy * szx)
    )
    coef_one = -8.0 * det_three
    rows = [
        [sxx + syy + szz, syz - szy, szx - sxz, sxy - syx],
        [syz - szy, sxx - syy - szz, sxy + syx, szx + sxz],
        [szx - sxz, sxy + syx, -sxx + syy - szz, syz + szy],
        [sxy - syx, szx + sxz, syz + szy, -sxx - syy + szz],
    ]
    coef_zero = det_four(rows)
    lam = 0.5 * (spread_rows + spread_cols)
    for turn in range(NEWTON):
        square = lam * lam
        value = (square + coef_two) * square + coef_one * lam + coef_zero
        slope = 4.0 * square * lam + 2.0 * coef_two * lam + coef_one
        lam = lam - value / slope
    return spread_rows + spread_cols - 2.0 * lam


def square_tile(x):
    return jnp.concatenate([x, jnp.zeros((128 - x.shape[0], 128), jnp.float32)], axis=0)


def fit_kernel(flags, parts, first, second):
    diagonal, swap = flags[1] == 1, flags[2] == 1
    total = parts[0]
    for a in range(1, SIDE):
        total = total + parts[a]
    lane, row = iota((ROWS, 128), 1), iota((ROWS, 128), 0)
    rest = total[3 * ROWS :]

    gathered = jnp.zeros((ROWS, 128), jnp.float32)
    for a in range(SIDE):
        tile = jnp.where((lane >= 48) & (lane < 56), parts[a, 3 * ROWS :], 0.0)
        gathered = gathered + pltpu.roll(tile, (8 * a - 48) % 128, 1)

    def per_sender(which):
        pick = (iota((128, 128), 0) == 8 * iota((128, 128), 1) + which).astype(jnp.float32)
        return jnp.dot(gathered, pick, precision=EXACT, preferred_element_type=jnp.float32)

    mass = per_sender(3)
    whole = jnp.sum(mass, axis=1, keepdims=True)

    def offsets(base):
        out = []
        for c in range(3):
            mean = per_sender(base + c)
            centroid = jnp.sum(mass * mean, axis=1, keepdims=True) / whole
            out.append(jnp.where(lane < SIDE, mean - centroid, 0.0))
        return out

    off_p, off_q = offsets(0), offsets(4)

    def spread(off, at):
        within = jnp.sum(jnp.where(lane == at, rest, 0.0), axis=1, keepdims=True)
        between = jnp.sum(mass * sum(o * o for o in off), axis=1, keepdims=True)
        return (within + between) / whole

    spread_p, spread_q = spread(off_p, 56), spread(off_q, 57)

    def as_row(column):
        return jnp.sum(jnp.where(row == lane, column, 0.0), axis=0, keepdims=True)

    upper = row <= lane
    corner = lane == ROWS
    row_p, row_q = as_row(spread_p), as_row(spread_q)
    spread_rows = jnp.where(upper, spread_p, jnp.where(diagonal, spread_q, spread_p))
    spread_cols = jnp.where(upper, jnp.where(diagonal, row_p, row_q), row_q)
    spread_rows = jnp.where(corner, spread_q, spread_rows)
    spread_cols = jnp.where(corner, spread_q, spread_cols)

    low_rows = jnp.concatenate([mass * jnp.where(diagonal, q, p) for p, q in zip(off_p, off_q)], axis=0)
    up_rows = jnp.concatenate([mass * p for p in off_p], axis=0)
    moment = []
    between = []
    for d in range(3):
        up = dot_t(up_rows, square_tile(jnp.where(diagonal, off_p[d], off_q[d])))
        low = dot_t(low_rows, square_tile(off_q[d]))
        between.append((up, low))
    for c in range(3):
        main = total[c * ROWS : (c + 1) * ROWS]
        tail = pltpu.roll(rest, (32 - 16 * c) % 128, 1)
        shifted = [main, pltpu.roll(main, 128 - 48, 1), jnp.where(lane < 32, pltpu.roll(main, 128 - 96, 1), tail)]
        for d in range(3):
            up, low = (b[c * ROWS : (c + 1) * ROWS] for b in between[d])
            value = shifted[d] + jnp.where(upper, up, low)
            end = jnp.sum(jnp.where(lane == 64 + 3 * c + d, rest, 0.0), axis=1, keepdims=True)
            end = end + jnp.sum(mass * off_q[c] * off_q[d], axis=1, keepdims=True)
            moment.append(jnp.where(corner, end, value) / whole)
    msd = quaternion_fit(moment, spread_rows, spread_cols)
    corner_value = jnp.sum(jnp.where(corner, msd, 0.0), axis=1, keepdims=True)
    msd = jnp.where(lane < ROWS, msd, 0.0)
    turned = square_tile(msd).T[:ROWS]
    plain_a = jnp.where(diagonal, jnp.where(upper, msd, turned), msd)
    mirrored = jnp.where(row > lane, msd, jnp.where(row == lane, corner_value, turned))
    plain_b = jnp.where(diagonal, mirrored, turned)
    first[...] = jnp.where(swap, plain_b, plain_a)
    second[...] = jnp.where(swap, plain_a, plain_b)


def join_kernel(flags, first, second, out):
    lane = iota((ROWS, 128), 1)
    a, b = first[...], second[...]
    left = jnp.where(flags[3] == 1, b, a)
    right = jnp.where(flags[3] == 1, a, b)
    out[...] = jnp.where(lane < ROWS, left, pltpu.roll(right, ROWS, 1))[:, : 2 * ROWS]


def on_device(coords, weights):
    first, second, swapped, half = routes()
    frame, atom = lax.axis_index("frame"), lax.axis_index("atom")
    place = frame * SIDE + atom
    last = (atom == SIDE - 1).astype(jnp.int32)
    column, z = frame // SIDE, frame % SIDE
    late_diagonal = (z >= SIDE // 2).astype(jnp.int32)
    table = jnp.asarray(np.array(swapped) + 2 * np.array(half), jnp.int32)[place]
    build_flags = jnp.stack([column, late_diagonal]).astype(jnp.int32)
    fit_flags = jnp.stack([column, late_diagonal * last, table % 2, table // 2]).astype(jnp.int32)
    mass = weights[None, :]

    def along(block, distance):
        route = [
            (c * SIDE + (k + distance) % SIDE, c * SIDE + k) for c in range(2) for k in range(SIDE)
        ]
        return lax.ppermute(block, "frame", route)

    def across(block):
        return lax.ppermute(block, "frame", [((f + SIDE) % (2 * SIDE), f) for f in range(2 * SIDE)])

    own = coords.reshape(3 * ROWS, coords.shape[2])
    plus4 = along(own, 4)
    minus3 = along(own, -3)
    minus1 = along(own, -1)
    other0 = across(own)
    other1 = across(minus1)
    other3 = across(minus3)
    plus5 = along(plus4, 1)

    atoms = own.shape[1]
    slots = len(EARLY) + len(LATE)
    result = jax.ShapeDtypeStruct((slots, 4 * ROWS, 128), jnp.float32)

    def scratch(n):
        return [
            pltpu.VMEM((n, 256, 3 * atoms), jnp.bfloat16),
            pltpu.VMEM((n, 3 * ROWS, 3 * atoms), jnp.bfloat16),
            pltpu.VMEM((n, 2, ROWS, 128), jnp.float32),
        ]

    smem = pl.BlockSpec(memory_space=pltpu.SMEM)
    params = pltpu.CompilerParams(vmem_limit_bytes=VMEM_LIMIT)
    whole = lambda *shape: pl.BlockSpec(shape, lambda i: (0,) * len(shape))
    block_spec = whole(3 * ROWS, atoms)
    pair_flops = 2 * 3 * ROWS * 256 * atoms * 3
    partial = pl.pallas_call(
        early_kernel,
        grid=(1,),
        out_shape=result,
        in_specs=[whole(1, atoms)] + [block_spec] * 7,
        out_specs=whole(len(EARLY), 4 * ROWS, 128),
        scratch_shapes=scratch(7),
        compiler_params=params,
        cost_estimate=pl.CostEstimate(flops=12 * pair_flops, bytes_accessed=4_000_000, transcendentals=0),
    )(mass, own, minus1, minus3, plus4, other0, other1, other3)
    partial = pl.pallas_call(
        late_kernel,
        grid=(1,),
        out_shape=result,
        in_specs=[smem, whole(1, atoms)] + [block_spec] * 5 + [pl.BlockSpec(memory_space=pl.ANY)],
        out_specs=pl.BlockSpec((len(LATE), 4 * ROWS, 128), lambda i: (len(EARLY) // len(LATE), 0, 0)),
        scratch_shapes=scratch(5),
        input_output_aliases={7: 0},
        compiler_params=params,
        cost_estimate=pl.CostEstimate(flops=6 * pair_flops, bytes_accessed=2_000_000, transcendentals=0),
    )(build_flags, mass, minus1, minus3, plus5, other1, other3, partial)

    parts = lax.all_to_all(partial, "atom", 0, 0, tiled=True)

    block = jax.ShapeDtypeStruct((ROWS, 128), jnp.float32)
    vmem = pl.BlockSpec(memory_space=pltpu.VMEM)
    one, two = pl.pallas_call(
        fit_kernel,
        out_shape=(block, block),
        in_specs=[smem, vmem],
        out_specs=(vmem, vmem),
        compiler_params=params,
    )(fit_flags, parts)
    one = lax.ppermute(one, ("frame", "atom"), list(enumerate(first)))
    two = lax.ppermute(two, ("frame", "atom"), list(enumerate(second)))
    return pl.pallas_call(
        join_kernel,
        out_shape=jax.ShapeDtypeStruct((ROWS, 2 * ROWS), jnp.float32),
        in_specs=[smem, vmem, vmem],
        out_specs=vmem,
        compiler_params=params,
    )(fit_flags, one, two)


def solution(mesh):
    placed = (P(None, "frame", "atom"), P("atom"))
    return jax.shard_map(
        on_device, mesh=mesh, in_specs=placed, out_specs=P("frame", "atom"), check_vma=False
    )
```

```python
import functools

import jax
import jax.numpy as jnp
import numpy as np
from jax import lax
from jax.experimental import pallas as pl
from jax.experimental.pallas import tpu as pltpu
from jax.sharding import PartitionSpec as P

NEWTON = 3
ROWS = 48
SIDE = 16
EXACT = lax.Precision.HIGHEST
VMEM_LIMIT = 40 * 1024 * 1024

OWN = (0, 2, 4, -3, -4)
OTHER = (2, 4, -3)
STACK = (3, 0, 4, 2)
EARLY = (
    (3, 1), (0, 1), (4, 1),
    (3, 2), (0, 2), (4, 2),
    (3, 5), (0, 5), (4, 5),
    (0, 3), (4, 3),
    (0, 7), (4, 7), (2, 7),
)
DIAGONAL = EARLY.index((4, 2))
LATE = ((0, 6), (2, 6))


def frame_block(column, z, index):
    if index < len(OWN):
        return column * SIDE + (z + OWN[index]) % SIDE
    return (1 - column) * SIDE + (z + OTHER[index - len(OWN)]) % SIDE


def routes():
    ends = []
    for column in range(2):
        for z in range(SIDE):
            for slot, (p, q) in enumerate(EARLY + LATE):
                if slot == len(EARLY) + 1 and column == 1:
                    p = 4
                a, b = frame_block(column, z, p), frame_block(column, z, q)
                if slot == DIAGONAL and z >= SIDE // 2:
                    ends.append(((a, a), (b, b)))
                else:
                    ends.append(((a, b), (b, a)))
    place = lambda end: end[0] * SIDE + end[1] // 2
    at = {}
    for device, pair in enumerate(ends):
        for which, end in enumerate(pair):
            at.setdefault(place(end), []).append((device, which))
    assert len(at) == len(ends) and all(len(v) == 2 for v in at.values())
    swapped = [None] * len(ends)
    for seed in range(len(ends)):
        device, enter = seed, 0
        while swapped[device] is None:
            swapped[device] = enter
            node = place(ends[device][1 - enter])
            device, enter = [e for e in at[node] if e != (device, 1 - enter)][0]
    first = [place(ends[d][swapped[d]]) for d in range(len(ends))]
    second = [place(ends[d][1 - swapped[d]]) for d in range(len(ends))]
    assert len(set(first)) == len(set(second)) == len(ends)
    half = [0] * len(ends)
    for d in range(len(ends)):
        half[first[d]] = ends[d][swapped[d]][1] % 2
        assert ends[d][1 - swapped[d]][1] % 2 == 1 - half[first[d]] or second[d] != first[d]
    return first, second, swapped, half


def lookup(step, values):
    out = jnp.int32(values[0])
    for k, value in enumerate(values):
        out = jnp.where(step == k, jnp.int32(value), out)
    return out


def iota(shape, axis):
    return lax.broadcasted_iota(jnp.int32, shape, axis)


def dot_t(a, b):
    return lax.dot_general(a, b, (((1,), (1,)), ((), ())), precision=EXACT, preferred_element_type=jnp.float32)


def product(a, b):
    return lax.dot_general(a, b, (((1,), (1,)), ((), ())), preferred_element_type=jnp.float32)


def halves(x):
    high = x.astype(jnp.bfloat16)
    return high, (x - high.astype(jnp.float32)).astype(jnp.bfloat16)


def stage(x, mass):
    local = jnp.sum(mass)
    mean = jnp.sum(x * mass, axis=1, keepdims=True) / local
    x = x - mean
    wx = x * mass
    square = jnp.sum(wx * x, axis=1, keepdims=True)
    return x, wx, mean, square[:ROWS] + square[ROWS : 2 * ROWS] + square[2 * ROWS :], local


def stage_rows(block, mass, at, weighted, feature):
    atoms = block.shape[1]
    _, wx, mean, square, local = stage(block[...], mass)
    high, low = halves(wx)
    for k, part in enumerate((high, high, low)):
        weighted[at * 3 * ROWS : (at + 1) * 3 * ROWS, k * atoms : (k + 1) * atoms] = part
    lane = iota((ROWS, 128), 1)
    out = jnp.where(lane == 51, local, jnp.where(lane == 56, square, 0.0))
    for c in range(3):
        out = jnp.where(lane == 48 + c, mean[c * ROWS : (c + 1) * ROWS], out)
    feature[at] = out


def stage_columns(block, mass, at, centered, feature):
    atoms = block.shape[1]
    x, _, mean, square, _ = stage(block[...], mass)
    high, low = halves(x)
    for k, part in enumerate((high, low, high)):
        centered[at, : 3 * ROWS, k * atoms : (k + 1) * atoms] = part
    lane = iota((ROWS, 128), 1)
    out = jnp.where(lane == 57, square, 0.0)
    for c in range(3):
        out = jnp.where(lane == 52 + c, mean[c * ROWS : (c + 1) * ROWS], out)
    feature[at] = out


def rest_of(tail):
    tail = jnp.where(iota((3 * ROWS, 128), 1) < 16, tail, 0.0)
    return tail[:ROWS] + pltpu.roll(tail[ROWS : 2 * ROWS], 16, 1) + pltpu.roll(tail[2 * ROWS :], 32, 1)


def put_pair(out, slot, value, feature):
    out[slot, : 3 * ROWS] = value[:, :128]
    out[slot, 3 * ROWS :] = rest_of(value[:, 128:]) + feature


def put_group(out, first, pairs, weighted, columns, row_feature, column_feature):
    start = STACK.index(pairs[0][0])
    rows = weighted[start * 3 * ROWS : (start + len(pairs)) * 3 * ROWS]
    values = product(rows, columns)
    for k in range(len(pairs)):
        value = values[k * 3 * ROWS : (k + 1) * 3 * ROWS]
        put_pair(out, first + k, value, row_feature[start + k] + column_feature)


def early_kernel(flags, mass_ref, *refs):
    blocks, (out, weighted, centered, row_feature, column_feature) = refs[:7], refs[7:]
    blocks = dict(zip((0, 1, 2, 3, 4, 5, 7), blocks))
    mass = mass_ref[...].astype(jnp.float32)
    for at, k in enumerate(STACK):
        stage_rows(blocks[k], mass, at, weighted, row_feature)
    order = (1, 2, 5, 3, 7)
    for at, k in enumerate(order):
        stage_columns(blocks[k], mass, at, centered, column_feature)
    first = 0
    for at, k in enumerate(order):
        pairs = [pair for pair in EARLY if pair[1] == k]
        assert tuple(EARLY[first : first + len(pairs)]) == tuple(pairs)
        assert tuple(STACK[STACK.index(pairs[0][0]) :][: len(pairs)]) == tuple(p for p, _ in pairs)
        put_group(out, first, pairs, weighted, centered[at], row_feature, column_feature[at])
        first += len(pairs)

    @pl.when(flags[1] == 1)
    def _():
        stage_columns(blocks[4], mass, 5, centered, column_feature)
        p, q = STACK.index(4), STACK.index(2)
        upper = product(weighted[p * 3 * ROWS : (p + 1) * 3 * ROWS], centered[5])
        lower = product(weighted[q * 3 * ROWS : (q + 1) * 3 * ROWS], centered[order.index(2)])
        i, j = iota((3 * ROWS, 256), 0) % ROWS, iota((3 * ROWS, 256), 1) % ROWS
        at = iota((ROWS, 256), 1)
        on = jnp.where((i == j) & (iota((3 * ROWS, 256), 1) < 3 * ROWS), lower, 0.0)
        lane = iota((ROWS, 128), 1)
        ends = row_feature[p] + column_feature[order.index(2)]
        for c in range(3):
            mine = on[c * ROWS : (c + 1) * ROWS]
            for d in range(3):
                inside = (at >= d * ROWS) & (at < (d + 1) * ROWS)
                value = jnp.sum(jnp.where(inside, mine, 0.0), axis=1, keepdims=True)
                ends = jnp.where(lane == 64 + 3 * c + d, value, ends)
        put_pair(out, DIAGONAL, jnp.where(i <= j, upper, lower), ends)


def late_kernel(flags, mass_ref, *refs):
    blocks, (_, out, weighted, centered, row_feature, column_feature) = refs[:4], refs[4:]
    mass = mass_ref[...].astype(jnp.float32)
    for at, block in enumerate(blocks[:3]):
        stage_rows(block, mass, at, weighted, row_feature)
    stage_columns(blocks[3], mass, 0, centered, column_feature)
    values = product(weighted[...], centered[0])
    put_pair(out, 0, values[: 3 * ROWS], row_feature[0] + column_feature[0])
    other = flags[0] == 1
    value = jnp.where(other, values[3 * ROWS : 6 * ROWS], values[6 * ROWS :])
    put_pair(out, 1, value, jnp.where(other, row_feature[1], row_feature[2]) + column_feature[0])


def det_four(rows):
    a00, a01, a02, a03 = rows[0]
    a10, a11, a12, a13 = rows[1]
    a20, a21, a22, a23 = rows[2]
    a30, a31, a32, a33 = rows[3]
    s0 = a00 * a11 - a10 * a01
    s1 = a00 * a12 - a10 * a02
    s2 = a00 * a13 - a10 * a03
    s3 = a01 * a12 - a11 * a02
    s4 = a01 * a13 - a11 * a03
    s5 = a02 * a13 - a12 * a03
    t5 = a22 * a33 - a32 * a23
    t4 = a21 * a33 - a31 * a23
    t3 = a21 * a32 - a31 * a22
    t2 = a20 * a33 - a30 * a23
    t1 = a20 * a32 - a30 * a22
    t0 = a20 * a31 - a30 * a21
    return s0 * t5 - s1 * t4 + s2 * t3 + s3 * t2 - s4 * t1 + s5 * t0


def quaternion_fit(moment, spread_rows, spread_cols):
    sxx, sxy, sxz, syx, syy, syz, szx, szy, szz = moment
    coef_two = -2.0 * sum(m * m for m in moment)
    det_three = (
        sxx * (syy * szz - syz * szy)
        - sxy * (syx * szz - syz * szx)
        + sxz * (syx * szy - syy * szx)
    )
    coef_one = -8.0 * det_three
    rows = [
        [sxx + syy + szz, syz - szy, szx - sxz, sxy - syx],
        [syz - szy, sxx - syy - szz, sxy + syx, szx + sxz],
        [szx - sxz, sxy + syx, -sxx + syy - szz, syz + szy],
        [sxy - syx, szx + sxz, syz + szy, -sxx - syy + szz],
    ]
    coef_zero = det_four(rows)
    lam = 0.5 * (spread_rows + spread_cols)
    for turn in range(NEWTON):
        square = lam * lam
        value = (square + coef_two) * square + coef_one * lam + coef_zero
        slope = 4.0 * square * lam + 2.0 * coef_two * lam + coef_one
        lam = lam - value / slope
    return spread_rows + spread_cols - 2.0 * lam


def square_tile(x):
    return jnp.concatenate([x, jnp.zeros((128 - x.shape[0], 128), jnp.float32)], axis=0)


def fit_kernel(flags, parts, first, second):
    diagonal, swap = flags[1] == 1, flags[2] == 1
    total = parts[0]
    for a in range(1, SIDE):
        total = total + parts[a]
    lane, row = iota((ROWS, 128), 1), iota((ROWS, 128), 0)
    rest = total[3 * ROWS :]

    gathered = jnp.zeros((ROWS, 128), jnp.float32)
    for a in range(SIDE):
        tile = jnp.where((lane >= 48) & (lane < 56), parts[a, 3 * ROWS :], 0.0)
        gathered = gathered + pltpu.roll(tile, (8 * a - 48) % 128, 1)

    def per_sender(which):
        pick = (iota((128, 128), 0) == 8 * iota((128, 128), 1) + which).astype(jnp.float32)
        return jnp.dot(gathered, pick, precision=EXACT, preferred_element_type=jnp.float32)

    mass = per_sender(3)
    whole = jnp.sum(mass, axis=1, keepdims=True)

    def offsets(base):
        out = []
        for c in range(3):
            mean = per_sender(base + c)
            centroid = jnp.sum(mass * mean, axis=1, keepdims=True) / whole
            out.append(jnp.where(lane < SIDE, mean - centroid, 0.0))
        return out

    off_p, off_q = offsets(0), offsets(4)

    def spread(off, at):
        within = jnp.sum(jnp.where(lane == at, rest, 0.0), axis=1, keepdims=True)
        between = jnp.sum(mass * sum(o * o for o in off), axis=1, keepdims=True)
        return (within + between) / whole

    spread_p, spread_q = spread(off_p, 56), spread(off_q, 57)

    def as_row(column):
        return jnp.sum(jnp.where(row == lane, column, 0.0), axis=0, keepdims=True)

    upper = row <= lane
    corner = lane == ROWS
    row_p, row_q = as_row(spread_p), as_row(spread_q)
    spread_rows = jnp.where(upper, spread_p, jnp.where(diagonal, spread_q, spread_p))
    spread_cols = jnp.where(upper, jnp.where(diagonal, row_p, row_q), row_q)
    spread_rows = jnp.where(corner, spread_q, spread_rows)
    spread_cols = jnp.where(corner, spread_q, spread_cols)

    low_rows = jnp.concatenate([mass * jnp.where(diagonal, q, p) for p, q in zip(off_p, off_q)], axis=0)
    up_rows = jnp.concatenate([mass * p for p in off_p], axis=0)
    moment = []
    between = []
    for d in range(3):
        up = dot_t(up_rows, square_tile(jnp.where(diagonal, off_p[d], off_q[d])))
        low = dot_t(low_rows, square_tile(off_q[d]))
        between.append((up, low))
    for c in range(3):
        main = total[c * ROWS : (c + 1) * ROWS]
        tail = pltpu.roll(rest, (32 - 16 * c) % 128, 1)
        shifted = [main, pltpu.roll(main, 128 - 48, 1), jnp.where(lane < 32, pltpu.roll(main, 128 - 96, 1), tail)]
        for d in range(3):
            up, low = (b[c * ROWS : (c + 1) * ROWS] for b in between[d])
            value = shifted[d] + jnp.where(upper, up, low)
            end = jnp.sum(jnp.where(lane == 64 + 3 * c + d, rest, 0.0), axis=1, keepdims=True)
            end = end + jnp.sum(mass * off_q[c] * off_q[d], axis=1, keepdims=True)
            moment.append(jnp.where(corner, end, value) / whole)
    msd = quaternion_fit(moment, spread_rows, spread_cols)
    corner_value = jnp.sum(jnp.where(corner, msd, 0.0), axis=1, keepdims=True)
    msd = jnp.where(lane < ROWS, msd, 0.0)
    turned = square_tile(msd).T[:ROWS]
    plain_a = jnp.where(diagonal, jnp.where(upper, msd, turned), msd)
    mirrored = jnp.where(row > lane, msd, jnp.where(row == lane, corner_value, turned))
    plain_b = jnp.where(diagonal, mirrored, turned)
    first[...] = jnp.where(swap, plain_b, plain_a)
    second[...] = jnp.where(swap, plain_a, plain_b)


def join_kernel(flags, first, second, out):
    lane = iota((ROWS, 128), 1)
    a, b = first[...], second[...]
    left = jnp.where(flags[3] == 1, b, a)
    right = jnp.where(flags[3] == 1, a, b)
    out[...] = jnp.where(lane < ROWS, left, pltpu.roll(right, ROWS, 1))[:, : 2 * ROWS]


def on_device(coords, weights):
    first, second, swapped, half = routes()
    frame, atom = lax.axis_index("frame"), lax.axis_index("atom")
    place = frame * SIDE + atom
    last = (atom == DIAGONAL).astype(jnp.int32)
    column, z = frame // SIDE, frame % SIDE
    late_diagonal = (z >= SIDE // 2).astype(jnp.int32)
    table = jnp.asarray(np.array(swapped) + 2 * np.array(half), jnp.int32)[place]
    build_flags = jnp.stack([column, late_diagonal]).astype(jnp.int32)
    fit_flags = jnp.stack([column, late_diagonal * last, table % 2, table // 2]).astype(jnp.int32)
    mass = weights[None, :]

    def along(block, distance):
        route = [
            (c * SIDE + (k + distance) % SIDE, c * SIDE + k) for c in range(2) for k in range(SIDE)
        ]
        return lax.ppermute(block, "frame", route)

    def across(block):
        return lax.ppermute(block, "frame", [((f + SIDE) % (2 * SIDE), f) for f in range(2 * SIDE)])

    own = coords.reshape(3 * ROWS, coords.shape[2])
    plus2 = along(own, 2)
    minus3 = along(own, -3)
    plus4 = along(plus2, 2)
    minus4 = along(minus3, -1)
    other2 = across(plus2)
    other3 = across(minus3)
    other4 = across(plus4)

    atoms = own.shape[1]
    slots = len(EARLY) + len(LATE)
    result = jax.ShapeDtypeStruct((slots, 4 * ROWS, 128), jnp.float32)

    def scratch(rows, columns):
        return [
            pltpu.VMEM((rows * 3 * ROWS, 3 * atoms), jnp.bfloat16),
            pltpu.VMEM((columns, 256, 3 * atoms), jnp.bfloat16),
            pltpu.VMEM((rows, ROWS, 128), jnp.float32),
            pltpu.VMEM((columns, ROWS, 128), jnp.float32),
        ]

    smem = pl.BlockSpec(memory_space=pltpu.SMEM)
    params = pltpu.CompilerParams(vmem_limit_bytes=VMEM_LIMIT)
    whole = lambda *shape: pl.BlockSpec(shape, lambda i: (0,) * len(shape))
    block_spec = whole(3 * ROWS, atoms)
    pair_flops = 2 * 3 * ROWS * 256 * atoms * 3
    partial = pl.pallas_call(
        early_kernel,
        grid=(1,),
        out_shape=result,
        in_specs=[smem, whole(1, atoms)] + [block_spec] * 7,
        out_specs=whole(len(EARLY), 4 * ROWS, 128),
        scratch_shapes=scratch(4, 6),
        compiler_params=params,
        cost_estimate=pl.CostEstimate(flops=14 * pair_flops, bytes_accessed=4_000_000, transcendentals=0),
    )(build_flags, mass, own, plus2, plus4, minus3, minus4, other2, other3)
    partial = pl.pallas_call(
        late_kernel,
        grid=(1,),
        out_shape=result,
        in_specs=[smem, whole(1, atoms)] + [block_spec] * 4 + [pl.BlockSpec(memory_space=pl.ANY)],
        out_specs=pl.BlockSpec((len(LATE), 4 * ROWS, 128), lambda i: (len(EARLY) // len(LATE), 0, 0)),
        scratch_shapes=scratch(3, 1),
        input_output_aliases={6: 0},
        compiler_params=params,
        cost_estimate=pl.CostEstimate(flops=3 * pair_flops, bytes_accessed=2_000_000, transcendentals=0),
    )(build_flags, mass, own, minus4, plus4, other4, partial)

    parts = lax.all_to_all(partial, "atom", 0, 0, tiled=True)

    block = jax.ShapeDtypeStruct((ROWS, 128), jnp.float32)
    vmem = pl.BlockSpec(memory_space=pltpu.VMEM)
    one, two = pl.pallas_call(
        fit_kernel,
        out_shape=(block, block),
        in_specs=[smem, vmem],
        out_specs=(vmem, vmem),
        compiler_params=params,
    )(fit_flags, parts)
    one = lax.ppermute(one, ("frame", "atom"), list(enumerate(first)))
    two = lax.ppermute(two, ("frame", "atom"), list(enumerate(second)))
    return pl.pallas_call(
        join_kernel,
        out_shape=jax.ShapeDtypeStruct((ROWS, 2 * ROWS), jnp.float32),
        in_specs=[smem, vmem, vmem],
        out_specs=vmem,
        compiler_params=params,
    )(fit_flags, one, two)


def solution(mesh):
    placed = (P(None, "frame", "atom"), P("atom"))
    return jax.shard_map(
        on_device, mesh=mesh, in_specs=placed, out_specs=P("frame", "atom"), check_vma=False
    )
```

```python
import functools

import jax
import jax.numpy as jnp
import numpy as np
from jax import lax
from jax.experimental import pallas as pl
from jax.experimental.pallas import tpu as pltpu
from jax.sharding import PartitionSpec as P

NEWTON = 3
ROWS = 48
SIDE = 16
EXACT = lax.Precision.HIGHEST
VMEM_LIMIT = 40 * 1024 * 1024

OWN = (0, 2, 4, -3, -4)
OTHER = (2, 4, -3)
STACK = (3, 0, 4, 2)
EARLY = (
    (3, 1), (0, 1), (4, 1),
    (3, 2), (0, 2), (4, 2),
    (3, 5), (0, 5), (4, 5),
    (0, 3), (4, 3),
    (0, 7), (4, 7), (2, 7),
)
DIAGONAL = EARLY.index((4, 2))
LATE = ((0, 6), (2, 6))
POSITION = (11, 4, 12, 5, 0, 2, 10, 3, 1, 9, 6, 8, 13, 7, 14, 15)
CHIPS = SIDE // 2


def frame_block(column, z, index):
    if index < len(OWN):
        return column * SIDE + (z + OWN[index]) % SIDE
    return (1 - column) * SIDE + (z + OTHER[index - len(OWN)]) % SIDE


def ends_of(column, z, pair):
    p, q = (EARLY + LATE)[pair]
    if pair == len(EARLY) + 1 and column == 1:
        p = 4
    a, b = frame_block(column, z, p), frame_block(column, z, q)
    if pair == DIAGONAL and z >= SIDE // 2:
        return ((a, a), (b, b))
    return ((a, b), (b, a))


def around(a, b, n):
    return min((a - b) % n, (b - a) % n)


def distance(column, z, chip, end):
    to_column, to_z = divmod(end[0], SIDE)
    to_chip = end[1] // 4
    x, to_x = 2 * (chip % 2) + column, 2 * (to_chip % 2) + to_column
    return around(z, to_z, SIDE) + around(chip // 2, to_chip // 2, 4) + around(x, to_x, 4)


def order_of_chips(column, z):
    cost = [[0] * CHIPS for _ in range(CHIPS)]
    for k in range(CHIPS):
        for chip in range(CHIPS):
            for pair in POSITION[2 * k : 2 * k + 2]:
                far = max(distance(column, z, chip, end) for end in ends_of(column, z, pair))
                cost[k][chip] = max(cost[k][chip], 4**far)
    best = {0: (0, ())}
    for k in range(CHIPS):
        later = {}
        for taken, (value, order) in best.items():
            for chip in range(CHIPS):
                if not taken >> chip & 1:
                    entry = (value + cost[k][chip], order + (chip,))
                    key = taken | 1 << chip
                    later[key] = min(later.get(key, entry), entry)
        best = later
    return best[(1 << CHIPS) - 1][1]


def routes():
    orders, ends, diagonal = [], [], []
    for column in range(2):
        for z in range(SIDE):
            order = order_of_chips(column, z)
            orders.append(order)
            for device in range(SIDE):
                pair = POSITION[2 * order.index(device // 2) + device % 2]
                ends.append(ends_of(column, z, pair))
                diagonal.append(int(pair == DIAGONAL and z >= SIDE // 2))
    place = lambda end: end[0] * SIDE + end[1] // 2
    at = {}
    for device, pair in enumerate(ends):
        for which, end in enumerate(pair):
            at.setdefault(place(end), []).append((device, which))
    assert len(at) == len(ends) and all(len(v) == 2 for v in at.values())
    swapped = [None] * len(ends)
    for seed in range(len(ends)):
        device, enter = seed, 0
        while swapped[device] is None:
            swapped[device] = enter
            node = place(ends[device][1 - enter])
            device, enter = [e for e in at[node] if e != (device, 1 - enter)][0]
    first = [place(ends[d][swapped[d]]) for d in range(len(ends))]
    second = [place(ends[d][1 - swapped[d]]) for d in range(len(ends))]
    assert len(set(first)) == len(set(second)) == len(ends)
    half = [0] * len(ends)
    for d in range(len(ends)):
        half[first[d]] = ends[d][swapped[d]][1] % 2
    table = [a + 2 * b + 4 * c for a, b, c in zip(swapped, half, diagonal)]
    return orders, first, second, table


def lookup(step, values):
    out = jnp.int32(values[0])
    for k, value in enumerate(values):
        out = jnp.where(step == k, jnp.int32(value), out)
    return out


def iota(shape, axis):
    return lax.broadcasted_iota(jnp.int32, shape, axis)


def dot_t(a, b):
    return lax.dot_general(a, b, (((1,), (1,)), ((), ())), precision=EXACT, preferred_element_type=jnp.float32)


def product(a, b):
    return lax.dot_general(a, b, (((1,), (1,)), ((), ())), preferred_element_type=jnp.float32)


def halves(x):
    high = x.astype(jnp.bfloat16)
    return high, (x - high.astype(jnp.float32)).astype(jnp.bfloat16)


def stage(x, mass):
    local = jnp.sum(mass)
    mean = jnp.sum(x * mass, axis=1, keepdims=True) / local
    x = x - mean
    wx = x * mass
    square = jnp.sum(wx * x, axis=1, keepdims=True)
    return x, wx, mean, square[:ROWS] + square[ROWS : 2 * ROWS] + square[2 * ROWS :], local


def stage_rows(block, mass, at, core, weighted, feature):
    atoms = block.shape[1]
    _, wx, mean, square, local = stage(block[...], mass)
    high, low = halves(wx)
    for k, part in enumerate((high, high, low)):
        weighted[at * 3 * ROWS : (at + 1) * 3 * ROWS, k * atoms : (k + 1) * atoms] = part
    lane = iota((ROWS, 128), 1) - 8 * core
    out = jnp.where(lane == 51, local, jnp.where(lane == 64 - 8 * core, square, 0.0))
    for c in range(3):
        out = jnp.where(lane == 48 + c, mean[c * ROWS : (c + 1) * ROWS], out)
    feature[at] = out


def stage_columns(block, mass, at, core, centered, feature):
    atoms = block.shape[1]
    x, _, mean, square, _ = stage(block[...], mass)
    high, low = halves(x)
    for k, part in enumerate((high, low, high)):
        centered[at, : 3 * ROWS, k * atoms : (k + 1) * atoms] = part
    lane = iota((ROWS, 128), 1) - 8 * core
    out = jnp.where(lane == 65 - 8 * core, square, 0.0)
    for c in range(3):
        out = jnp.where(lane == 52 + c, mean[c * ROWS : (c + 1) * ROWS], out)
    feature[at] = out


def rest_of(tail):
    tail = jnp.where(iota((3 * ROWS, 128), 1) < 16, tail, 0.0)
    return tail[:ROWS] + pltpu.roll(tail[ROWS : 2 * ROWS], 16, 1) + pltpu.roll(tail[2 * ROWS :], 32, 1)


def put_pair(out, pair, core, value, feature):
    k, owner = divmod(POSITION.index(pair), 2)
    k = k % out[0].shape[0]
    rest = rest_of(value[:, 128:]) + feature
    for ref, here in zip(out, (core == owner, core != owner)):

        @pl.when(here)
        def _():
            ref[k, : 3 * ROWS] = value[:, :128]
            ref[k, 3 * ROWS :] = rest


def put_group(out, first, pairs, core, weighted, columns, row_feature, column_feature):
    start = STACK.index(pairs[0][0])
    rows = weighted[start * 3 * ROWS : (start + len(pairs)) * 3 * ROWS]
    values = product(rows, columns)
    for k in range(len(pairs)):
        value = values[k * 3 * ROWS : (k + 1) * 3 * ROWS]
        put_pair(out, first + k, core, value, row_feature[start + k] + column_feature)


def early_kernel(flags, mass_ref, *refs):
    blocks, out, (weighted, centered, row_feature, column_feature) = refs[:7], refs[7:9], refs[9:]
    core = flags[2]
    blocks = dict(zip((0, 1, 2, 3, 4, 5, 7), blocks))
    mass = mass_ref[...].astype(jnp.float32)
    for at, k in enumerate(STACK):
        stage_rows(blocks[k], mass, at, core, weighted, row_feature)
    order = (1, 2, 5, 3, 7)
    for at, k in enumerate(order):
        stage_columns(blocks[k], mass, at, core, centered, column_feature)
    first = 0
    for at, k in enumerate(order):
        pairs = [pair for pair in EARLY if pair[1] == k]
        assert tuple(EARLY[first : first + len(pairs)]) == tuple(pairs)
        assert tuple(STACK[STACK.index(pairs[0][0]) :][: len(pairs)]) == tuple(p for p, _ in pairs)
        put_group(out, first, pairs, core, weighted, centered[at], row_feature, column_feature[at])
        first += len(pairs)

    @pl.when(flags[1] == 1)
    def _():
        stage_columns(blocks[4], mass, 5, core, centered, column_feature)
        p, q = STACK.index(4), STACK.index(2)
        upper = product(weighted[p * 3 * ROWS : (p + 1) * 3 * ROWS], centered[5])
        lower = product(weighted[q * 3 * ROWS : (q + 1) * 3 * ROWS], centered[order.index(2)])
        i, j = iota((3 * ROWS, 256), 0) % ROWS, iota((3 * ROWS, 256), 1) % ROWS
        at = iota((ROWS, 256), 1)
        on = jnp.where((i == j) & (iota((3 * ROWS, 256), 1) < 3 * ROWS), lower, 0.0)
        lane = iota((ROWS, 128), 1)
        ends = row_feature[p] + column_feature[order.index(2)]
        for c in range(3):
            mine = on[c * ROWS : (c + 1) * ROWS]
            for d in range(3):
                inside = (at >= d * ROWS) & (at < (d + 1) * ROWS)
                value = jnp.sum(jnp.where(inside, mine, 0.0), axis=1, keepdims=True)
                ends = jnp.where(lane == 66 + 3 * c + d, value, ends)
        put_pair(out, DIAGONAL, core, jnp.where(i <= j, upper, lower), ends)


def late_kernel(flags, mass_ref, *refs):
    blocks, out, (weighted, centered, row_feature, column_feature) = refs[:4], refs[6:8], refs[8:]
    core = flags[2]
    mass = mass_ref[...].astype(jnp.float32)
    for at, block in enumerate(blocks[:3]):
        stage_rows(block, mass, at, core, weighted, row_feature)
    stage_columns(blocks[3], mass, 0, core, centered, column_feature)
    values = product(weighted[...], centered[0])
    first = len(EARLY)
    put_pair(out, first, core, values[: 3 * ROWS], row_feature[0] + column_feature[0])
    other = flags[0] == 1
    value = jnp.where(other, values[3 * ROWS : 6 * ROWS], values[6 * ROWS :])
    put_pair(out, first + 1, core, value, jnp.where(other, row_feature[1], row_feature[2]) + column_feature[0])


def det_four(rows):
    a00, a01, a02, a03 = rows[0]
    a10, a11, a12, a13 = rows[1]
    a20, a21, a22, a23 = rows[2]
    a30, a31, a32, a33 = rows[3]
    s0 = a00 * a11 - a10 * a01
    s1 = a00 * a12 - a10 * a02
    s2 = a00 * a13 - a10 * a03
    s3 = a01 * a12 - a11 * a02
    s4 = a01 * a13 - a11 * a03
    s5 = a02 * a13 - a12 * a03
    t5 = a22 * a33 - a32 * a23
    t4 = a21 * a33 - a31 * a23
    t3 = a21 * a32 - a31 * a22
    t2 = a20 * a33 - a30 * a23
    t1 = a20 * a32 - a30 * a22
    t0 = a20 * a31 - a30 * a21
    return s0 * t5 - s1 * t4 + s2 * t3 + s3 * t2 - s4 * t1 + s5 * t0


def quaternion_fit(moment, spread_rows, spread_cols):
    sxx, sxy, sxz, syx, syy, syz, szx, szy, szz = moment
    coef_two = -2.0 * sum(m * m for m in moment)
    det_three = (
        sxx * (syy * szz - syz * szy)
        - sxy * (syx * szz - syz * szx)
        + sxz * (syx * szy - syy * szx)
    )
    coef_one = -8.0 * det_three
    rows = [
        [sxx + syy + szz, syz - szy, szx - sxz, sxy - syx],
        [syz - szy, sxx - syy - szz, sxy + syx, szx + sxz],
        [szx - sxz, sxy + syx, -sxx + syy - szz, syz + szy],
        [sxy - syx, szx + sxz, syz + szy, -sxx - syy + szz],
    ]
    coef_zero = det_four(rows)
    lam = 0.5 * (spread_rows + spread_cols)
    for turn in range(NEWTON):
        square = lam * lam
        value = (square + coef_two) * square + coef_one * lam + coef_zero
        slope = 4.0 * square * lam + 2.0 * coef_two * lam + coef_one
        lam = lam - value / slope
    return spread_rows + spread_cols - 2.0 * lam


def square_tile(x):
    return jnp.concatenate([x, jnp.zeros((128 - x.shape[0], 128), jnp.float32)], axis=0)


def fit_kernel(flags, parts, first, second):
    diagonal, swap = flags[2] == 1, flags[0] == 1
    total = parts[0]
    for a in range(1, CHIPS):
        total = total + parts[a]
    lane, row = iota((ROWS, 128), 1), iota((ROWS, 128), 0)
    rest = total[3 * ROWS :]

    gathered = jnp.zeros((ROWS, 128), jnp.float32)
    for a in range(CHIPS):
        tile = jnp.where((lane >= 48) & (lane < 64), parts[a, 3 * ROWS :], 0.0)
        gathered = gathered + pltpu.roll(tile, (16 * a - 48) % 128, 1)

    def per_sender(which):
        pick = (iota((128, 128), 0) == 8 * iota((128, 128), 1) + which).astype(jnp.float32)
        return jnp.dot(gathered, pick, precision=EXACT, preferred_element_type=jnp.float32)

    mass = per_sender(3)
    whole = jnp.sum(mass, axis=1, keepdims=True)

    def offsets(base):
        out = []
        for c in range(3):
            mean = per_sender(base + c)
            centroid = jnp.sum(mass * mean, axis=1, keepdims=True) / whole
            out.append(jnp.where(lane < SIDE, mean - centroid, 0.0))
        return out

    off_p, off_q = offsets(0), offsets(4)

    def spread(off, at):
        within = jnp.sum(jnp.where(lane == at, rest, 0.0), axis=1, keepdims=True)
        between = jnp.sum(mass * sum(o * o for o in off), axis=1, keepdims=True)
        return (within + between) / whole

    spread_p, spread_q = spread(off_p, 64), spread(off_q, 65)

    def as_row(column):
        return jnp.sum(jnp.where(row == lane, column, 0.0), axis=0, keepdims=True)

    upper = row <= lane
    corner = lane == ROWS
    row_p, row_q = as_row(spread_p), as_row(spread_q)
    spread_rows = jnp.where(upper, spread_p, jnp.where(diagonal, spread_q, spread_p))
    spread_cols = jnp.where(upper, jnp.where(diagonal, row_p, row_q), row_q)
    spread_rows = jnp.where(corner, spread_q, spread_rows)
    spread_cols = jnp.where(corner, spread_q, spread_cols)

    low_rows = jnp.concatenate([mass * jnp.where(diagonal, q, p) for p, q in zip(off_p, off_q)], axis=0)
    up_rows = jnp.concatenate([mass * p for p in off_p], axis=0)
    moment = []
    between = []
    for d in range(3):
        up = dot_t(up_rows, square_tile(jnp.where(diagonal, off_p[d], off_q[d])))
        low = dot_t(low_rows, square_tile(off_q[d]))
        between.append((up, low))
    for c in range(3):
        main = total[c * ROWS : (c + 1) * ROWS]
        tail = pltpu.roll(rest, (32 - 16 * c) % 128, 1)
        shifted = [main, pltpu.roll(main, 128 - 48, 1), jnp.where(lane < 32, pltpu.roll(main, 128 - 96, 1), tail)]
        for d in range(3):
            up, low = (b[c * ROWS : (c + 1) * ROWS] for b in between[d])
            value = shifted[d] + jnp.where(upper, up, low)
            end = jnp.sum(jnp.where(lane == 66 + 3 * c + d, rest, 0.0), axis=1, keepdims=True)
            end = end + jnp.sum(mass * off_q[c] * off_q[d], axis=1, keepdims=True)
            moment.append(jnp.where(corner, end, value) / whole)
    msd = quaternion_fit(moment, spread_rows, spread_cols)
    corner_value = jnp.sum(jnp.where(corner, msd, 0.0), axis=1, keepdims=True)
    msd = jnp.where(lane < ROWS, msd, 0.0)
    turned = square_tile(msd).T[:ROWS]
    plain_a = jnp.where(diagonal, jnp.where(upper, msd, turned), msd)
    mirrored = jnp.where(row > lane, msd, jnp.where(row == lane, corner_value, turned))
    plain_b = jnp.where(diagonal, mirrored, turned)
    first[...] = jnp.where(swap, plain_b, plain_a)
    second[...] = jnp.where(swap, plain_a, plain_b)


def join_kernel(flags, first, second, out):
    lane = iota((ROWS, 128), 1)
    a, b = first[...], second[...]
    left = jnp.where(flags[1] == 1, b, a)
    right = jnp.where(flags[1] == 1, a, b)
    out[...] = jnp.where(lane < ROWS, left, pltpu.roll(right, ROWS, 1))[:, : 2 * ROWS]


def on_device(coords, weights):
    orders, first, second, table = routes()
    frame, atom = lax.axis_index("frame"), lax.axis_index("atom")
    build_flags = jnp.stack([frame // SIDE, (frame % SIDE) // (SIDE // 2), atom % 2]).astype(jnp.int32)
    mine = jnp.asarray(np.array(table), jnp.int32)[frame * SIDE + atom]
    fit_flags = jnp.stack([mine & 1, mine >> 1 & 1, mine >> 2])
    mass = weights[None, :]

    def along(block, distance):
        route = [
            (c * SIDE + (k + distance) % SIDE, c * SIDE + k) for c in range(2) for k in range(SIDE)
        ]
        return lax.ppermute(block, "frame", route)

    def across(block):
        return lax.ppermute(block, "frame", [((f + SIDE) % (2 * SIDE), f) for f in range(2 * SIDE)])

    own = coords.reshape(3 * ROWS, coords.shape[2])
    plus2 = along(own, 2)
    minus3 = along(own, -3)
    plus4 = along(plus2, 2)
    minus4 = along(minus3, -1)
    other2 = across(plus2)
    other3 = across(minus3)
    other4 = across(plus4)

    atoms = own.shape[1]
    result = [jax.ShapeDtypeStruct((CHIPS, 4 * ROWS, 128), jnp.float32)] * 2

    def scratch(rows, columns):
        return [
            pltpu.VMEM((rows * 3 * ROWS, 3 * atoms), jnp.bfloat16),
            pltpu.VMEM((columns, 256, 3 * atoms), jnp.bfloat16),
            pltpu.VMEM((rows, ROWS, 128), jnp.float32),
            pltpu.VMEM((columns, ROWS, 128), jnp.float32),
        ]

    smem = pl.BlockSpec(memory_space=pltpu.SMEM)
    params = pltpu.CompilerParams(vmem_limit_bytes=VMEM_LIMIT)
    whole = lambda *shape: pl.BlockSpec(shape, lambda i: (0,) * len(shape))
    block_spec = whole(3 * ROWS, atoms)
    pair_flops = 2 * 3 * ROWS * 256 * atoms * 3
    partial = pl.pallas_call(
        early_kernel,
        grid=(1,),
        out_shape=result,
        in_specs=[smem, whole(1, atoms)] + [block_spec] * 7,
        out_specs=[whole(len(EARLY) // 2, 4 * ROWS, 128)] * 2,
        scratch_shapes=scratch(4, 6),
        compiler_params=params,
        cost_estimate=pl.CostEstimate(flops=14 * pair_flops, bytes_accessed=4_000_000, transcendentals=0),
    )(build_flags, mass, own, plus2, plus4, minus3, minus4, other2, other3)
    keep, send = pl.pallas_call(
        late_kernel,
        grid=(1,),
        out_shape=result,
        in_specs=[smem, whole(1, atoms)] + [block_spec] * 4 + [pl.BlockSpec(memory_space=pl.ANY)] * 2,
        out_specs=[pl.BlockSpec((1, 4 * ROWS, 128), lambda i: (CHIPS - 1, 0, 0))] * 2,
        scratch_shapes=scratch(3, 1),
        input_output_aliases={6: 0, 7: 1},
        compiler_params=params,
        cost_estimate=pl.CostEstimate(flops=3 * pair_flops, bytes_accessed=2_000_000, transcendentals=0),
    )(build_flags, mass, own, minus4, plus4, other4, *partial)

    taken = lax.ppermute(send, "atom", [(a, a ^ 1) for a in range(SIDE)])
    groups = [[f * SIDE + 2 * chip + c for chip in orders[f]] for f in range(2 * SIDE) for c in range(2)]
    parts = lax.all_to_all(
        keep + taken, ("frame", "atom"), 0, 0, axis_index_groups=groups, tiled=True
    )

    block = jax.ShapeDtypeStruct((ROWS, 128), jnp.float32)
    vmem = pl.BlockSpec(memory_space=pltpu.VMEM)
    one, two = pl.pallas_call(
        fit_kernel,
        out_shape=(block, block),
        in_specs=[smem, vmem],
        out_specs=(vmem, vmem),
        compiler_params=params,
    )(fit_flags, parts)
    one = lax.ppermute(one, ("frame", "atom"), list(enumerate(first)))
    two = lax.ppermute(two, ("frame", "atom"), list(enumerate(second)))
    return pl.pallas_call(
        join_kernel,
        out_shape=jax.ShapeDtypeStruct((ROWS, 2 * ROWS), jnp.float32),
        in_specs=[smem, vmem, vmem],
        out_specs=vmem,
        compiler_params=params,
    )(fit_flags, one, two)


def solution(mesh):
    placed = (P(None, "frame", "atom"), P("atom"))
    return jax.shard_map(
        on_device, mesh=mesh, in_specs=placed, out_specs=P("frame", "atom"), check_vma=False
    )
```

```python
import functools

import jax
import jax.numpy as jnp
import numpy as np
from jax import lax
from jax.experimental import pallas as pl
from jax.experimental.pallas import tpu as pltpu
from jax.sharding import PartitionSpec as P

NEWTON = 3
ROWS = 48
SIDE = 16
EXACT = lax.Precision.HIGHEST
VMEM_LIMIT = 40 * 1024 * 1024

OWN = (0, 2, 4, -3, -4)
OTHER = (2, 4, -3)
STACK = (3, 0, 4, 2)
SAME = (
    (3, 1), (0, 1), (4, 1),
    (3, 2), (0, 2), (4, 2),
    (0, 3), (4, 3),
)
CROSS = (
    (3, 5), (0, 5), (4, 5),
    (0, 7), (4, 7), (2, 7),
)
LATE = ((0, 6), (2, 6))
PAIRS = SAME + CROSS + LATE
DIAGONAL = PAIRS.index((4, 2))
POSITION = (11, 4, 12, 5, 0, 2, 7, 3, 1, 6, 8, 10, 13, 9, 14, 15)
CHIPS = SIDE // 2


def frame_block(column, z, index):
    if index < len(OWN):
        return column * SIDE + (z + OWN[index]) % SIDE
    return (1 - column) * SIDE + (z + OTHER[index - len(OWN)]) % SIDE


def ends_of(column, z, pair):
    p, q = PAIRS[pair]
    if pair == len(PAIRS) - 1 and column == 1:
        p = 4
    a, b = frame_block(column, z, p), frame_block(column, z, q)
    if pair == DIAGONAL and z >= SIDE // 2:
        return ((a, a), (b, b))
    return ((a, b), (b, a))


def around(a, b, n):
    return min((a - b) % n, (b - a) % n)


def distance(column, z, chip, end):
    to_column, to_z = divmod(end[0], SIDE)
    to_chip = end[1] // 4
    x, to_x = 2 * (chip % 2) + column, 2 * (to_chip % 2) + to_column
    return around(z, to_z, SIDE) + around(chip // 2, to_chip // 2, 4) + around(x, to_x, 4)


def order_of_chips(column, z):
    cost = [[0] * CHIPS for _ in range(CHIPS)]
    for k in range(CHIPS):
        for chip in range(CHIPS):
            for pair in POSITION[2 * k : 2 * k + 2]:
                far = max(distance(column, z, chip, end) for end in ends_of(column, z, pair))
                cost[k][chip] = max(cost[k][chip], 4**far)
    best = {0: (0, ())}
    for k in range(CHIPS):
        later = {}
        for taken, (value, order) in best.items():
            for chip in range(CHIPS):
                if not taken >> chip & 1:
                    entry = (value + cost[k][chip], order + (chip,))
                    key = taken | 1 << chip
                    later[key] = min(later.get(key, entry), entry)
        best = later
    return best[(1 << CHIPS) - 1][1]


def routes():
    orders, ends, diagonal = [], [], []
    for column in range(2):
        for z in range(SIDE):
            order = order_of_chips(column, z)
            orders.append(order)
            for device in range(SIDE):
                pair = POSITION[2 * order.index(device // 2) + device % 2]
                ends.append(ends_of(column, z, pair))
                diagonal.append(int(pair == DIAGONAL and z >= SIDE // 2))
    place = lambda end: end[0] * SIDE + end[1] // 2
    at = {}
    for device, pair in enumerate(ends):
        for which, end in enumerate(pair):
            at.setdefault(place(end), []).append((device, which))
    assert len(at) == len(ends) and all(len(v) == 2 for v in at.values())
    swapped = [None] * len(ends)
    for seed in range(len(ends)):
        device, enter = seed, 0
        while swapped[device] is None:
            swapped[device] = enter
            node = place(ends[device][1 - enter])
            device, enter = [e for e in at[node] if e != (device, 1 - enter)][0]
    first = [place(ends[d][swapped[d]]) for d in range(len(ends))]
    second = [place(ends[d][1 - swapped[d]]) for d in range(len(ends))]
    assert len(set(first)) == len(set(second)) == len(ends)
    half = [0] * len(ends)
    for d in range(len(ends)):
        half[first[d]] = ends[d][swapped[d]][1] % 2
    table = [a + 2 * b + 4 * c for a, b, c in zip(swapped, half, diagonal)]
    return orders, first, second, table


def lookup(step, values):
    out = jnp.int32(values[0])
    for k, value in enumerate(values):
        out = jnp.where(step == k, jnp.int32(value), out)
    return out


def iota(shape, axis):
    return lax.broadcasted_iota(jnp.int32, shape, axis)


def dot_t(a, b):
    return lax.dot_general(a, b, (((1,), (1,)), ((), ())), precision=EXACT, preferred_element_type=jnp.float32)


def product(a, b):
    return lax.dot_general(a, b, (((1,), (1,)), ((), ())), preferred_element_type=jnp.float32)


def halves(x):
    high = x.astype(jnp.bfloat16)
    return high, (x - high.astype(jnp.float32)).astype(jnp.bfloat16)


def stage(x, mass):
    local = jnp.sum(mass)
    mean = jnp.sum(x * mass, axis=1, keepdims=True) / local
    x = x - mean
    wx = x * mass
    square = jnp.sum(wx * x, axis=1, keepdims=True)
    return x, wx, mean, square[:ROWS] + square[ROWS : 2 * ROWS] + square[2 * ROWS :], local


def stage_rows(block, mass, at, core, weighted, feature):
    atoms = block.shape[1]
    _, wx, mean, square, local = stage(block[...], mass)
    high, low = halves(wx)
    for k, part in enumerate((high, high, low)):
        weighted[at * 3 * ROWS : (at + 1) * 3 * ROWS, k * atoms : (k + 1) * atoms] = part
    lane = iota((ROWS, 128), 1) - 8 * core
    out = jnp.where(lane == 51, local, jnp.where(lane == 64 - 8 * core, square, 0.0))
    for c in range(3):
        out = jnp.where(lane == 48 + c, mean[c * ROWS : (c + 1) * ROWS], out)
    feature[at] = out


def stage_columns(block, mass, at, core, centered, feature):
    atoms = block.shape[1]
    x, _, mean, square, _ = stage(block[...], mass)
    high, low = halves(x)
    for k, part in enumerate((high, low, high)):
        centered[at, : 3 * ROWS, k * atoms : (k + 1) * atoms] = part
    lane = iota((ROWS, 128), 1) - 8 * core
    out = jnp.where(lane == 65 - 8 * core, square, 0.0)
    for c in range(3):
        out = jnp.where(lane == 52 + c, mean[c * ROWS : (c + 1) * ROWS], out)
    feature[at] = out


def rest_of(tail):
    tail = jnp.where(iota((3 * ROWS, 128), 1) < 16, tail, 0.0)
    return tail[:ROWS] + pltpu.roll(tail[ROWS : 2 * ROWS], 16, 1) + pltpu.roll(tail[2 * ROWS :], 32, 1)


def put_pair(out, pair, core, value, feature):
    k, owner = divmod(POSITION.index(pair), 2)
    at = jnp.where(core == owner, k, CHIPS + k)
    out[at, : 3 * ROWS] = value[:, :128]
    out[at, 3 * ROWS :] = rest_of(value[:, 128:]) + feature


def put_groups(out, pairs, order, core, weighted, centered, row_feature, column_feature):
    for at, k in enumerate(order):
        group = [pair for pair in pairs if pair[1] == k]
        start = STACK.index(group[0][0])
        assert STACK[start : start + len(group)] == tuple(p for p, _ in group)
        values = product(weighted[start * 3 * ROWS : (start + len(group)) * 3 * ROWS], centered[at])
        for n, pair in enumerate(group):
            value = values[n * 3 * ROWS : (n + 1) * 3 * ROWS]
            put_pair(out, PAIRS.index(pair), core, value, row_feature[start + n] + column_feature[at])


def same_kernel(flags, mass_ref, own_hbm, plus2, plus4, minus3, minus4, out, weighted, row_feature, own, arrived, centered, column_feature):
    fetch = pltpu.make_async_copy(own_hbm, own, arrived)
    fetch.start()
    core = flags[2]
    mass = mass_ref[...].astype(jnp.float32)
    order = (1, 2, 3)
    for at, block in enumerate((plus2, plus4, minus3)):
        stage_columns(block, mass, at, core, centered, column_feature)
    for at, block in ((0, minus3), (2, minus4), (3, plus4)):
        stage_rows(block, mass, at, core, weighted, row_feature)
    fetch.wait()
    stage_rows(own, mass, STACK.index(0), core, weighted, row_feature)
    put_groups(out, SAME, order, core, weighted, centered, row_feature, column_feature)

    @pl.when(flags[1] == 1)
    def _():
        stage_columns(minus4, mass, 3, core, centered, column_feature)
        p, q, last = STACK.index(4), STACK.index(2), order.index(2)
        upper = product(weighted[p * 3 * ROWS : (p + 1) * 3 * ROWS], centered[3])
        lower = product(weighted[q * 3 * ROWS : (q + 1) * 3 * ROWS], centered[last])
        i, j = iota((3 * ROWS, 256), 0) % ROWS, iota((3 * ROWS, 256), 1) % ROWS
        at = iota((ROWS, 256), 1)
        on = jnp.where((i == j) & (iota((3 * ROWS, 256), 1) < 3 * ROWS), lower, 0.0)
        lane = iota((ROWS, 128), 1)
        ends = row_feature[p] + column_feature[last]
        for c in range(3):
            mine = on[c * ROWS : (c + 1) * ROWS]
            for d in range(3):
                inside = (at >= d * ROWS) & (at < (d + 1) * ROWS)
                value = jnp.sum(jnp.where(inside, mine, 0.0), axis=1, keepdims=True)
                ends = jnp.where(lane == 66 + 3 * c + d, value, ends)
        put_pair(out, DIAGONAL, core, jnp.where(i <= j, upper, lower), ends)


def cross_kernel(flags, mass_ref, weighted, row_feature, other2, other3, _, out, centered, column_feature):
    core = flags[2]
    mass = mass_ref[...].astype(jnp.float32)
    for at, block in enumerate((other2, other3)):
        stage_columns(block, mass, at, core, centered, column_feature)
    put_groups(out, CROSS, (5, 7), core, weighted, centered, row_feature, column_feature)


def late_kernel(flags, mass_ref, weighted, row_feature, other4, sums, send, keep, last, centered, column_feature):
    core = flags[2]
    mass = mass_ref[...].astype(jnp.float32)
    stage_columns(other4, mass, 0, core, centered, column_feature)
    values = product(weighted[3 * ROWS :], centered[0])
    other = flags[0] == 1
    for n in range(2):
        rows = values[: 3 * ROWS] if n == 0 else jnp.where(other, values[3 * ROWS : 6 * ROWS], values[6 * ROWS :])
        feature = row_feature[1] if n == 0 else jnp.where(other, row_feature[2], row_feature[3])
        at = jnp.where(core == n, 0, 1)
        last[at, : 3 * ROWS] = rows[:, :128]
        last[at, 3 * ROWS :] = rest_of(rows[:, 128:]) + feature + column_feature[0]
    keep[0] = last[0]
    send[CHIPS - 1] = last[1]
    send[: CHIPS - 1] = sums[CHIPS : 2 * CHIPS - 1]


def merge_kernel(sums, keep, taken, out):
    out[: CHIPS - 1] = sums[: CHIPS - 1] + taken[: CHIPS - 1]
    out[CHIPS - 1] = keep[0] + taken[CHIPS - 1]


def det_four(rows):
    a00, a01, a02, a03 = rows[0]
    a10, a11, a12, a13 = rows[1]
    a20, a21, a22, a23 = rows[2]
    a30, a31, a32, a33 = rows[3]
    s0 = a00 * a11 - a10 * a01
    s1 = a00 * a12 - a10 * a02
    s2 = a00 * a13 - a10 * a03
    s3 = a01 * a12 - a11 * a02
    s4 = a01 * a13 - a11 * a03
    s5 = a02 * a13 - a12 * a03
    t5 = a22 * a33 - a32 * a23
    t4 = a21 * a33 - a31 * a23
    t3 = a21 * a32 - a31 * a22
    t2 = a20 * a33 - a30 * a23
    t1 = a20 * a32 - a30 * a22
    t0 = a20 * a31 - a30 * a21
    return s0 * t5 - s1 * t4 + s2 * t3 + s3 * t2 - s4 * t1 + s5 * t0


def quaternion_fit(moment, spread_rows, spread_cols):
    sxx, sxy, sxz, syx, syy, syz, szx, szy, szz = moment
    coef_two = -2.0 * sum(m * m for m in moment)
    det_three = (
        sxx * (syy * szz - syz * szy)
        - sxy * (syx * szz - syz * szx)
        + sxz * (syx * szy - syy * szx)
    )
    coef_one = -8.0 * det_three
    rows = [
        [sxx + syy + szz, syz - szy, szx - sxz, sxy - syx],
        [syz - szy, sxx - syy - szz, sxy + syx, szx + sxz],
        [szx - sxz, sxy + syx, -sxx + syy - szz, syz + szy],
        [sxy - syx, szx + sxz, syz + szy, -sxx - syy + szz],
    ]
    coef_zero = det_four(rows)
    lam = 0.5 * (spread_rows + spread_cols)
    for turn in range(NEWTON):
        square = lam * lam
        value = (square + coef_two) * square + coef_one * lam + coef_zero
        slope = 4.0 * square * lam + 2.0 * coef_two * lam + coef_one
        lam = lam - value / slope
    return spread_rows + spread_cols - 2.0 * lam


def square_tile(x):
    return jnp.concatenate([x, jnp.zeros((128 - x.shape[0], 128), jnp.float32)], axis=0)


def fit_kernel(flags, parts, first, second):
    diagonal, swap = flags[2] == 1, flags[0] == 1
    total = parts[0]
    for a in range(1, CHIPS):
        total = total + parts[a]
    lane, row = iota((ROWS, 128), 1), iota((ROWS, 128), 0)
    rest = total[3 * ROWS :]

    gathered = jnp.zeros((ROWS, 128), jnp.float32)
    for a in range(CHIPS):
        tile = jnp.where((lane >= 48) & (lane < 64), parts[a, 3 * ROWS :], 0.0)
        gathered = gathered + pltpu.roll(tile, (16 * a - 48) % 128, 1)

    def per_sender(which):
        pick = (iota((128, 128), 0) == 8 * iota((128, 128), 1) + which).astype(jnp.float32)
        return jnp.dot(gathered, pick, precision=EXACT, preferred_element_type=jnp.float32)

    mass = per_sender(3)
    whole = jnp.sum(mass, axis=1, keepdims=True)

    def offsets(base):
        out = []
        for c in range(3):
            mean = per_sender(base + c)
            centroid = jnp.sum(mass * mean, axis=1, keepdims=True) / whole
            out.append(jnp.where(lane < SIDE, mean - centroid, 0.0))
        return out

    off_p, off_q = offsets(0), offsets(4)

    def spread(off, at):
        within = jnp.sum(jnp.where(lane == at, rest, 0.0), axis=1, keepdims=True)
        between = jnp.sum(mass * sum(o * o for o in off), axis=1, keepdims=True)
        return (within + between) / whole

    spread_p, spread_q = spread(off_p, 64), spread(off_q, 65)

    def as_row(column):
        return jnp.sum(jnp.where(row == lane, column, 0.0), axis=0, keepdims=True)

    upper = row <= lane
    corner = lane == ROWS
    row_p, row_q = as_row(spread_p), as_row(spread_q)
    spread_rows = jnp.where(upper, spread_p, jnp.where(diagonal, spread_q, spread_p))
    spread_cols = jnp.where(upper, jnp.where(diagonal, row_p, row_q), row_q)
    spread_rows = jnp.where(corner, spread_q, spread_rows)
    spread_cols = jnp.where(corner, spread_q, spread_cols)

    low_rows = jnp.concatenate([mass * jnp.where(diagonal, q, p) for p, q in zip(off_p, off_q)], axis=0)
    up_rows = jnp.concatenate([mass * p for p in off_p], axis=0)
    moment = []
    between = []
    for d in range(3):
        up = dot_t(up_rows, square_tile(jnp.where(diagonal, off_p[d], off_q[d])))
        low = dot_t(low_rows, square_tile(off_q[d]))
        between.append((up, low))
    for c in range(3):
        main = total[c * ROWS : (c + 1) * ROWS]
        tail = pltpu.roll(rest, (32 - 16 * c) % 128, 1)
        shifted = [main, pltpu.roll(main, 128 - 48, 1), jnp.where(lane < 32, pltpu.roll(main, 128 - 96, 1), tail)]
        for d in range(3):
            up, low = (b[c * ROWS : (c + 1) * ROWS] for b in between[d])
            value = shifted[d] + jnp.where(upper, up, low)
            end = jnp.sum(jnp.where(lane == 66 + 3 * c + d, rest, 0.0), axis=1, keepdims=True)
            end = end + jnp.sum(mass * off_q[c] * off_q[d], axis=1, keepdims=True)
            moment.append(jnp.where(corner, end, value) / whole)
    msd = quaternion_fit(moment, spread_rows, spread_cols)
    corner_value = jnp.sum(jnp.where(corner, msd, 0.0), axis=1, keepdims=True)
    msd = jnp.where(lane < ROWS, msd, 0.0)
    turned = square_tile(msd).T[:ROWS]
    plain_a = jnp.where(diagonal, jnp.where(upper, msd, turned), msd)
    mirrored = jnp.where(row > lane, msd, jnp.where(row == lane, corner_value, turned))
    plain_b = jnp.where(diagonal, mirrored, turned)
    first[...] = jnp.where(swap, plain_b, plain_a)
    second[...] = jnp.where(swap, plain_a, plain_b)


def join_kernel(flags, first, second, out):
    lane = iota((ROWS, 128), 1)
    a, b = first[...], second[...]
    left = jnp.where(flags[1] == 1, b, a)
    right = jnp.where(flags[1] == 1, a, b)
    out[...] = jnp.where(lane < ROWS, left, pltpu.roll(right, ROWS, 1))[:, : 2 * ROWS]


def on_device(coords, weights):
    orders, first, second, table = routes()
    frame, atom = lax.axis_index("frame"), lax.axis_index("atom")
    build_flags = jnp.stack([frame // SIDE, (frame % SIDE) // (SIDE // 2), atom % 2]).astype(jnp.int32)
    mine = jnp.asarray(np.array(table), jnp.int32)[frame * SIDE + atom]
    fit_flags = jnp.stack([mine & 1, mine >> 1 & 1, mine >> 2])
    mass = weights[None, :]

    def along(block, distance):
        route = [
            (c * SIDE + (k + distance) % SIDE, c * SIDE + k) for c in range(2) for k in range(SIDE)
        ]
        return lax.ppermute(block, "frame", route)

    def across(block):
        return lax.ppermute(block, "frame", [((f + SIDE) % (2 * SIDE), f) for f in range(2 * SIDE)])

    own = coords.reshape(3 * ROWS, coords.shape[2])
    plus2 = along(own, 2)
    minus3 = along(own, -3)
    plus4 = along(plus2, 2)
    minus4 = along(minus3, -1)
    other2 = across(plus2)
    other3 = across(minus3)
    other4 = across(plus4)

    atoms = own.shape[1]
    smem = pl.BlockSpec(memory_space=pltpu.SMEM)
    vmem = pl.BlockSpec(memory_space=pltpu.VMEM)
    params = pltpu.CompilerParams(vmem_limit_bytes=VMEM_LIMIT)

    def columns_scratch(n):
        return [pltpu.VMEM((n, 256, 3 * atoms), jnp.bfloat16), pltpu.VMEM((n, ROWS, 128), jnp.float32)]

    def cost(pairs):
        return pl.CostEstimate(flops=pairs * 2 * 3 * ROWS * 256 * atoms * 3, bytes_accessed=4_000_000, transcendentals=0)

    def sums_of(n):
        return jax.ShapeDtypeStruct((n, 4 * ROWS, 128), jnp.float32)

    sums, weighted, row_feature = pl.pallas_call(
        same_kernel,
        out_shape=[
            sums_of(2 * CHIPS),
            jax.ShapeDtypeStruct((len(STACK) * 3 * ROWS, 3 * atoms), jnp.bfloat16),
            jax.ShapeDtypeStruct((len(STACK), ROWS, 128), jnp.float32),
        ],
        in_specs=[smem, vmem, pl.BlockSpec(memory_space=pltpu.HBM)] + [vmem] * 4,
        out_specs=[vmem] * 3,
        scratch_shapes=[pltpu.VMEM(own.shape, jnp.float32), pltpu.SemaphoreType.DMA(())] + columns_scratch(4),
        compiler_params=params,
        cost_estimate=cost(len(SAME) + 1),
    )(build_flags, mass, own, plus2, plus4, minus3, minus4)
    sums = pl.pallas_call(
        cross_kernel,
        out_shape=sums_of(2 * CHIPS),
        in_specs=[smem] + [vmem] * 6,
        out_specs=vmem,
        scratch_shapes=columns_scratch(2),
        input_output_aliases={6: 0},
        compiler_params=params,
        cost_estimate=cost(len(CROSS)),
    )(build_flags, mass, weighted, row_feature, other2, other3, sums)
    send, keep = pl.pallas_call(
        late_kernel,
        out_shape=[sums_of(CHIPS), sums_of(1)],
        in_specs=[smem] + [vmem] * 5,
        out_specs=[vmem] * 2,
        scratch_shapes=[pltpu.VMEM((2, 4 * ROWS, 128), jnp.float32)] + columns_scratch(1),
        compiler_params=params,
        cost_estimate=cost(len(LATE) + 1),
    )(build_flags, mass, weighted, row_feature, other4, sums)
    taken = lax.ppermute(send, "atom", [(a, a ^ 1) for a in range(SIDE)])
    merged = pl.pallas_call(
        merge_kernel,
        out_shape=sums_of(CHIPS),
        in_specs=[vmem] * 3,
        out_specs=vmem,
        compiler_params=params,
    )(sums, keep, taken)
    groups = [[f * SIDE + 2 * chip + c for chip in orders[f]] for f in range(2 * SIDE) for c in range(2)]
    parts = lax.all_to_all(merged, ("frame", "atom"), 0, 0, axis_index_groups=groups, tiled=True)

    block = jax.ShapeDtypeStruct((ROWS, 128), jnp.float32)
    one, two = pl.pallas_call(
        fit_kernel,
        out_shape=(block, block),
        in_specs=[smem, vmem],
        out_specs=(vmem, vmem),
        compiler_params=params,
    )(fit_flags, parts)
    one = lax.ppermute(one, ("frame", "atom"), list(enumerate(first)))
    two = lax.ppermute(two, ("frame", "atom"), list(enumerate(second)))
    return pl.pallas_call(
        join_kernel,
        out_shape=jax.ShapeDtypeStruct((ROWS, 2 * ROWS), jnp.float32),
        in_specs=[smem, vmem, vmem],
        out_specs=vmem,
        compiler_params=params,
    )(fit_flags, one, two)


def solution(mesh):
    placed = (P(None, "frame", "atom"), P("atom"))
    return jax.shard_map(
        on_device, mesh=mesh, in_specs=placed, out_specs=P("frame", "atom"), check_vma=False
    )
```

```python
import functools

import jax
import jax.numpy as jnp
import numpy as np
from jax import lax
from jax.experimental import pallas as pl
from jax.experimental.pallas import tpu as pltpu
from jax.sharding import PartitionSpec as P

NEWTON = 3
ROWS = 48
SIDE = 16
EXACT = lax.Precision.HIGHEST
VMEM_LIMIT = 40 * 1024 * 1024

OWN = (0, 2, 4, -3, -4)
OTHER = (2, 4, -3)
STACK = (3, 0, 4, 2)
EARLY = (
    (3, 1), (0, 1), (4, 1),
    (3, 2), (0, 2), (4, 2),
    (0, 3), (4, 3),
    (3, 5), (0, 5), (4, 5),
    (0, 7), (4, 7), (2, 7),
)
LATE = ((0, 6), (2, 6))
PAIRS = EARLY + LATE
DIAGONAL = PAIRS.index((4, 2))
POSITION = (11, 4, 12, 5, 0, 2, 7, 3, 1, 6, 8, 10, 13, 9, 14, 15)
CHIPS = SIDE // 2


def frame_block(column, z, index):
    if index < len(OWN):
        return column * SIDE + (z + OWN[index]) % SIDE
    return (1 - column) * SIDE + (z + OTHER[index - len(OWN)]) % SIDE


def ends_of(column, z, pair):
    p, q = PAIRS[pair]
    if pair == len(PAIRS) - 1 and column == 1:
        p = 4
    a, b = frame_block(column, z, p), frame_block(column, z, q)
    if pair == DIAGONAL and z >= SIDE // 2:
        return ((a, a), (b, b))
    return ((a, b), (b, a))


def around(a, b, n):
    return min((a - b) % n, (b - a) % n)


def distance(column, z, chip, end):
    to_column, to_z = divmod(end[0], SIDE)
    to_chip = end[1] // 4
    x, to_x = 2 * (chip % 2) + column, 2 * (to_chip % 2) + to_column
    return around(z, to_z, SIDE) + around(chip // 2, to_chip // 2, 4) + around(x, to_x, 4)


def order_of_chips(column, z):
    cost = [[0] * CHIPS for _ in range(CHIPS)]
    for k in range(CHIPS):
        for chip in range(CHIPS):
            for pair in POSITION[2 * k : 2 * k + 2]:
                far = max(distance(column, z, chip, end) for end in ends_of(column, z, pair))
                cost[k][chip] = max(cost[k][chip], 4**far)
    best = {0: (0, ())}
    for k in range(CHIPS):
        later = {}
        for taken, (value, order) in best.items():
            for chip in range(CHIPS):
                if not taken >> chip & 1:
                    entry = (value + cost[k][chip], order + (chip,))
                    key = taken | 1 << chip
                    later[key] = min(later.get(key, entry), entry)
        best = later
    return best[(1 << CHIPS) - 1][1]


def routes():
    orders, ends, diagonal = [], [], []
    for column in range(2):
        for z in range(SIDE):
            order = order_of_chips(column, z)
            orders.append(order)
            for device in range(SIDE):
                pair = POSITION[2 * order.index(device // 2) + device % 2]
                ends.append(ends_of(column, z, pair))
                diagonal.append(int(pair == DIAGONAL and z >= SIDE // 2))
    place = lambda end: end[0] * SIDE + end[1] // 2
    at = {}
    for device, pair in enumerate(ends):
        for which, end in enumerate(pair):
            at.setdefault(place(end), []).append((device, which))
    assert len(at) == len(ends) and all(len(v) == 2 for v in at.values())
    swapped = [None] * len(ends)
    for seed in range(len(ends)):
        device, enter = seed, 0
        while swapped[device] is None:
            swapped[device] = enter
            node = place(ends[device][1 - enter])
            device, enter = [e for e in at[node] if e != (device, 1 - enter)][0]
    first = [place(ends[d][swapped[d]]) for d in range(len(ends))]
    second = [place(ends[d][1 - swapped[d]]) for d in range(len(ends))]
    assert len(set(first)) == len(set(second)) == len(ends)
    half = [0] * len(ends)
    for d in range(len(ends)):
        half[first[d]] = ends[d][swapped[d]][1] % 2
    table = [a + 2 * b + 4 * c for a, b, c in zip(swapped, half, diagonal)]
    return orders, first, second, table


def lookup(step, values):
    out = jnp.int32(values[0])
    for k, value in enumerate(values):
        out = jnp.where(step == k, jnp.int32(value), out)
    return out


def iota(shape, axis):
    return lax.broadcasted_iota(jnp.int32, shape, axis)


def dot_t(a, b):
    return lax.dot_general(a, b, (((1,), (1,)), ((), ())), precision=EXACT, preferred_element_type=jnp.float32)


def product(a, b):
    return lax.dot_general(a, b, (((1,), (1,)), ((), ())), preferred_element_type=jnp.float32)


def halves(x):
    high = x.astype(jnp.bfloat16)
    return high, (x - high.astype(jnp.float32)).astype(jnp.bfloat16)


def stage(x, mass):
    local = jnp.sum(mass)
    mean = jnp.sum(x * mass, axis=1, keepdims=True) / local
    x = x - mean
    wx = x * mass
    square = jnp.sum(wx * x, axis=1, keepdims=True)
    return x, wx, mean, square[:ROWS] + square[ROWS : 2 * ROWS] + square[2 * ROWS :], local


def stage_rows(block, mass, at, core, weighted, feature):
    atoms = block.shape[1]
    _, wx, mean, square, local = stage(block[...], mass)
    high, low = halves(wx)
    for k, part in enumerate((high, high, low)):
        weighted[at * 3 * ROWS : (at + 1) * 3 * ROWS, k * atoms : (k + 1) * atoms] = part
    lane = iota((ROWS, 128), 1) - 8 * core
    out = jnp.where(lane == 51, local, jnp.where(lane == 64 - 8 * core, square, 0.0))
    for c in range(3):
        out = jnp.where(lane == 48 + c, mean[c * ROWS : (c + 1) * ROWS], out)
    feature[at] = out


def stage_columns(block, mass, at, core, centered, feature):
    atoms = block.shape[1]
    x, _, mean, square, _ = stage(block[...], mass)
    high, low = halves(x)
    for k, part in enumerate((high, low, high)):
        centered[at, : 3 * ROWS, k * atoms : (k + 1) * atoms] = part
    lane = iota((ROWS, 128), 1) - 8 * core
    out = jnp.where(lane == 65 - 8 * core, square, 0.0)
    for c in range(3):
        out = jnp.where(lane == 52 + c, mean[c * ROWS : (c + 1) * ROWS], out)
    feature[at] = out


def rest_of(tail):
    tail = jnp.where(iota((3 * ROWS, 128), 1) < 16, tail, 0.0)
    return tail[:ROWS] + pltpu.roll(tail[ROWS : 2 * ROWS], 16, 1) + pltpu.roll(tail[2 * ROWS :], 32, 1)


def put_pair(out, pair, core, value, feature):
    k, owner = divmod(POSITION.index(pair), 2)
    at = jnp.where(core == owner, k, CHIPS + k)
    out[at, : 3 * ROWS] = value[:, :128]
    out[at, 3 * ROWS :] = rest_of(value[:, 128:]) + feature


def put_groups(out, pairs, order, core, weighted, centered, row_feature, column_feature):
    for at, k in enumerate(order):
        group = [pair for pair in pairs if pair[1] == k]
        start = STACK.index(group[0][0])
        assert STACK[start : start + len(group)] == tuple(p for p, _ in group)
        values = product(weighted[start * 3 * ROWS : (start + len(group)) * 3 * ROWS], centered[at])
        for n, pair in enumerate(group):
            value = values[n * 3 * ROWS : (n + 1) * 3 * ROWS]
            put_pair(out, PAIRS.index(pair), core, value, row_feature[start + n] + column_feature[at])


def first_kernel(flags, mass_ref, own, plus2, other2, other3, weighted, row_feature, centered, column_feature):
    core = flags[2]
    mass = mass_ref[...].astype(jnp.float32)
    stage_rows(own, mass, STACK.index(0), core, weighted, row_feature)
    for at, block in enumerate((plus2, other2, other3)):
        stage_columns(block, mass, at, core, centered, column_feature)


def early_kernel(
    flags, mass_ref, plus4, minus3, minus4, first_centered, first_feature, _, __,
    out, weighted, row_feature, centered, column_feature,
):
    core = flags[2]
    mass = mass_ref[...].astype(jnp.float32)
    order = (2, 3)
    for at, block in enumerate((plus4, minus3)):
        stage_columns(block, mass, at, core, centered, column_feature)
    for at, block in ((0, minus3), (2, minus4), (3, plus4)):
        stage_rows(block, mass, at, core, weighted, row_feature)
    put_groups(out, EARLY, (1, 5, 7), core, weighted, first_centered, row_feature, first_feature)
    put_groups(out, EARLY, order, core, weighted, centered, row_feature, column_feature)

    @pl.when(flags[1] == 1)
    def _():
        stage_columns(minus4, mass, 2, core, centered, column_feature)
        p, q, last = STACK.index(4), STACK.index(2), order.index(2)
        upper = product(weighted[p * 3 * ROWS : (p + 1) * 3 * ROWS], centered[2])
        lower = product(weighted[q * 3 * ROWS : (q + 1) * 3 * ROWS], centered[last])
        i, j = iota((3 * ROWS, 256), 0) % ROWS, iota((3 * ROWS, 256), 1) % ROWS
        at = iota((ROWS, 256), 1)
        on = jnp.where((i == j) & (iota((3 * ROWS, 256), 1) < 3 * ROWS), lower, 0.0)
        lane = iota((ROWS, 128), 1)
        ends = row_feature[p] + column_feature[last]
        for c in range(3):
            mine = on[c * ROWS : (c + 1) * ROWS]
            for d in range(3):
                inside = (at >= d * ROWS) & (at < (d + 1) * ROWS)
                value = jnp.sum(jnp.where(inside, mine, 0.0), axis=1, keepdims=True)
                ends = jnp.where(lane == 66 + 3 * c + d, value, ends)
        put_pair(out, DIAGONAL, core, jnp.where(i <= j, upper, lower), ends)


def late_kernel(flags, mass_ref, weighted, row_feature, other4, sums, send, keep, last, centered, column_feature):
    core = flags[2]
    mass = mass_ref[...].astype(jnp.float32)
    stage_columns(other4, mass, 0, core, centered, column_feature)
    values = product(weighted[3 * ROWS :], centered[0])
    other = flags[0] == 1
    for n in range(2):
        rows = values[: 3 * ROWS] if n == 0 else jnp.where(other, values[3 * ROWS : 6 * ROWS], values[6 * ROWS :])
        feature = row_feature[1] if n == 0 else jnp.where(other, row_feature[2], row_feature[3])
        at = jnp.where(core == n, 0, 1)
        last[at, : 3 * ROWS] = rows[:, :128]
        last[at, 3 * ROWS :] = rest_of(rows[:, 128:]) + feature + column_feature[0]
    keep[0] = last[0]
    send[CHIPS - 1] = last[1]
    send[: CHIPS - 1] = sums[CHIPS : 2 * CHIPS - 1]


def merge_kernel(sums, keep, taken, out):
    out[: CHIPS - 1] = sums[: CHIPS - 1] + taken[: CHIPS - 1]
    out[CHIPS - 1] = keep[0] + taken[CHIPS - 1]


def det_four(rows):
    a00, a01, a02, a03 = rows[0]
    a10, a11, a12, a13 = rows[1]
    a20, a21, a22, a23 = rows[2]
    a30, a31, a32, a33 = rows[3]
    s0 = a00 * a11 - a10 * a01
    s1 = a00 * a12 - a10 * a02
    s2 = a00 * a13 - a10 * a03
    s3 = a01 * a12 - a11 * a02
    s4 = a01 * a13 - a11 * a03
    s5 = a02 * a13 - a12 * a03
    t5 = a22 * a33 - a32 * a23
    t4 = a21 * a33 - a31 * a23
    t3 = a21 * a32 - a31 * a22
    t2 = a20 * a33 - a30 * a23
    t1 = a20 * a32 - a30 * a22
    t0 = a20 * a31 - a30 * a21
    return s0 * t5 - s1 * t4 + s2 * t3 + s3 * t2 - s4 * t1 + s5 * t0


def quaternion_fit(moment, spread_rows, spread_cols):
    sxx, sxy, sxz, syx, syy, syz, szx, szy, szz = moment
    coef_two = -2.0 * sum(m * m for m in moment)
    det_three = (
        sxx * (syy * szz - syz * szy)
        - sxy * (syx * szz - syz * szx)
        + sxz * (syx * szy - syy * szx)
    )
    coef_one = -8.0 * det_three
    rows = [
        [sxx + syy + szz, syz - szy, szx - sxz, sxy - syx],
        [syz - szy, sxx - syy - szz, sxy + syx, szx + sxz],
        [szx - sxz, sxy + syx, -sxx + syy - szz, syz + szy],
        [sxy - syx, szx + sxz, syz + szy, -sxx - syy + szz],
    ]
    coef_zero = det_four(rows)
    lam = 0.5 * (spread_rows + spread_cols)
    for turn in range(NEWTON):
        square = lam * lam
        value = (square + coef_two) * square + coef_one * lam + coef_zero
        slope = 4.0 * square * lam + 2.0 * coef_two * lam + coef_one
        lam = lam - value / slope
    return spread_rows + spread_cols - 2.0 * lam


def square_tile(x):
    return jnp.concatenate([x, jnp.zeros((128 - x.shape[0], 128), jnp.float32)], axis=0)


def fit_kernel(flags, parts, first, second):
    diagonal, swap = flags[2] == 1, flags[0] == 1
    total = parts[0]
    for a in range(1, CHIPS):
        total = total + parts[a]
    lane, row = iota((ROWS, 128), 1), iota((ROWS, 128), 0)
    rest = total[3 * ROWS :]

    gathered = jnp.zeros((ROWS, 128), jnp.float32)
    for a in range(CHIPS):
        tile = jnp.where((lane >= 48) & (lane < 64), parts[a, 3 * ROWS :], 0.0)
        gathered = gathered + pltpu.roll(tile, (16 * a - 48) % 128, 1)

    def per_sender(which):
        pick = (iota((128, 128), 0) == 8 * iota((128, 128), 1) + which).astype(jnp.float32)
        return jnp.dot(gathered, pick, precision=EXACT, preferred_element_type=jnp.float32)

    mass = per_sender(3)
    whole = jnp.sum(mass, axis=1, keepdims=True)

    def offsets(base):
        out = []
        for c in range(3):
            mean = per_sender(base + c)
            centroid = jnp.sum(mass * mean, axis=1, keepdims=True) / whole
            out.append(jnp.where(lane < SIDE, mean - centroid, 0.0))
        return out

    off_p, off_q = offsets(0), offsets(4)

    def spread(off, at):
        within = jnp.sum(jnp.where(lane == at, rest, 0.0), axis=1, keepdims=True)
        between = jnp.sum(mass * sum(o * o for o in off), axis=1, keepdims=True)
        return (within + between) / whole

    spread_p, spread_q = spread(off_p, 64), spread(off_q, 65)

    def as_row(column):
        return jnp.sum(jnp.where(row == lane, column, 0.0), axis=0, keepdims=True)

    upper = row <= lane
    corner = lane == ROWS
    row_p, row_q = as_row(spread_p), as_row(spread_q)
    spread_rows = jnp.where(upper, spread_p, jnp.where(diagonal, spread_q, spread_p))
    spread_cols = jnp.where(upper, jnp.where(diagonal, row_p, row_q), row_q)
    spread_rows = jnp.where(corner, spread_q, spread_rows)
    spread_cols = jnp.where(corner, spread_q, spread_cols)

    low_rows = jnp.concatenate([mass * jnp.where(diagonal, q, p) for p, q in zip(off_p, off_q)], axis=0)
    up_rows = jnp.concatenate([mass * p for p in off_p], axis=0)
    moment = []
    between = []
    for d in range(3):
        up = dot_t(up_rows, square_tile(jnp.where(diagonal, off_p[d], off_q[d])))
        low = dot_t(low_rows, square_tile(off_q[d]))
        between.append((up, low))
    for c in range(3):
        main = total[c * ROWS : (c + 1) * ROWS]
        tail = pltpu.roll(rest, (32 - 16 * c) % 128, 1)
        shifted = [main, pltpu.roll(main, 128 - 48, 1), jnp.where(lane < 32, pltpu.roll(main, 128 - 96, 1), tail)]
        for d in range(3):
            up, low = (b[c * ROWS : (c + 1) * ROWS] for b in between[d])
            value = shifted[d] + jnp.where(upper, up, low)
            end = jnp.sum(jnp.where(lane == 66 + 3 * c + d, rest, 0.0), axis=1, keepdims=True)
            end = end + jnp.sum(mass * off_q[c] * off_q[d], axis=1, keepdims=True)
            moment.append(jnp.where(corner, end, value) / whole)
    msd = quaternion_fit(moment, spread_rows, spread_cols)
    corner_value = jnp.sum(jnp.where(corner, msd, 0.0), axis=1, keepdims=True)
    msd = jnp.where(lane < ROWS, msd, 0.0)
    turned = square_tile(msd).T[:ROWS]
    plain_a = jnp.where(diagonal, jnp.where(upper, msd, turned), msd)
    mirrored = jnp.where(row > lane, msd, jnp.where(row == lane, corner_value, turned))
    plain_b = jnp.where(diagonal, mirrored, turned)
    first[...] = jnp.where(swap, plain_b, plain_a)
    second[...] = jnp.where(swap, plain_a, plain_b)


def join_kernel(flags, first, second, out):
    lane = iota((ROWS, 128), 1)
    a, b = first[...], second[...]
    left = jnp.where(flags[1] == 1, b, a)
    right = jnp.where(flags[1] == 1, a, b)
    out[...] = jnp.where(lane < ROWS, left, pltpu.roll(right, ROWS, 1))[:, : 2 * ROWS]


def on_device(coords, weights):
    orders, first, second, table = routes()
    frame, atom = lax.axis_index("frame"), lax.axis_index("atom")
    build_flags = jnp.stack([frame // SIDE, (frame % SIDE) // (SIDE // 2), atom % 2]).astype(jnp.int32)
    mine = jnp.asarray(np.array(table), jnp.int32)[frame * SIDE + atom]
    fit_flags = jnp.stack([mine & 1, mine >> 1 & 1, mine >> 2])
    mass = weights[None, :]

    def along(block, distance):
        route = [
            (c * SIDE + (k + distance) % SIDE, c * SIDE + k) for c in range(2) for k in range(SIDE)
        ]
        return lax.ppermute(block, "frame", route)

    def across(block):
        return lax.ppermute(block, "frame", [((f + SIDE) % (2 * SIDE), f) for f in range(2 * SIDE)])

    own = coords.reshape(3 * ROWS, coords.shape[2])
    plus2 = along(own, 2)
    minus3 = along(own, -3)
    plus4 = along(plus2, 2)
    minus4 = along(minus3, -1)
    other2 = across(plus2)
    other3 = across(minus3)
    other4 = across(plus4)

    atoms = own.shape[1]
    smem = pl.BlockSpec(memory_space=pltpu.SMEM)
    vmem = pl.BlockSpec(memory_space=pltpu.VMEM)
    params = pltpu.CompilerParams(vmem_limit_bytes=VMEM_LIMIT)

    def columns_scratch(n):
        return [pltpu.VMEM((n, 256, 3 * atoms), jnp.bfloat16), pltpu.VMEM((n, ROWS, 128), jnp.float32)]

    def cost(pairs):
        return pl.CostEstimate(flops=pairs * 2 * 3 * ROWS * 256 * atoms * 3, bytes_accessed=4_000_000, transcendentals=0)

    def sums_of(n):
        return jax.ShapeDtypeStruct((n, 4 * ROWS, 128), jnp.float32)

    staged = [
        jax.ShapeDtypeStruct((len(STACK) * 3 * ROWS, 3 * atoms), jnp.bfloat16),
        jax.ShapeDtypeStruct((len(STACK), ROWS, 128), jnp.float32),
    ]
    columns = [
        jax.ShapeDtypeStruct((3, 256, 3 * atoms), jnp.bfloat16),
        jax.ShapeDtypeStruct((3, ROWS, 128), jnp.float32),
    ]
    weighted, row_feature, centered, column_feature = pl.pallas_call(
        first_kernel,
        out_shape=staged + columns,
        in_specs=[smem] + [vmem] * 5,
        out_specs=[vmem] * 4,
        compiler_params=params,
        cost_estimate=cost(len(EARLY)),
    )(build_flags, mass, own, plus2, other2, other3)
    sums, weighted, row_feature = pl.pallas_call(
        early_kernel,
        out_shape=[sums_of(2 * CHIPS)] + staged,
        in_specs=[smem] + [vmem] * 8,
        out_specs=[vmem] * 3,
        scratch_shapes=columns_scratch(3),
        input_output_aliases={7: 1, 8: 2},
        compiler_params=params,
        cost_estimate=cost(len(EARLY) + 1),
    )(build_flags, mass, plus4, minus3, minus4, centered, column_feature, weighted, row_feature)
    send, keep = pl.pallas_call(
        late_kernel,
        out_shape=[sums_of(CHIPS), sums_of(1)],
        in_specs=[smem] + [vmem] * 5,
        out_specs=[vmem] * 2,
        scratch_shapes=[pltpu.VMEM((2, 4 * ROWS, 128), jnp.float32)] + columns_scratch(1),
        compiler_params=params,
        cost_estimate=cost(len(LATE) + 1),
    )(build_flags, mass, weighted, row_feature, other4, sums)
    taken = lax.ppermute(send, "atom", [(a, a ^ 1) for a in range(SIDE)])
    merged = pl.pallas_call(
        merge_kernel,
        out_shape=sums_of(CHIPS),
        in_specs=[vmem] * 3,
        out_specs=vmem,
        compiler_params=params,
    )(sums, keep, taken)
    groups = [[f * SIDE + 2 * chip + c for chip in orders[f]] for f in range(2 * SIDE) for c in range(2)]
    parts = lax.all_to_all(merged, ("frame", "atom"), 0, 0, axis_index_groups=groups, tiled=True)

    block = jax.ShapeDtypeStruct((ROWS, 128), jnp.float32)
    one, two = pl.pallas_call(
        fit_kernel,
        out_shape=(block, block),
        in_specs=[smem, vmem],
        out_specs=(vmem, vmem),
        compiler_params=params,
    )(fit_flags, parts)
    one = lax.ppermute(one, ("frame", "atom"), list(enumerate(first)))
    two = lax.ppermute(two, ("frame", "atom"), list(enumerate(second)))
    return pl.pallas_call(
        join_kernel,
        out_shape=jax.ShapeDtypeStruct((ROWS, 2 * ROWS), jnp.float32),
        in_specs=[smem, vmem, vmem],
        out_specs=vmem,
        compiler_params=params,
    )(fit_flags, one, two)


def solution(mesh):
    placed = (P(None, "frame", "atom"), P("atom"))
    return jax.shard_map(
        on_device, mesh=mesh, in_specs=placed, out_specs=P("frame", "atom"), check_vma=False
    )
```

```python
import functools

import jax
import jax.numpy as jnp
import numpy as np
from jax import lax
from jax.experimental import pallas as pl
from jax.experimental.pallas import tpu as pltpu
from jax.sharding import PartitionSpec as P

NEWTON = 3
ROWS = 48
SIDE = 16
EXACT = lax.Precision.HIGHEST
VMEM_LIMIT = 40 * 1024 * 1024

OWN = (0, 2, 4, -3, -4)
OTHER = (2, 4, -3)
STACK = (3, 0, 4, 2)
EARLY = (
    (3, 1), (0, 1), (4, 1),
    (3, 2), (0, 2), (4, 2),
    (0, 3), (4, 3),
    (3, 5), (0, 5), (4, 5),
    (0, 7), (4, 7), (2, 7),
)
LATE = ((0, 6), (2, 6))
PAIRS = EARLY + LATE
DIAGONAL = PAIRS.index((4, 2))
POSITION = (13, 9, 5, 3, 8, 10, 11, 4, 12, 7, 2, 0, 6, 1, 14, 15)
CHIPS = SIDE // 2


def frame_block(column, z, index):
    if index < len(OWN):
        return column * SIDE + (z + OWN[index]) % SIDE
    return (1 - column) * SIDE + (z + OTHER[index - len(OWN)]) % SIDE


def ends_of(column, z, pair):
    p, q = PAIRS[pair]
    if pair == len(PAIRS) - 1 and column == 1:
        p = 4
    a, b = frame_block(column, z, p), frame_block(column, z, q)
    if pair == DIAGONAL and z >= SIDE // 2:
        return ((a, a), (b, b))
    return ((a, b), (b, a))


def around(a, b, n):
    return min((a - b) % n, (b - a) % n)


def distance(column, z, chip, end):
    to_column, to_z = divmod(end[0], SIDE)
    to_chip = end[1] // 4
    x, to_x = 2 * (chip % 2) + column, 2 * (to_chip % 2) + to_column
    return around(z, to_z, SIDE) + around(chip // 2, to_chip // 2, 4) + around(x, to_x, 4)


def order_of_chips(column, z):
    cost = [[0] * CHIPS for _ in range(CHIPS)]
    for k in range(CHIPS):
        for chip in range(CHIPS):
            for pair in POSITION[2 * k : 2 * k + 2]:
                far = [distance(column, z, chip, end) for end in ends_of(column, z, pair)]
                cost[k][chip] += 2 ** sum(far) + 2 * 4 ** max(far)
    best = {0: (0, ())}
    for k in range(CHIPS):
        later = {}
        for taken, (value, order) in best.items():
            for chip in range(CHIPS):
                if not taken >> chip & 1:
                    entry = (value + cost[k][chip], order + (chip,))
                    key = taken | 1 << chip
                    later[key] = min(later.get(key, entry), entry)
        best = later
    return best[(1 << CHIPS) - 1][1]


def routes():
    orders, ends, diagonal = [], [], []
    for column in range(2):
        for z in range(SIDE):
            order = order_of_chips(column, z)
            orders.append(order)
            for device in range(SIDE):
                pair = POSITION[2 * order.index(device // 2) + device % 2]
                ends.append(ends_of(column, z, pair))
                diagonal.append(int(pair == DIAGONAL and z >= SIDE // 2))
    place = lambda end: end[0] * SIDE + end[1] // 2
    at = {}
    for device, pair in enumerate(ends):
        for which, end in enumerate(pair):
            at.setdefault(place(end), []).append((device, which))
    assert len(at) == len(ends) and all(len(v) == 2 for v in at.values())
    swapped = [None] * len(ends)
    for seed in range(len(ends)):
        device, enter = seed, 0
        while swapped[device] is None:
            swapped[device] = enter
            node = place(ends[device][1 - enter])
            device, enter = [e for e in at[node] if e != (device, 1 - enter)][0]
    first = [place(ends[d][swapped[d]]) for d in range(len(ends))]
    second = [place(ends[d][1 - swapped[d]]) for d in range(len(ends))]
    assert len(set(first)) == len(set(second)) == len(ends)
    half = [0] * len(ends)
    for d in range(len(ends)):
        half[first[d]] = ends[d][swapped[d]][1] % 2
    table = [a + 2 * b + 4 * c for a, b, c in zip(swapped, half, diagonal)]
    return orders, first, second, table


def lookup(step, values):
    out = jnp.int32(values[0])
    for k, value in enumerate(values):
        out = jnp.where(step == k, jnp.int32(value), out)
    return out


def iota(shape, axis):
    return lax.broadcasted_iota(jnp.int32, shape, axis)


def dot_t(a, b):
    return lax.dot_general(a, b, (((1,), (1,)), ((), ())), precision=EXACT, preferred_element_type=jnp.float32)


def product(a, b):
    return lax.dot_general(a, b, (((1,), (1,)), ((), ())), preferred_element_type=jnp.float32)


def halves(x):
    high = x.astype(jnp.bfloat16)
    return high, (x - high.astype(jnp.float32)).astype(jnp.bfloat16)


def stage(x, mass):
    local = jnp.sum(mass)
    mean = jnp.sum(x * mass, axis=1, keepdims=True) / local
    x = x - mean
    wx = x * mass
    square = jnp.sum(wx * x, axis=1, keepdims=True)
    return x, wx, mean, square[:ROWS] + square[ROWS : 2 * ROWS] + square[2 * ROWS :], local


def stage_rows(block, mass, at, core, weighted, feature):
    atoms = block.shape[1]
    _, wx, mean, square, local = stage(block[...], mass)
    high, low = halves(wx)
    for k, part in enumerate((high, high, low)):
        weighted[at * 3 * ROWS : (at + 1) * 3 * ROWS, k * atoms : (k + 1) * atoms] = part
    lane = iota((ROWS, 128), 1) - 8 * core
    out = jnp.where(lane == 51, local, jnp.where(lane == 64 - 8 * core, square, 0.0))
    for c in range(3):
        out = jnp.where(lane == 48 + c, mean[c * ROWS : (c + 1) * ROWS], out)
    feature[at] = out


def stage_columns(block, mass, at, core, centered, feature):
    atoms = block.shape[1]
    x, _, mean, square, _ = stage(block[...], mass)
    high, low = halves(x)
    for k, part in enumerate((high, low, high)):
        centered[at, : 3 * ROWS, k * atoms : (k + 1) * atoms] = part
    lane = iota((ROWS, 128), 1) - 8 * core
    out = jnp.where(lane == 65 - 8 * core, square, 0.0)
    for c in range(3):
        out = jnp.where(lane == 52 + c, mean[c * ROWS : (c + 1) * ROWS], out)
    feature[at] = out


def rest_of(tail):
    tail = jnp.where(iota((3 * ROWS, 128), 1) < 16, tail, 0.0)
    return tail[:ROWS] + pltpu.roll(tail[ROWS : 2 * ROWS], 16, 1) + pltpu.roll(tail[2 * ROWS :], 32, 1)


def put_pair(out, pair, core, value, feature):
    k, owner = divmod(POSITION.index(pair), 2)
    at = jnp.where(core == owner, k, CHIPS + k)
    out[at, : 3 * ROWS] = value[:, :128]
    out[at, 3 * ROWS :] = rest_of(value[:, 128:]) + feature


def put_groups(out, pairs, order, core, weighted, centered, row_feature, column_feature):
    for at, k in enumerate(order):
        group = [pair for pair in pairs if pair[1] == k]
        start = STACK.index(group[0][0])
        assert STACK[start : start + len(group)] == tuple(p for p, _ in group)
        values = product(weighted[start * 3 * ROWS : (start + len(group)) * 3 * ROWS], centered[at])
        for n, pair in enumerate(group):
            value = values[n * 3 * ROWS : (n + 1) * 3 * ROWS]
            put_pair(out, PAIRS.index(pair), core, value, row_feature[start + n] + column_feature[at])


def first_kernel(flags, mass_ref, own, plus2, other2, other3, weighted, row_feature, centered, column_feature):
    core = flags[2]
    mass = mass_ref[...].astype(jnp.float32)
    stage_rows(own, mass, STACK.index(0), core, weighted, row_feature)
    for at, block in enumerate((plus2, other2, other3)):
        stage_columns(block, mass, at, core, centered, column_feature)


def early_kernel(
    flags, mass_ref, plus4, minus3, minus4, first_centered, first_feature, _, __,
    out, weighted, row_feature, centered, column_feature,
):
    core = flags[2]
    mass = mass_ref[...].astype(jnp.float32)
    order = (2, 3)
    for at, block in enumerate((plus4, minus3)):
        stage_columns(block, mass, at, core, centered, column_feature)
    for at, block in ((0, minus3), (2, minus4), (3, plus4)):
        stage_rows(block, mass, at, core, weighted, row_feature)
    put_groups(out, EARLY, (1, 5, 7), core, weighted, first_centered, row_feature, first_feature)
    put_groups(out, EARLY, order, core, weighted, centered, row_feature, column_feature)

    @pl.when(flags[1] == 1)
    def _():
        stage_columns(minus4, mass, 2, core, centered, column_feature)
        p, q, last = STACK.index(4), STACK.index(2), order.index(2)
        upper = product(weighted[p * 3 * ROWS : (p + 1) * 3 * ROWS], centered[2])
        lower = product(weighted[q * 3 * ROWS : (q + 1) * 3 * ROWS], centered[last])
        i, j = iota((3 * ROWS, 256), 0) % ROWS, iota((3 * ROWS, 256), 1) % ROWS
        at = iota((ROWS, 256), 1)
        on = jnp.where((i == j) & (iota((3 * ROWS, 256), 1) < 3 * ROWS), lower, 0.0)
        lane = iota((ROWS, 128), 1)
        ends = row_feature[p] + column_feature[last]
        for c in range(3):
            mine = on[c * ROWS : (c + 1) * ROWS]
            for d in range(3):
                inside = (at >= d * ROWS) & (at < (d + 1) * ROWS)
                value = jnp.sum(jnp.where(inside, mine, 0.0), axis=1, keepdims=True)
                ends = jnp.where(lane == 66 + 3 * c + d, value, ends)
        put_pair(out, DIAGONAL, core, jnp.where(i <= j, upper, lower), ends)


def late_kernel(flags, mass_ref, weighted, row_feature, other4, sums, send, keep, last, centered, column_feature):
    core = flags[2]
    mass = mass_ref[...].astype(jnp.float32)
    stage_columns(other4, mass, 0, core, centered, column_feature)
    values = product(weighted[3 * ROWS :], centered[0])
    other = flags[0] == 1
    for n in range(2):
        rows = values[: 3 * ROWS] if n == 0 else jnp.where(other, values[3 * ROWS : 6 * ROWS], values[6 * ROWS :])
        feature = row_feature[1] if n == 0 else jnp.where(other, row_feature[2], row_feature[3])
        at = jnp.where(core == n, 0, 1)
        last[at, : 3 * ROWS] = rows[:, :128]
        last[at, 3 * ROWS :] = rest_of(rows[:, 128:]) + feature + column_feature[0]
    keep[0] = last[0]
    send[CHIPS - 1] = last[1]
    send[: CHIPS - 1] = sums[CHIPS : 2 * CHIPS - 1]


def merge_kernel(sums, keep, taken, out):
    out[: CHIPS - 1] = sums[: CHIPS - 1] + taken[: CHIPS - 1]
    out[CHIPS - 1] = keep[0] + taken[CHIPS - 1]


def det_four(rows):
    a00, a01, a02, a03 = rows[0]
    a10, a11, a12, a13 = rows[1]
    a20, a21, a22, a23 = rows[2]
    a30, a31, a32, a33 = rows[3]
    s0 = a00 * a11 - a10 * a01
    s1 = a00 * a12 - a10 * a02
    s2 = a00 * a13 - a10 * a03
    s3 = a01 * a12 - a11 * a02
    s4 = a01 * a13 - a11 * a03
    s5 = a02 * a13 - a12 * a03
    t5 = a22 * a33 - a32 * a23
    t4 = a21 * a33 - a31 * a23
    t3 = a21 * a32 - a31 * a22
    t2 = a20 * a33 - a30 * a23
    t1 = a20 * a32 - a30 * a22
    t0 = a20 * a31 - a30 * a21
    return s0 * t5 - s1 * t4 + s2 * t3 + s3 * t2 - s4 * t1 + s5 * t0


def quaternion_fit(moment, spread_rows, spread_cols):
    sxx, sxy, sxz, syx, syy, syz, szx, szy, szz = moment
    coef_two = -2.0 * sum(m * m for m in moment)
    det_three = (
        sxx * (syy * szz - syz * szy)
        - sxy * (syx * szz - syz * szx)
        + sxz * (syx * szy - syy * szx)
    )
    coef_one = -8.0 * det_three
    rows = [
        [sxx + syy + szz, syz - szy, szx - sxz, sxy - syx],
        [syz - szy, sxx - syy - szz, sxy + syx, szx + sxz],
        [szx - sxz, sxy + syx, -sxx + syy - szz, syz + szy],
        [sxy - syx, szx + sxz, syz + szy, -sxx - syy + szz],
    ]
    coef_zero = det_four(rows)
    lam = 0.5 * (spread_rows + spread_cols)
    for turn in range(NEWTON):
        square = lam * lam
        value = (square + coef_two) * square + coef_one * lam + coef_zero
        slope = 4.0 * square * lam + 2.0 * coef_two * lam + coef_one
        lam = lam - value / slope
    return spread_rows + spread_cols - 2.0 * lam


def square_tile(x):
    return jnp.concatenate([x, jnp.zeros((128 - x.shape[0], 128), jnp.float32)], axis=0)


def fit_kernel(flags, parts, first, second):
    diagonal, swap = flags[1] == 1, flags[0] == 1
    total = parts[0]
    for a in range(1, CHIPS):
        total = total + parts[a]
    lane, row = iota((ROWS, 128), 1), iota((ROWS, 128), 0)
    rest = total[3 * ROWS :]

    gathered = jnp.zeros((ROWS, 128), jnp.float32)
    for a in range(CHIPS):
        tile = jnp.where((lane >= 48) & (lane < 64), parts[a, 3 * ROWS :], 0.0)
        gathered = gathered + pltpu.roll(tile, (16 * a - 48) % 128, 1)

    sender = lane % 8 == 0

    def per_sender(which):
        return jnp.where(sender, pltpu.roll(gathered, (128 - which) % 128, 1), 0.0)

    mass = per_sender(3)
    whole = jnp.sum(mass, axis=1, keepdims=True)

    def offsets(base):
        out = []
        for c in range(3):
            mean = per_sender(base + c)
            centroid = jnp.sum(mass * mean, axis=1, keepdims=True) / whole
            out.append(jnp.where(sender, mean - centroid, 0.0))
        return out

    off_p, off_q = offsets(0), offsets(4)

    def spread(off, at):
        within = jnp.sum(jnp.where(lane == at, rest, 0.0), axis=1, keepdims=True)
        between = jnp.sum(mass * sum(o * o for o in off), axis=1, keepdims=True)
        return (within + between) / whole

    spread_p, spread_q = spread(off_p, 64), spread(off_q, 65)

    def as_row(column):
        return jnp.sum(jnp.where(row == lane, column, 0.0), axis=0, keepdims=True)

    upper = row <= lane
    corner = lane == ROWS
    row_p, row_q = as_row(spread_p), as_row(spread_q)
    spread_rows = jnp.where(upper, spread_p, jnp.where(diagonal, spread_q, spread_p))
    spread_cols = jnp.where(upper, jnp.where(diagonal, row_p, row_q), row_q)
    spread_rows = jnp.where(corner, spread_q, spread_rows)
    spread_cols = jnp.where(corner, spread_q, spread_cols)

    def parts_of(blocks, first):
        high, low = halves(jnp.concatenate(blocks, axis=0))
        return jnp.concatenate([high, high, low] if first else [high, low, high], axis=1)

    up_rows = parts_of([mass * p for p in off_p], True)
    low_rows = parts_of([mass * jnp.where(diagonal, q, p) for p, q in zip(off_p, off_q)], True)
    moment = []
    between = []
    for d in range(3):
        up = product(up_rows, parts_of([square_tile(jnp.where(diagonal, off_p[d], off_q[d]))], False))
        low = product(low_rows, parts_of([square_tile(off_q[d])], False))
        between.append((up, low))
    for c in range(3):
        main = total[c * ROWS : (c + 1) * ROWS]
        tail = pltpu.roll(rest, (32 - 16 * c) % 128, 1)
        shifted = [main, pltpu.roll(main, 128 - 48, 1), jnp.where(lane < 32, pltpu.roll(main, 128 - 96, 1), tail)]
        for d in range(3):
            up, low = (b[c * ROWS : (c + 1) * ROWS] for b in between[d])
            value = shifted[d] + jnp.where(upper, up, low)
            end = jnp.sum(jnp.where(lane == 66 + 3 * c + d, rest, 0.0), axis=1, keepdims=True)
            end = end + jnp.sum(mass * off_q[c] * off_q[d], axis=1, keepdims=True)
            moment.append(jnp.where(corner, end, value) / whole)
    msd = quaternion_fit(moment, spread_rows, spread_cols)
    corner_value = jnp.sum(jnp.where(corner, msd, 0.0), axis=1, keepdims=True)
    msd = jnp.where(lane < ROWS, msd, 0.0)
    turned = square_tile(msd).T[:ROWS]
    plain_a = jnp.where(diagonal, jnp.where(upper, msd, turned), msd)
    mirrored = jnp.where(row > lane, msd, jnp.where(row == lane, corner_value, turned))
    plain_b = jnp.where(diagonal, mirrored, turned)
    first[...] = jnp.where(swap, plain_b, plain_a)
    second[...] = jnp.where(swap, plain_a, plain_b)


def on_device(coords, weights):
    orders, first, second, table = routes()
    frame, atom = lax.axis_index("frame"), lax.axis_index("atom")
    build_flags = jnp.stack([frame // SIDE, (frame % SIDE) // (SIDE // 2), atom % 2]).astype(jnp.int32)
    mine = jnp.asarray(np.array(table), jnp.int32)[frame * SIDE + atom]
    fit_flags = jnp.stack([mine & 1, mine >> 2])
    mass = weights[None, :]

    def along(block, distance):
        route = [
            (c * SIDE + (k + distance) % SIDE, c * SIDE + k) for c in range(2) for k in range(SIDE)
        ]
        return lax.ppermute(block, "frame", route)

    def across(block):
        return lax.ppermute(block, "frame", [((f + SIDE) % (2 * SIDE), f) for f in range(2 * SIDE)])

    own = coords.reshape(3 * ROWS, coords.shape[2])
    plus2 = along(own, 2)
    minus3 = along(own, -3)
    plus4 = along(plus2, 2)
    minus4 = along(minus3, -1)
    other2 = across(plus2)
    other3 = across(minus3)
    other4 = across(plus4)

    atoms = own.shape[1]
    smem = pl.BlockSpec(memory_space=pltpu.SMEM)
    vmem = pl.BlockSpec(memory_space=pltpu.VMEM)
    params = pltpu.CompilerParams(vmem_limit_bytes=VMEM_LIMIT)

    def columns_scratch(n):
        return [pltpu.VMEM((n, 256, 3 * atoms), jnp.bfloat16), pltpu.VMEM((n, ROWS, 128), jnp.float32)]

    def cost(pairs):
        return pl.CostEstimate(flops=pairs * 2 * 3 * ROWS * 256 * atoms * 3, bytes_accessed=4_000_000, transcendentals=0)

    def sums_of(n):
        return jax.ShapeDtypeStruct((n, 4 * ROWS, 128), jnp.float32)

    staged = [
        jax.ShapeDtypeStruct((len(STACK) * 3 * ROWS, 3 * atoms), jnp.bfloat16),
        jax.ShapeDtypeStruct((len(STACK), ROWS, 128), jnp.float32),
    ]
    columns = [
        jax.ShapeDtypeStruct((3, 256, 3 * atoms), jnp.bfloat16),
        jax.ShapeDtypeStruct((3, ROWS, 128), jnp.float32),
    ]
    weighted, row_feature, centered, column_feature = pl.pallas_call(
        first_kernel,
        out_shape=staged + columns,
        in_specs=[smem] + [vmem] * 5,
        out_specs=[vmem] * 4,
        compiler_params=params,
        cost_estimate=cost(len(EARLY)),
    )(build_flags, mass, own, plus2, other2, other3)
    sums, weighted, row_feature = pl.pallas_call(
        early_kernel,
        out_shape=[sums_of(2 * CHIPS)] + staged,
        in_specs=[smem] + [vmem] * 8,
        out_specs=[vmem] * 3,
        scratch_shapes=columns_scratch(3),
        input_output_aliases={7: 1, 8: 2},
        compiler_params=params,
        cost_estimate=cost(len(EARLY) + 1),
    )(build_flags, mass, plus4, minus3, minus4, centered, column_feature, weighted, row_feature)
    send, keep = pl.pallas_call(
        late_kernel,
        out_shape=[sums_of(CHIPS), sums_of(1)],
        in_specs=[smem] + [vmem] * 5,
        out_specs=[vmem] * 2,
        scratch_shapes=[pltpu.VMEM((2, 4 * ROWS, 128), jnp.float32)] + columns_scratch(1),
        compiler_params=params,
        cost_estimate=cost(len(LATE) + 1),
    )(build_flags, mass, weighted, row_feature, other4, sums)
    taken = lax.ppermute(send, "atom", [(a, a ^ 1) for a in range(SIDE)])
    merged = pl.pallas_call(
        merge_kernel,
        out_shape=sums_of(CHIPS),
        in_specs=[vmem] * 3,
        out_specs=vmem,
        compiler_params=params,
    )(sums, keep, taken)
    groups = [[f * SIDE + 2 * chip + c for chip in orders[f]] for f in range(2 * SIDE) for c in range(2)]
    parts = lax.all_to_all(merged, ("frame", "atom"), 0, 0, axis_index_groups=groups, tiled=True)

    block = jax.ShapeDtypeStruct((ROWS, 128), jnp.float32)
    one, two = pl.pallas_call(
        fit_kernel,
        out_shape=(block, block),
        in_specs=[smem, vmem],
        out_specs=(vmem, vmem),
        compiler_params=params,
    )(fit_flags, parts)
    one = lax.ppermute(one, ("frame", "atom"), list(enumerate(first)))
    two = lax.ppermute(two, ("frame", "atom"), list(enumerate(second)))
    left = jnp.where(mine >> 1 & 1, two, one)
    right = jnp.where(mine >> 1 & 1, one, two)
    return jnp.concatenate([left[:, :ROWS], right[:, :ROWS]], axis=1)


def solution(mesh):
    placed = (P(None, "frame", "atom"), P("atom"))
    return jax.shard_map(
        on_device, mesh=mesh, in_specs=placed, out_specs=P("frame", "atom"), check_vma=False
    )
```

```python
import functools

import jax
import jax.numpy as jnp
import numpy as np
from jax import lax
from jax.experimental import pallas as pl
from jax.experimental.pallas import tpu as pltpu
from jax.sharding import PartitionSpec as P

NEWTON = 3
ROWS = 48
SIDE = 16
EXACT = lax.Precision.HIGHEST
VMEM_LIMIT = 40 * 1024 * 1024

OWN = (0, 2, 4, -3, -4)
OTHER = (2, 4, -3)
STACK = (3, 0, 4, 2)
EARLY = (
    (3, 1), (0, 1), (4, 1),
    (3, 2), (0, 2), (4, 2),
    (0, 3), (4, 3),
    (3, 5), (0, 5), (4, 5),
    (0, 7), (4, 7), (2, 7),
)
LATE = ((0, 6), (2, 6))
PAIRS = EARLY + LATE
DIAGONAL = PAIRS.index((4, 2))
POSITION = (13, 9, 5, 3, 8, 10, 11, 4, 12, 7, 2, 0, 6, 1, 14, 15)
CHIPS = SIDE // 2
SUM_ROWS = 3 * ROWS + 32


def frame_block(column, z, index):
    if index < len(OWN):
        return column * SIDE + (z + OWN[index]) % SIDE
    return (1 - column) * SIDE + (z + OTHER[index - len(OWN)]) % SIDE


def ends_of(column, z, pair):
    p, q = PAIRS[pair]
    if pair == len(PAIRS) - 1 and column == 1:
        p = 4
    a, b = frame_block(column, z, p), frame_block(column, z, q)
    if pair == DIAGONAL and z >= SIDE // 2:
        return ((a, a), (b, b))
    return ((a, b), (b, a))


def around(a, b, n):
    return min((a - b) % n, (b - a) % n)


def distance(column, z, chip, end):
    to_column, to_z = divmod(end[0], SIDE)
    to_chip = end[1] // 4
    x, to_x = 2 * (chip % 2) + column, 2 * (to_chip % 2) + to_column
    return around(z, to_z, SIDE) + around(chip // 2, to_chip // 2, 4) + around(x, to_x, 4)


def order_of_chips(column, z):
    cost = [[0] * CHIPS for _ in range(CHIPS)]
    for k in range(CHIPS):
        for chip in range(CHIPS):
            for pair in POSITION[2 * k : 2 * k + 2]:
                far = [distance(column, z, chip, end) for end in ends_of(column, z, pair)]
                cost[k][chip] += 2 ** sum(far) + 2 * 4 ** max(far)
    best = {0: (0, ())}
    for k in range(CHIPS):
        later = {}
        for taken, (value, order) in best.items():
            for chip in range(CHIPS):
                if not taken >> chip & 1:
                    entry = (value + cost[k][chip], order + (chip,))
                    key = taken | 1 << chip
                    later[key] = min(later.get(key, entry), entry)
        best = later
    return best[(1 << CHIPS) - 1][1]


def routes():
    orders, ends, diagonal = [], [], []
    for column in range(2):
        for z in range(SIDE):
            order = order_of_chips(column, z)
            orders.append(order)
            for device in range(SIDE):
                pair = POSITION[2 * order.index(device // 2) + device % 2]
                ends.append(ends_of(column, z, pair))
                diagonal.append(int(pair == DIAGONAL and z >= SIDE // 2))
    place = lambda end: end[0] * SIDE + end[1] // 2
    at = {}
    for device, pair in enumerate(ends):
        for which, end in enumerate(pair):
            at.setdefault(place(end), []).append((device, which))
    assert len(at) == len(ends) and all(len(v) == 2 for v in at.values())
    swapped = [None] * len(ends)
    for seed in range(len(ends)):
        device, enter = seed, 0
        while swapped[device] is None:
            swapped[device] = enter
            node = place(ends[device][1 - enter])
            device, enter = [e for e in at[node] if e != (device, 1 - enter)][0]
    first = [place(ends[d][swapped[d]]) for d in range(len(ends))]
    second = [place(ends[d][1 - swapped[d]]) for d in range(len(ends))]
    assert len(set(first)) == len(set(second)) == len(ends)
    half = [0] * len(ends)
    for d in range(len(ends)):
        half[first[d]] = ends[d][swapped[d]][1] % 2
    table = [a + 2 * b + 4 * c for a, b, c in zip(swapped, half, diagonal)]
    return orders, first, second, table


def lookup(step, values):
    out = jnp.int32(values[0])
    for k, value in enumerate(values):
        out = jnp.where(step == k, jnp.int32(value), out)
    return out


def iota(shape, axis):
    return lax.broadcasted_iota(jnp.int32, shape, axis)


def dot_t(a, b):
    return lax.dot_general(a, b, (((1,), (1,)), ((), ())), precision=EXACT, preferred_element_type=jnp.float32)


def product(a, b):
    return lax.dot_general(a, b, (((1,), (1,)), ((), ())), preferred_element_type=jnp.float32)


def halves(x):
    high = x.astype(jnp.bfloat16)
    return high, (x - high.astype(jnp.float32)).astype(jnp.bfloat16)


def stage(x, mass):
    local = jnp.sum(mass)
    mean = jnp.sum(x * mass, axis=1, keepdims=True) / local
    x = x - mean
    wx = x * mass
    square = jnp.sum(wx * x, axis=1, keepdims=True)
    return x, wx, mean, square[:ROWS] + square[ROWS : 2 * ROWS] + square[2 * ROWS :], local


def stage_rows(block, mass, at, core, weighted, feature):
    atoms = block.shape[1]
    _, wx, mean, square, local = stage(block[...], mass)
    high, low = halves(wx)
    for k, part in enumerate((high, high, low)):
        weighted[at * 3 * ROWS : (at + 1) * 3 * ROWS, k * atoms : (k + 1) * atoms] = part
    lane = iota((ROWS, 128), 1) - 8 * core
    out = jnp.where(lane == 51, local, jnp.where(lane == 64 - 8 * core, square, 0.0))
    for c in range(3):
        out = jnp.where(lane == 48 + c, mean[c * ROWS : (c + 1) * ROWS], out)
    feature[at] = out


def stage_columns(block, mass, at, core, centered, feature):
    atoms = block.shape[1]
    x, _, mean, square, _ = stage(block[...], mass)
    high, low = halves(x)
    for k, part in enumerate((high, low, high)):
        centered[at, : 3 * ROWS, k * atoms : (k + 1) * atoms] = part
    lane = iota((ROWS, 128), 1) - 8 * core
    out = jnp.where(lane == 65 - 8 * core, square, 0.0)
    for c in range(3):
        out = jnp.where(lane == 52 + c, mean[c * ROWS : (c + 1) * ROWS], out)
    feature[at] = out


def rest_of(tail):
    tail = jnp.where(iota((3 * ROWS, 128), 1) < 16, tail, 0.0)
    return tail[:ROWS] + pltpu.roll(tail[ROWS : 2 * ROWS], 16, 1) + pltpu.roll(tail[2 * ROWS :], 32, 1)


def packed(rest):
    lane, tail = iota((16, 128), 1), rest[32:]
    low = pltpu.roll(jnp.where(lane < 48, tail, 0.0), 80, 1)
    high = pltpu.roll(jnp.where(lane < 48, 0.0, tail), 32, 1)
    return rest[:32] + jnp.concatenate([low, high], axis=0)


def unpacked(rows):
    tail = jnp.where(iota((16, 128), 1) < 48, pltpu.roll(rows[:16], 48, 1), pltpu.roll(rows[16:], 96, 1))
    return jnp.concatenate([rows, tail], axis=0)


def put_pair(out, pair, core, value, feature):
    k, owner = divmod(POSITION.index(pair), 2)
    at = jnp.where(core == owner, k, CHIPS + k)
    out[at, : 3 * ROWS] = value[:, :128]
    out[at, 3 * ROWS :] = packed(rest_of(value[:, 128:]) + feature)


def put_groups(out, pairs, order, core, weighted, centered, row_feature, column_feature):
    for at, k in enumerate(order):
        group = [pair for pair in pairs if pair[1] == k]
        start = STACK.index(group[0][0])
        assert STACK[start : start + len(group)] == tuple(p for p, _ in group)
        values = product(weighted[start * 3 * ROWS : (start + len(group)) * 3 * ROWS], centered[at])
        for n, pair in enumerate(group):
            value = values[n * 3 * ROWS : (n + 1) * 3 * ROWS]
            put_pair(out, PAIRS.index(pair), core, value, row_feature[start + n] + column_feature[at])


def first_kernel(flags, mass_ref, own, plus2, other2, other3, weighted, row_feature, centered, column_feature):
    core = flags[2]
    mass = mass_ref[...].astype(jnp.float32)
    stage_rows(own, mass, STACK.index(0), core, weighted, row_feature)
    for at, block in enumerate((plus2, other2, other3)):
        stage_columns(block, mass, at, core, centered, column_feature)


def early_kernel(
    flags, mass_ref, plus4, minus3, minus4, first_centered, first_feature, _, __,
    out, weighted, row_feature, centered, column_feature,
):
    core = flags[2]
    mass = mass_ref[...].astype(jnp.float32)
    order = (2, 3)
    for at, block in enumerate((plus4, minus3)):
        stage_columns(block, mass, at, core, centered, column_feature)
    for at, block in ((0, minus3), (2, minus4), (3, plus4)):
        stage_rows(block, mass, at, core, weighted, row_feature)
    put_groups(out, EARLY, (1, 5, 7), core, weighted, first_centered, row_feature, first_feature)
    put_groups(out, EARLY, order, core, weighted, centered, row_feature, column_feature)

    @pl.when(flags[1] == 1)
    def _():
        stage_columns(minus4, mass, 2, core, centered, column_feature)
        p, q, last = STACK.index(4), STACK.index(2), order.index(2)
        upper = product(weighted[p * 3 * ROWS : (p + 1) * 3 * ROWS], centered[2])
        lower = product(weighted[q * 3 * ROWS : (q + 1) * 3 * ROWS], centered[last])
        i, j = iota((3 * ROWS, 256), 0) % ROWS, iota((3 * ROWS, 256), 1) % ROWS
        at = iota((ROWS, 256), 1)
        on = jnp.where((i == j) & (iota((3 * ROWS, 256), 1) < 3 * ROWS), lower, 0.0)
        lane = iota((ROWS, 128), 1)
        ends = row_feature[p] + column_feature[last]
        for c in range(3):
            mine = on[c * ROWS : (c + 1) * ROWS]
            for d in range(3):
                inside = (at >= d * ROWS) & (at < (d + 1) * ROWS)
                value = jnp.sum(jnp.where(inside, mine, 0.0), axis=1, keepdims=True)
                ends = jnp.where(lane == 66 + 3 * c + d, value, ends)
        put_pair(out, DIAGONAL, core, jnp.where(i <= j, upper, lower), ends)


def late_kernel(flags, mass_ref, weighted, row_feature, other4, sums, send, keep, last, centered, column_feature):
    core = flags[2]
    mass = mass_ref[...].astype(jnp.float32)
    stage_columns(other4, mass, 0, core, centered, column_feature)
    values = product(weighted[3 * ROWS :], centered[0])
    other = flags[0] == 1
    for n in range(2):
        rows = values[: 3 * ROWS] if n == 0 else jnp.where(other, values[3 * ROWS : 6 * ROWS], values[6 * ROWS :])
        feature = row_feature[1] if n == 0 else jnp.where(other, row_feature[2], row_feature[3])
        at = jnp.where(core == n, 0, 1)
        last[at, : 3 * ROWS] = rows[:, :128]
        last[at, 3 * ROWS :] = packed(rest_of(rows[:, 128:]) + feature + column_feature[0])
    keep[0] = last[0]
    send[CHIPS - 1] = last[1]
    send[: CHIPS - 1] = sums[CHIPS : 2 * CHIPS - 1]


def merge_kernel(sums, keep, taken, out):
    out[: CHIPS - 1] = sums[: CHIPS - 1] + taken[: CHIPS - 1]
    out[CHIPS - 1] = keep[0] + taken[CHIPS - 1]


def det_four(rows):
    a00, a01, a02, a03 = rows[0]
    a10, a11, a12, a13 = rows[1]
    a20, a21, a22, a23 = rows[2]
    a30, a31, a32, a33 = rows[3]
    s0 = a00 * a11 - a10 * a01
    s1 = a00 * a12 - a10 * a02
    s2 = a00 * a13 - a10 * a03
    s3 = a01 * a12 - a11 * a02
    s4 = a01 * a13 - a11 * a03
    s5 = a02 * a13 - a12 * a03
    t5 = a22 * a33 - a32 * a23
    t4 = a21 * a33 - a31 * a23
    t3 = a21 * a32 - a31 * a22
    t2 = a20 * a33 - a30 * a23
    t1 = a20 * a32 - a30 * a22
    t0 = a20 * a31 - a30 * a21
    return s0 * t5 - s1 * t4 + s2 * t3 + s3 * t2 - s4 * t1 + s5 * t0


def quaternion_fit(moment, spread_rows, spread_cols):
    sxx, sxy, sxz, syx, syy, syz, szx, szy, szz = moment
    coef_two = -2.0 * sum(m * m for m in moment)
    det_three = (
        sxx * (syy * szz - syz * szy)
        - sxy * (syx * szz - syz * szx)
        + sxz * (syx * szy - syy * szx)
    )
    coef_one = -8.0 * det_three
    rows = [
        [sxx + syy + szz, syz - szy, szx - sxz, sxy - syx],
        [syz - szy, sxx - syy - szz, sxy + syx, szx + sxz],
        [szx - sxz, sxy + syx, -sxx + syy - szz, syz + szy],
        [sxy - syx, szx + sxz, syz + szy, -sxx - syy + szz],
    ]
    coef_zero = det_four(rows)
    lam = 0.5 * (spread_rows + spread_cols)
    for turn in range(NEWTON):
        square = lam * lam
        value = (square + coef_two) * square + coef_one * lam + coef_zero
        slope = 4.0 * square * lam + 2.0 * coef_two * lam + coef_one
        lam = lam - value / slope
    return spread_rows + spread_cols - 2.0 * lam


def square_tile(x):
    return jnp.concatenate([x, jnp.zeros((128 - x.shape[0], 128), jnp.float32)], axis=0)


def fit_kernel(flags, parts, first, second):
    diagonal, swap = flags[1] == 1, flags[0] == 1
    total = parts[0]
    for a in range(1, CHIPS):
        total = total + parts[a]
    lane, row = iota((ROWS, 128), 1), iota((ROWS, 128), 0)
    rest = unpacked(total[3 * ROWS :])

    gathered = jnp.zeros((ROWS, 128), jnp.float32)
    for a in range(CHIPS):
        tile = jnp.where((lane >= 48) & (lane < 64), unpacked(parts[a, 3 * ROWS :]), 0.0)
        gathered = gathered + pltpu.roll(tile, (16 * a - 48) % 128, 1)

    sender = lane % 8 == 0

    def per_sender(which):
        return jnp.where(sender, pltpu.roll(gathered, (128 - which) % 128, 1), 0.0)

    mass = per_sender(3)
    whole = jnp.sum(mass, axis=1, keepdims=True)

    def offsets(base):
        out = []
        for c in range(3):
            mean = per_sender(base + c)
            centroid = jnp.sum(mass * mean, axis=1, keepdims=True) / whole
            out.append(jnp.where(sender, mean - centroid, 0.0))
        return out

    off_p, off_q = offsets(0), offsets(4)

    def spread(off, at):
        within = jnp.sum(jnp.where(lane == at, rest, 0.0), axis=1, keepdims=True)
        between = jnp.sum(mass * sum(o * o for o in off), axis=1, keepdims=True)
        return (within + between) / whole

    spread_p, spread_q = spread(off_p, 64), spread(off_q, 65)

    def as_row(column):
        return jnp.sum(jnp.where(row == lane, column, 0.0), axis=0, keepdims=True)

    upper = row <= lane
    corner = lane == ROWS
    row_p, row_q = as_row(spread_p), as_row(spread_q)
    spread_rows = jnp.where(upper, spread_p, jnp.where(diagonal, spread_q, spread_p))
    spread_cols = jnp.where(upper, jnp.where(diagonal, row_p, row_q), row_q)
    spread_rows = jnp.where(corner, spread_q, spread_rows)
    spread_cols = jnp.where(corner, spread_q, spread_cols)

    def parts_of(blocks, first):
        high, low = halves(jnp.concatenate(blocks, axis=0))
        return jnp.concatenate([high, high, low] if first else [high, low, high], axis=1)

    up_rows = parts_of([mass * p for p in off_p], True)
    low_rows = parts_of([mass * jnp.where(diagonal, q, p) for p, q in zip(off_p, off_q)], True)
    moment = []
    between = []
    for d in range(3):
        up = product(up_rows, parts_of([square_tile(jnp.where(diagonal, off_p[d], off_q[d]))], False))
        low = product(low_rows, parts_of([square_tile(off_q[d])], False))
        between.append((up, low))
    for c in range(3):
        main = total[c * ROWS : (c + 1) * ROWS]
        tail = pltpu.roll(rest, (32 - 16 * c) % 128, 1)
        shifted = [main, pltpu.roll(main, 128 - 48, 1), jnp.where(lane < 32, pltpu.roll(main, 128 - 96, 1), tail)]
        for d in range(3):
            up, low = (b[c * ROWS : (c + 1) * ROWS] for b in between[d])
            value = shifted[d] + jnp.where(upper, up, low)
            end = jnp.sum(jnp.where(lane == 66 + 3 * c + d, rest, 0.0), axis=1, keepdims=True)
            end = end + jnp.sum(mass * off_q[c] * off_q[d], axis=1, keepdims=True)
            moment.append(jnp.where(corner, end, value) / whole)
    msd = quaternion_fit(moment, spread_rows, spread_cols)
    corner_value = jnp.sum(jnp.where(corner, msd, 0.0), axis=1, keepdims=True)
    msd = jnp.where(lane < ROWS, msd, 0.0)
    turned = square_tile(msd).T[:ROWS]
    plain_a = jnp.where(diagonal, jnp.where(upper, msd, turned), msd)
    mirrored = jnp.where(row > lane, msd, jnp.where(row == lane, corner_value, turned))
    plain_b = jnp.where(diagonal, mirrored, turned)
    for out, here, there in ((first, plain_a, plain_b), (second, plain_b, plain_a)):
        value = jnp.where(swap, there, here)
        out[...] = value[: ROWS // 2] + pltpu.roll(value[ROWS // 2 :], 64, 1)


def on_device(coords, weights):
    orders, first, second, table = routes()
    frame, atom = lax.axis_index("frame"), lax.axis_index("atom")
    build_flags = jnp.stack([frame // SIDE, (frame % SIDE) // (SIDE // 2), atom % 2]).astype(jnp.int32)
    mine = jnp.asarray(np.array(table), jnp.int32)[frame * SIDE + atom]
    fit_flags = jnp.stack([mine & 1, mine >> 2])
    mass = weights[None, :]

    def along(block, distance):
        route = [
            (c * SIDE + (k + distance) % SIDE, c * SIDE + k) for c in range(2) for k in range(SIDE)
        ]
        return lax.ppermute(block, "frame", route)

    def across(block):
        return lax.ppermute(block, "frame", [((f + SIDE) % (2 * SIDE), f) for f in range(2 * SIDE)])

    own = coords.reshape(3 * ROWS, coords.shape[2])
    plus2 = along(own, 2)
    minus3 = along(own, -3)
    plus4 = along(plus2, 2)
    minus4 = along(minus3, -1)
    other2 = across(plus2)
    other3 = across(minus3)
    other4 = across(plus4)

    atoms = own.shape[1]
    smem = pl.BlockSpec(memory_space=pltpu.SMEM)
    vmem = pl.BlockSpec(memory_space=pltpu.VMEM)
    params = pltpu.CompilerParams(vmem_limit_bytes=VMEM_LIMIT)

    def columns_scratch(n):
        return [pltpu.VMEM((n, 256, 3 * atoms), jnp.bfloat16), pltpu.VMEM((n, ROWS, 128), jnp.float32)]

    def cost(pairs):
        return pl.CostEstimate(flops=pairs * 2 * 3 * ROWS * 256 * atoms * 3, bytes_accessed=4_000_000, transcendentals=0)

    def sums_of(n):
        return jax.ShapeDtypeStruct((n, SUM_ROWS, 128), jnp.float32)

    staged = [
        jax.ShapeDtypeStruct((len(STACK) * 3 * ROWS, 3 * atoms), jnp.bfloat16),
        jax.ShapeDtypeStruct((len(STACK), ROWS, 128), jnp.float32),
    ]
    columns = [
        jax.ShapeDtypeStruct((3, 256, 3 * atoms), jnp.bfloat16),
        jax.ShapeDtypeStruct((3, ROWS, 128), jnp.float32),
    ]
    weighted, row_feature, centered, column_feature = pl.pallas_call(
        first_kernel,
        out_shape=staged + columns,
        in_specs=[smem] + [vmem] * 5,
        out_specs=[vmem] * 4,
        compiler_params=params,
        cost_estimate=cost(len(EARLY)),
    )(build_flags, mass, own, plus2, other2, other3)
    sums, weighted, row_feature = pl.pallas_call(
        early_kernel,
        out_shape=[sums_of(2 * CHIPS)] + staged,
        in_specs=[smem] + [vmem] * 8,
        out_specs=[vmem] * 3,
        scratch_shapes=columns_scratch(3),
        input_output_aliases={7: 1, 8: 2},
        compiler_params=params,
        cost_estimate=cost(len(EARLY) + 1),
    )(build_flags, mass, plus4, minus3, minus4, centered, column_feature, weighted, row_feature)
    send, keep = pl.pallas_call(
        late_kernel,
        out_shape=[sums_of(CHIPS), sums_of(1)],
        in_specs=[smem] + [vmem] * 5,
        out_specs=[vmem] * 2,
        scratch_shapes=[pltpu.VMEM((2, SUM_ROWS, 128), jnp.float32)] + columns_scratch(1),
        compiler_params=params,
        cost_estimate=cost(len(LATE) + 1),
    )(build_flags, mass, weighted, row_feature, other4, sums)
    taken = lax.ppermute(send, "atom", [(a, a ^ 1) for a in range(SIDE)])
    merged = pl.pallas_call(
        merge_kernel,
        out_shape=sums_of(CHIPS),
        in_specs=[vmem] * 3,
        out_specs=vmem,
        compiler_params=params,
    )(sums, keep, taken)
    groups = [[f * SIDE + 2 * chip + c for chip in orders[f]] for f in range(2 * SIDE) for c in range(2)]
    parts = lax.all_to_all(merged, ("frame", "atom"), 0, 0, axis_index_groups=groups, tiled=True)

    block = jax.ShapeDtypeStruct((ROWS // 2, 128), jnp.float32)
    one, two = pl.pallas_call(
        fit_kernel,
        out_shape=(block, block),
        in_specs=[smem, vmem],
        out_specs=(vmem, vmem),
        compiler_params=params,
    )(fit_flags, parts)
    one = lax.ppermute(one, ("frame", "atom"), list(enumerate(first)))
    two = lax.ppermute(two, ("frame", "atom"), list(enumerate(second)))
    left = jnp.where(mine >> 1 & 1, two, one)
    right = jnp.where(mine >> 1 & 1, one, two)
    upper = jnp.concatenate([left[:, :ROWS], right[:, :ROWS]], axis=1)
    lower = jnp.concatenate([left[:, 64 : 64 + ROWS], right[:, 64 : 64 + ROWS]], axis=1)
    return jnp.concatenate([upper, lower], axis=0)


def solution(mesh):
    placed = (P(None, "frame", "atom"), P("atom"))
    return jax.shard_map(
        on_device, mesh=mesh, in_specs=placed, out_specs=P("frame", "atom"), check_vma=False
    )
```

```python
import functools

import jax
import jax.numpy as jnp
import numpy as np
from jax import lax
from jax.experimental import pallas as pl
from jax.experimental.pallas import tpu as pltpu
from jax.sharding import PartitionSpec as P

NEWTON = 3
ROWS = 48
SIDE = 16
EXACT = lax.Precision.HIGHEST
VMEM_LIMIT = 40 * 1024 * 1024

OWN = (0, 2, 4, -3, -4)
OTHER = (2, 4, -3)
STACK = (3, 0, 4, 2)
EARLY = (
    (3, 1), (0, 1), (4, 1),
    (3, 2), (0, 2), (4, 2),
    (0, 3), (4, 3),
    (3, 5), (0, 5), (4, 5),
    (0, 7), (4, 7), (2, 7),
)
LATE = ((0, 6), (2, 6))
PAIRS = EARLY + LATE
DIAGONAL = PAIRS.index((4, 2))
POSITION = (13, 9, 5, 3, 8, 10, 11, 4, 12, 7, 2, 0, 6, 1, 14, 15)
CHIPS = SIDE // 2
SUM_ROWS = 3 * ROWS + 32


def frame_block(column, z, index):
    if index < len(OWN):
        return column * SIDE + (z + OWN[index]) % SIDE
    return (1 - column) * SIDE + (z + OTHER[index - len(OWN)]) % SIDE


def ends_of(column, z, pair):
    p, q = PAIRS[pair]
    if pair == len(PAIRS) - 1 and column == 1:
        p = 4
    a, b = frame_block(column, z, p), frame_block(column, z, q)
    if pair == DIAGONAL and z < SIDE // 2:
        return ((a, a), (b, b))
    return ((a, b), (b, a))


def around(a, b, n):
    return min((a - b) % n, (b - a) % n)


def distance(column, z, chip, end):
    to_column, to_z = divmod(end[0], SIDE)
    to_chip = end[1] // 4
    x, to_x = 2 * (chip % 2) + column, 2 * (to_chip % 2) + to_column
    return around(z, to_z, SIDE) + around(chip // 2, to_chip // 2, 4) + around(x, to_x, 4)


def order_of_chips(column, z):
    cost = [[0] * CHIPS for _ in range(CHIPS)]
    for k in range(CHIPS):
        for chip in range(CHIPS):
            for pair in POSITION[2 * k : 2 * k + 2]:
                far = [distance(column, z, chip, end) for end in ends_of(column, z, pair)]
                cost[k][chip] += 2 ** sum(far) + 2 * 4 ** max(far)
    best = {0: (0, ())}
    for k in range(CHIPS):
        later = {}
        for taken, (value, order) in best.items():
            for chip in range(CHIPS):
                if not taken >> chip & 1:
                    entry = (value + cost[k][chip], order + (chip,))
                    key = taken | 1 << chip
                    later[key] = min(later.get(key, entry), entry)
        best = later
    return best[(1 << CHIPS) - 1][1]


def routes():
    orders, ends, diagonal = [], [], []
    for column in range(2):
        for z in range(SIDE):
            order = order_of_chips(column, z)
            orders.append(order)
            for device in range(SIDE):
                pair = POSITION[2 * order.index(device // 2) + device % 2]
                ends.append(ends_of(column, z, pair))
                diagonal.append(int(pair == DIAGONAL and z < SIDE // 2))
    place = lambda end: end[0] * SIDE + end[1] // 2
    at = {}
    for device, pair in enumerate(ends):
        for which, end in enumerate(pair):
            at.setdefault(place(end), []).append((device, which))
    assert len(at) == len(ends) and all(len(v) == 2 for v in at.values())
    swapped = [None] * len(ends)
    for seed in range(len(ends)):
        device, enter = seed, 0
        while swapped[device] is None:
            swapped[device] = enter
            node = place(ends[device][1 - enter])
            device, enter = [e for e in at[node] if e != (device, 1 - enter)][0]
    first = [place(ends[d][swapped[d]]) for d in range(len(ends))]
    second = [place(ends[d][1 - swapped[d]]) for d in range(len(ends))]
    assert len(set(first)) == len(set(second)) == len(ends)
    half = [0] * len(ends)
    for d in range(len(ends)):
        half[first[d]] = ends[d][swapped[d]][1] % 2
    table = [a + 2 * b + 4 * c for a, b, c in zip(swapped, half, diagonal)]
    return orders, first, second, table


def lookup(step, values):
    out = jnp.int32(values[0])
    for k, value in enumerate(values):
        out = jnp.where(step == k, jnp.int32(value), out)
    return out


def iota(shape, axis):
    return lax.broadcasted_iota(jnp.int32, shape, axis)


def dot_t(a, b):
    return lax.dot_general(a, b, (((1,), (1,)), ((), ())), precision=EXACT, preferred_element_type=jnp.float32)


def product(a, b):
    return lax.dot_general(a, b, (((1,), (1,)), ((), ())), preferred_element_type=jnp.float32)


def halves(x):
    high = x.astype(jnp.bfloat16)
    return high, (x - high.astype(jnp.float32)).astype(jnp.bfloat16)


def stage(x, mass):
    local = jnp.sum(mass)
    mean = jnp.sum(x * mass, axis=1, keepdims=True) / local
    x = x - mean
    wx = x * mass
    square = jnp.sum(wx * x, axis=1, keepdims=True)
    return x, wx, mean, square[:ROWS] + square[ROWS : 2 * ROWS] + square[2 * ROWS :], local


def stage_rows(block, mass, at, core, weighted, feature):
    atoms = block.shape[1]
    _, wx, mean, square, local = stage(block[...], mass)
    high, low = halves(wx)
    for k, part in enumerate((high, high, low)):
        weighted[at * 3 * ROWS : (at + 1) * 3 * ROWS, k * atoms : (k + 1) * atoms] = part
    lane = iota((ROWS, 128), 1) - 8 * core
    out = jnp.where(lane == 51, local, jnp.where(lane == 64 - 8 * core, square, 0.0))
    for c in range(3):
        out = jnp.where(lane == 48 + c, mean[c * ROWS : (c + 1) * ROWS], out)
    feature[at] = out


def stage_columns(block, mass, at, core, centered, feature):
    atoms = block.shape[1]
    x, _, mean, square, _ = stage(block[...], mass)
    high, low = halves(x)
    for k, part in enumerate((high, low, high)):
        centered[at, : 3 * ROWS, k * atoms : (k + 1) * atoms] = part
    lane = iota((ROWS, 128), 1) - 8 * core
    out = jnp.where(lane == 65 - 8 * core, square, 0.0)
    for c in range(3):
        out = jnp.where(lane == 52 + c, mean[c * ROWS : (c + 1) * ROWS], out)
    feature[at] = out


def rest_of(tail):
    tail = jnp.where(iota((3 * ROWS, 128), 1) < 16, tail, 0.0)
    return tail[:ROWS] + pltpu.roll(tail[ROWS : 2 * ROWS], 16, 1) + pltpu.roll(tail[2 * ROWS :], 32, 1)


def packed(rest):
    lane, tail = iota((16, 128), 1), rest[32:]
    low = pltpu.roll(jnp.where(lane < 48, tail, 0.0), 80, 1)
    high = pltpu.roll(jnp.where(lane < 48, 0.0, tail), 32, 1)
    return rest[:32] + jnp.concatenate([low, high], axis=0)


def unpacked(rows):
    tail = jnp.where(iota((16, 128), 1) < 48, pltpu.roll(rows[:16], 48, 1), pltpu.roll(rows[16:], 96, 1))
    return jnp.concatenate([rows, tail], axis=0)


def put_pair(out, pair, core, value, feature):
    k, owner = divmod(POSITION.index(pair), 2)
    at = jnp.where(core == owner, k, CHIPS + k)
    out[at, : 3 * ROWS] = value[:, :128]
    out[at, 3 * ROWS :] = packed(rest_of(value[:, 128:]) + feature)


def put_groups(out, pairs, order, core, weighted, centered, row_feature, column_feature):
    for at, k in enumerate(order):
        group = [pair for pair in pairs if pair[1] == k]
        start = STACK.index(group[0][0])
        assert STACK[start : start + len(group)] == tuple(p for p, _ in group)
        values = product(weighted[start * 3 * ROWS : (start + len(group)) * 3 * ROWS], centered[at])
        for n, pair in enumerate(group):
            value = values[n * 3 * ROWS : (n + 1) * 3 * ROWS]
            put_pair(out, PAIRS.index(pair), core, value, row_feature[start + n] + column_feature[at])


def first_kernel(flags, mass_ref, own, plus2, other2, other3, weighted, row_feature, centered, column_feature):
    core = flags[2]
    mass = mass_ref[...].astype(jnp.float32)
    stage_rows(own, mass, STACK.index(0), core, weighted, row_feature)
    for at, block in enumerate((plus2, other2, other3)):
        stage_columns(block, mass, at, core, centered, column_feature)


def early_kernel(
    flags, mass_ref, plus4, minus3, minus4, first_centered, first_feature, _, __,
    out, weighted, row_feature, centered, column_feature,
):
    core = flags[2]
    mass = mass_ref[...].astype(jnp.float32)
    order = (2, 3)
    for at, block in enumerate((plus4, minus3)):
        stage_columns(block, mass, at, core, centered, column_feature)
    for at, block in ((0, minus3), (2, minus4), (3, plus4)):
        stage_rows(block, mass, at, core, weighted, row_feature)
    put_groups(out, EARLY, (1, 5, 7), core, weighted, first_centered, row_feature, first_feature)
    put_groups(out, EARLY, order, core, weighted, centered, row_feature, column_feature)

    @pl.when(flags[1] == 1)
    def _():
        stage_columns(minus4, mass, 2, core, centered, column_feature)
        p, q, last = STACK.index(4), STACK.index(2), order.index(2)
        upper = product(weighted[p * 3 * ROWS : (p + 1) * 3 * ROWS], centered[2])
        lower = product(weighted[q * 3 * ROWS : (q + 1) * 3 * ROWS], centered[last])
        i, j = iota((3 * ROWS, 256), 0) % ROWS, iota((3 * ROWS, 256), 1) % ROWS
        at = iota((ROWS, 256), 1)
        on = jnp.where((i == j) & (iota((3 * ROWS, 256), 1) < 3 * ROWS), lower, 0.0)
        lane = iota((ROWS, 128), 1)
        ends = row_feature[p] + column_feature[last]
        for c in range(3):
            mine = on[c * ROWS : (c + 1) * ROWS]
            for d in range(3):
                inside = (at >= d * ROWS) & (at < (d + 1) * ROWS)
                value = jnp.sum(jnp.where(inside, mine, 0.0), axis=1, keepdims=True)
                ends = jnp.where(lane == 66 + 3 * c + d, value, ends)
        put_pair(out, DIAGONAL, core, jnp.where(i <= j, upper, lower), ends)


def late_kernel(flags, mass_ref, weighted, row_feature, other4, sums, send, keep, last, centered, column_feature):
    core = flags[2]
    mass = mass_ref[...].astype(jnp.float32)
    stage_columns(other4, mass, 0, core, centered, column_feature)
    values = product(weighted[3 * ROWS :], centered[0])
    other = flags[0] == 1
    for n in range(2):
        rows = values[: 3 * ROWS] if n == 0 else jnp.where(other, values[3 * ROWS : 6 * ROWS], values[6 * ROWS :])
        feature = row_feature[1] if n == 0 else jnp.where(other, row_feature[2], row_feature[3])
        at = jnp.where(core == n, 0, 1)
        last[at, : 3 * ROWS] = rows[:, :128]
        last[at, 3 * ROWS :] = packed(rest_of(rows[:, 128:]) + feature + column_feature[0])
    keep[0] = last[0]
    send[CHIPS - 1] = last[1]
    send[: CHIPS - 1] = sums[CHIPS : 2 * CHIPS - 1]


def merge_kernel(sums, keep, taken, out):
    out[: CHIPS - 1] = sums[: CHIPS - 1] + taken[: CHIPS - 1]
    out[CHIPS - 1] = keep[0] + taken[CHIPS - 1]


def det_four(rows):
    a00, a01, a02, a03 = rows[0]
    a10, a11, a12, a13 = rows[1]
    a20, a21, a22, a23 = rows[2]
    a30, a31, a32, a33 = rows[3]
    s0 = a00 * a11 - a10 * a01
    s1 = a00 * a12 - a10 * a02
    s2 = a00 * a13 - a10 * a03
    s3 = a01 * a12 - a11 * a02
    s4 = a01 * a13 - a11 * a03
    s5 = a02 * a13 - a12 * a03
    t5 = a22 * a33 - a32 * a23
    t4 = a21 * a33 - a31 * a23
    t3 = a21 * a32 - a31 * a22
    t2 = a20 * a33 - a30 * a23
    t1 = a20 * a32 - a30 * a22
    t0 = a20 * a31 - a30 * a21
    return s0 * t5 - s1 * t4 + s2 * t3 + s3 * t2 - s4 * t1 + s5 * t0


def quaternion_fit(moment, spread_rows, spread_cols):
    sxx, sxy, sxz, syx, syy, syz, szx, szy, szz = moment
    coef_two = -2.0 * sum(m * m for m in moment)
    det_three = (
        sxx * (syy * szz - syz * szy)
        - sxy * (syx * szz - syz * szx)
        + sxz * (syx * szy - syy * szx)
    )
    coef_one = -8.0 * det_three
    rows = [
        [sxx + syy + szz, syz - szy, szx - sxz, sxy - syx],
        [syz - szy, sxx - syy - szz, sxy + syx, szx + sxz],
        [szx - sxz, sxy + syx, -sxx + syy - szz, syz + szy],
        [sxy - syx, szx + sxz, syz + szy, -sxx - syy + szz],
    ]
    coef_zero = det_four(rows)
    lam = 0.5 * (spread_rows + spread_cols)
    for turn in range(NEWTON):
        square = lam * lam
        value = (square + coef_two) * square + coef_one * lam + coef_zero
        slope = 4.0 * square * lam + 2.0 * coef_two * lam + coef_one
        lam = lam - value / slope
    return spread_rows + spread_cols - 2.0 * lam


def square_tile(x):
    return jnp.concatenate([x, jnp.zeros((128 - x.shape[0], 128), jnp.float32)], axis=0)


def fit_kernel(flags, parts, first, second):
    diagonal, swap = flags[1] == 1, flags[0] == 1
    total = parts[0]
    for a in range(1, CHIPS):
        total = total + parts[a]
    lane, row = iota((ROWS, 128), 1), iota((ROWS, 128), 0)
    rest = unpacked(total[3 * ROWS :])

    gathered = jnp.zeros((ROWS, 128), jnp.float32)
    for a in range(CHIPS):
        tile = jnp.where((lane >= 48) & (lane < 64), unpacked(parts[a, 3 * ROWS :]), 0.0)
        gathered = gathered + pltpu.roll(tile, (16 * a - 48) % 128, 1)

    sender = lane % 8 == 0

    def per_sender(which):
        return jnp.where(sender, pltpu.roll(gathered, (128 - which) % 128, 1), 0.0)

    mass = per_sender(3)
    whole = jnp.sum(mass, axis=1, keepdims=True)

    def offsets(base):
        out = []
        for c in range(3):
            mean = per_sender(base + c)
            centroid = jnp.sum(mass * mean, axis=1, keepdims=True) / whole
            out.append(jnp.where(sender, mean - centroid, 0.0))
        return out

    off_p, off_q = offsets(0), offsets(4)

    def spread(off, at):
        within = jnp.sum(jnp.where(lane == at, rest, 0.0), axis=1, keepdims=True)
        between = jnp.sum(mass * sum(o * o for o in off), axis=1, keepdims=True)
        return (within + between) / whole

    spread_p, spread_q = spread(off_p, 64), spread(off_q, 65)

    def as_row(column):
        return jnp.sum(jnp.where(row == lane, column, 0.0), axis=0, keepdims=True)

    upper = row <= lane
    corner = lane == ROWS
    row_p, row_q = as_row(spread_p), as_row(spread_q)
    spread_rows = jnp.where(upper, spread_p, jnp.where(diagonal, spread_q, spread_p))
    spread_cols = jnp.where(upper, jnp.where(diagonal, row_p, row_q), row_q)
    spread_rows = jnp.where(corner, spread_q, spread_rows)
    spread_cols = jnp.where(corner, spread_q, spread_cols)

    def parts_of(blocks, first):
        high, low = halves(jnp.concatenate(blocks, axis=0))
        return jnp.concatenate([high, high, low] if first else [high, low, high], axis=1)

    up_rows = parts_of([mass * p for p in off_p], True)
    low_rows = parts_of([mass * jnp.where(diagonal, q, p) for p, q in zip(off_p, off_q)], True)
    moment = []
    between = []
    for d in range(3):
        up = product(up_rows, parts_of([square_tile(jnp.where(diagonal, off_p[d], off_q[d]))], False))
        low = product(low_rows, parts_of([square_tile(off_q[d])], False))
        between.append((up, low))
    for c in range(3):
        main = total[c * ROWS : (c + 1) * ROWS]
        tail = pltpu.roll(rest, (32 - 16 * c) % 128, 1)
        shifted = [main, pltpu.roll(main, 128 - 48, 1), jnp.where(lane < 32, pltpu.roll(main, 128 - 96, 1), tail)]
        for d in range(3):
            up, low = (b[c * ROWS : (c + 1) * ROWS] for b in between[d])
            value = shifted[d] + jnp.where(upper, up, low)
            end = jnp.sum(jnp.where(lane == 66 + 3 * c + d, rest, 0.0), axis=1, keepdims=True)
            end = end + jnp.sum(mass * off_q[c] * off_q[d], axis=1, keepdims=True)
            moment.append(jnp.where(corner, end, value) / whole)
    msd = quaternion_fit(moment, spread_rows, spread_cols)
    corner_value = jnp.sum(jnp.where(corner, msd, 0.0), axis=1, keepdims=True)
    msd = jnp.where(lane < ROWS, msd, 0.0)
    turned = square_tile(msd).T[:ROWS]
    plain_a = jnp.where(diagonal, jnp.where(upper, msd, turned), msd)
    mirrored = jnp.where(row > lane, msd, jnp.where(row == lane, corner_value, turned))
    plain_b = jnp.where(diagonal, mirrored, turned)
    for out, here, there in ((first, plain_a, plain_b), (second, plain_b, plain_a)):
        value = jnp.where(swap, there, here)
        out[...] = value[: ROWS // 2] + pltpu.roll(value[ROWS // 2 :], 64, 1)


def on_device(coords, weights):
    orders, first, second, table = routes()
    frame, atom = lax.axis_index("frame"), lax.axis_index("atom")
    build_flags = jnp.stack([frame // SIDE, 1 - (frame % SIDE) // (SIDE // 2), atom % 2]).astype(jnp.int32)
    mine = jnp.asarray(np.array(table), jnp.int32)[frame * SIDE + atom]
    fit_flags = jnp.stack([mine & 1, mine >> 2])
    mass = weights[None, :]

    def along(block, distance):
        route = [
            (c * SIDE + (k + distance) % SIDE, c * SIDE + k) for c in range(2) for k in range(SIDE)
        ]
        return lax.ppermute(block, "frame", route)

    def across(block):
        return lax.ppermute(block, "frame", [((f + SIDE) % (2 * SIDE), f) for f in range(2 * SIDE)])

    own = coords.reshape(3 * ROWS, coords.shape[2])
    plus2 = along(own, 2)
    minus3 = along(own, -3)
    plus4 = along(plus2, 2)
    minus4 = along(minus3, -1)
    other2 = across(plus2)
    other3 = across(minus3)
    other4 = across(plus4)

    atoms = own.shape[1]
    smem = pl.BlockSpec(memory_space=pltpu.SMEM)
    vmem = pl.BlockSpec(memory_space=pltpu.VMEM)
    params = pltpu.CompilerParams(vmem_limit_bytes=VMEM_LIMIT)

    def columns_scratch(n):
        return [pltpu.VMEM((n, 256, 3 * atoms), jnp.bfloat16), pltpu.VMEM((n, ROWS, 128), jnp.float32)]

    def cost(pairs):
        return pl.CostEstimate(flops=pairs * 2 * 3 * ROWS * 256 * atoms * 3, bytes_accessed=4_000_000, transcendentals=0)

    def sums_of(n):
        return jax.ShapeDtypeStruct((n, SUM_ROWS, 128), jnp.float32)

    staged = [
        jax.ShapeDtypeStruct((len(STACK) * 3 * ROWS, 3 * atoms), jnp.bfloat16),
        jax.ShapeDtypeStruct((len(STACK), ROWS, 128), jnp.float32),
    ]
    columns = [
        jax.ShapeDtypeStruct((3, 256, 3 * atoms), jnp.bfloat16),
        jax.ShapeDtypeStruct((3, ROWS, 128), jnp.float32),
    ]
    weighted, row_feature, centered, column_feature = pl.pallas_call(
        first_kernel,
        out_shape=staged + columns,
        in_specs=[smem] + [vmem] * 5,
        out_specs=[vmem] * 4,
        compiler_params=params,
        cost_estimate=cost(len(EARLY)),
    )(build_flags, mass, own, plus2, other2, other3)
    sums, weighted, row_feature = pl.pallas_call(
        early_kernel,
        out_shape=[sums_of(2 * CHIPS)] + staged,
        in_specs=[smem] + [vmem] * 8,
        out_specs=[vmem] * 3,
        scratch_shapes=columns_scratch(3),
        input_output_aliases={7: 1, 8: 2},
        compiler_params=params,
        cost_estimate=cost(len(EARLY) + 1),
    )(build_flags, mass, plus4, minus3, minus4, centered, column_feature, weighted, row_feature)
    send, keep = pl.pallas_call(
        late_kernel,
        out_shape=[sums_of(CHIPS), sums_of(1)],
        in_specs=[smem] + [vmem] * 5,
        out_specs=[vmem] * 2,
        scratch_shapes=[pltpu.VMEM((2, SUM_ROWS, 128), jnp.float32)] + columns_scratch(1),
        compiler_params=params,
        cost_estimate=cost(len(LATE) + 1),
    )(build_flags, mass, weighted, row_feature, other4, sums)
    taken = lax.ppermute(send, "atom", [(a, a ^ 1) for a in range(SIDE)])
    merged = pl.pallas_call(
        merge_kernel,
        out_shape=sums_of(CHIPS),
        in_specs=[vmem] * 3,
        out_specs=vmem,
        compiler_params=params,
    )(sums, keep, taken)
    groups = [[f * SIDE + 2 * chip + c for chip in orders[f]] for f in range(2 * SIDE) for c in range(2)]
    parts = lax.all_to_all(merged, ("frame", "atom"), 0, 0, axis_index_groups=groups, tiled=True)

    block = jax.ShapeDtypeStruct((ROWS // 2, 128), jnp.float32)
    one, two = pl.pallas_call(
        fit_kernel,
        out_shape=(block, block),
        in_specs=[smem, vmem],
        out_specs=(vmem, vmem),
        compiler_params=params,
    )(fit_flags, parts)
    one = lax.ppermute(one, ("frame", "atom"), list(enumerate(first)))
    two = lax.ppermute(two, ("frame", "atom"), list(enumerate(second)))
    left = jnp.where(mine >> 1 & 1, two, one)
    right = jnp.where(mine >> 1 & 1, one, two)
    upper = jnp.concatenate([left[:, :ROWS], right[:, :ROWS]], axis=1)
    lower = jnp.concatenate([left[:, 64 : 64 + ROWS], right[:, 64 : 64 + ROWS]], axis=1)
    return jnp.concatenate([upper, lower], axis=0)


def solution(mesh):
    placed = (P(None, "frame", "atom"), P("atom"))
    return jax.shard_map(
        on_device, mesh=mesh, in_specs=placed, out_specs=P("frame", "atom"), check_vma=False
    )
```

```python
import functools

import jax
import jax.numpy as jnp
import numpy as np
from jax import lax
from jax.experimental import pallas as pl
from jax.experimental.pallas import tpu as pltpu
from jax.sharding import PartitionSpec as P

NEWTON = 3
ROWS = 48
SIDE = 16
EXACT = lax.Precision.HIGHEST
VMEM_LIMIT = 40 * 1024 * 1024

OWN = (0, 2, 4, -3, -4)
OTHER = (2, 4, -3)
STACK = (3, 0, 4, 2)
EARLY = (
    (3, 1), (0, 1), (4, 1),
    (3, 2), (0, 2), (4, 2),
    (0, 3), (4, 3),
    (3, 5), (0, 5), (4, 5),
    (0, 7), (4, 7), (2, 7),
)
LATE = ((0, 6), (2, 6))
PAIRS = EARLY + LATE
DIAGONAL = PAIRS.index((4, 2))
POSITION = (13, 9, 5, 3, 8, 10, 11, 4, 12, 7, 2, 0, 6, 1, 14, 15)
CHIPS = SIDE // 2
SUM_ROWS = 3 * ROWS + 32


def frame_block(column, z, index):
    if index < len(OWN):
        return column * SIDE + (z + OWN[index]) % SIDE
    return (1 - column) * SIDE + (z + OTHER[index - len(OWN)]) % SIDE


def two_diagonals(z):
    return (z + SIDE - 2) % SIDE < SIDE // 2


def ends_of(column, z, pair):
    p, q = PAIRS[pair]
    if pair == len(PAIRS) - 1 and column == 1:
        p = 4
    a, b = frame_block(column, z, p), frame_block(column, z, q)
    if pair == DIAGONAL and two_diagonals(z):
        return ((a, a), (b, b))
    return ((a, b), (b, a))


def around(a, b, n):
    return min((a - b) % n, (b - a) % n)


def distance(column, z, chip, end):
    to_column, to_z = divmod(end[0], SIDE)
    to_chip = end[1] // 4
    x, to_x = 2 * (chip % 2) + column, 2 * (to_chip % 2) + to_column
    return around(z, to_z, SIDE) + around(chip // 2, to_chip // 2, 4) + around(x, to_x, 4)


def order_of_chips(column, z):
    cost = [[0] * CHIPS for _ in range(CHIPS)]
    for k in range(CHIPS):
        for chip in range(CHIPS):
            for pair in POSITION[2 * k : 2 * k + 2]:
                far = [distance(column, z, chip, end) for end in ends_of(column, z, pair)]
                cost[k][chip] += 2 ** sum(far) + 2 * 4 ** max(far)
    best = {0: (0, ())}
    for k in range(CHIPS):
        later = {}
        for taken, (value, order) in best.items():
            for chip in range(CHIPS):
                if not taken >> chip & 1:
                    entry = (value + cost[k][chip], order + (chip,))
                    key = taken | 1 << chip
                    later[key] = min(later.get(key, entry), entry)
        best = later
    return best[(1 << CHIPS) - 1][1]


def routes():
    orders, ends, diagonal = [], [], []
    for column in range(2):
        for z in range(SIDE):
            order = order_of_chips(column, z)
            orders.append(order)
            for device in range(SIDE):
                pair = POSITION[2 * order.index(device // 2) + device % 2]
                ends.append(ends_of(column, z, pair))
                diagonal.append(int(pair == DIAGONAL and two_diagonals(z)))
    place = lambda end: end[0] * SIDE + end[1] // 2
    at = {}
    for device, pair in enumerate(ends):
        for which, end in enumerate(pair):
            at.setdefault(place(end), []).append((device, which))
    assert len(at) == len(ends) and all(len(v) == 2 for v in at.values())
    swapped = [None] * len(ends)
    for seed in range(len(ends)):
        device, enter = seed, 0
        while swapped[device] is None:
            swapped[device] = enter
            node = place(ends[device][1 - enter])
            device, enter = [e for e in at[node] if e != (device, 1 - enter)][0]
    first = [place(ends[d][swapped[d]]) for d in range(len(ends))]
    second = [place(ends[d][1 - swapped[d]]) for d in range(len(ends))]
    assert len(set(first)) == len(set(second)) == len(ends)
    half = [0] * len(ends)
    for d in range(len(ends)):
        half[first[d]] = ends[d][swapped[d]][1] % 2
    table = [a + 2 * b + 4 * c for a, b, c in zip(swapped, half, diagonal)]
    return orders, first, second, table


def lookup(step, values):
    out = jnp.int32(values[0])
    for k, value in enumerate(values):
        out = jnp.where(step == k, jnp.int32(value), out)
    return out


def iota(shape, axis):
    return lax.broadcasted_iota(jnp.int32, shape, axis)


def dot_t(a, b):
    return lax.dot_general(a, b, (((1,), (1,)), ((), ())), precision=EXACT, preferred_element_type=jnp.float32)


def product(a, b):
    return lax.dot_general(a, b, (((1,), (1,)), ((), ())), preferred_element_type=jnp.float32)


def halves(x):
    high = x.astype(jnp.bfloat16)
    return high, (x - high.astype(jnp.float32)).astype(jnp.bfloat16)


def stage(x, mass):
    local = jnp.sum(mass)
    mean = jnp.sum(x * mass, axis=1, keepdims=True) / local
    x = x - mean
    wx = x * mass
    square = jnp.sum(wx * x, axis=1, keepdims=True)
    return x, wx, mean, square[:ROWS] + square[ROWS : 2 * ROWS] + square[2 * ROWS :], local


def stage_rows(block, mass, at, core, weighted, feature):
    atoms = block.shape[1]
    _, wx, mean, square, local = stage(block[...], mass)
    high, low = halves(wx)
    for k, part in enumerate((high, high, low)):
        weighted[at * 3 * ROWS : (at + 1) * 3 * ROWS, k * atoms : (k + 1) * atoms] = part
    lane = iota((ROWS, 128), 1) - 8 * core
    out = jnp.where(lane == 51, local, jnp.where(lane == 64 - 8 * core, square, 0.0))
    for c in range(3):
        out = jnp.where(lane == 48 + c, mean[c * ROWS : (c + 1) * ROWS], out)
    feature[at] = out


def stage_columns(block, mass, at, core, centered, feature):
    atoms = block.shape[1]
    x, _, mean, square, _ = stage(block[...], mass)
    high, low = halves(x)
    for k, part in enumerate((high, low, high)):
        centered[at, : 3 * ROWS, k * atoms : (k + 1) * atoms] = part
    lane = iota((ROWS, 128), 1) - 8 * core
    out = jnp.where(lane == 65 - 8 * core, square, 0.0)
    for c in range(3):
        out = jnp.where(lane == 52 + c, mean[c * ROWS : (c + 1) * ROWS], out)
    feature[at] = out


def rest_of(tail):
    tail = jnp.where(iota((3 * ROWS, 128), 1) < 16, tail, 0.0)
    return tail[:ROWS] + pltpu.roll(tail[ROWS : 2 * ROWS], 16, 1) + pltpu.roll(tail[2 * ROWS :], 32, 1)


def packed(rest):
    lane, tail = iota((16, 128), 1), rest[32:]
    low = pltpu.roll(jnp.where(lane < 48, tail, 0.0), 80, 1)
    high = pltpu.roll(jnp.where(lane < 48, 0.0, tail), 32, 1)
    return rest[:32] + jnp.concatenate([low, high], axis=0)


def unpacked(rows):
    tail = jnp.where(iota((16, 128), 1) < 48, pltpu.roll(rows[:16], 48, 1), pltpu.roll(rows[16:], 96, 1))
    return jnp.concatenate([rows, tail], axis=0)


def put_pair(out, pair, core, value, feature):
    k, owner = divmod(POSITION.index(pair), 2)
    at = jnp.where(core == owner, k, CHIPS + k)
    out[at, : 3 * ROWS] = value[:, :128]
    out[at, 3 * ROWS :] = packed(rest_of(value[:, 128:]) + feature)


def put_groups(out, pairs, order, core, weighted, centered, row_feature, column_feature):
    for at, k in enumerate(order):
        group = [pair for pair in pairs if pair[1] == k]
        start = STACK.index(group[0][0])
        assert STACK[start : start + len(group)] == tuple(p for p, _ in group)
        values = product(weighted[start * 3 * ROWS : (start + len(group)) * 3 * ROWS], centered[at])
        for n, pair in enumerate(group):
            value = values[n * 3 * ROWS : (n + 1) * 3 * ROWS]
            put_pair(out, PAIRS.index(pair), core, value, row_feature[start + n] + column_feature[at])


def first_kernel(flags, mass_ref, own, plus2, other2, weighted, row_feature, centered, column_feature):
    core = flags[2]
    mass = mass_ref[...].astype(jnp.float32)
    stage_rows(own, mass, STACK.index(0), core, weighted, row_feature)
    for at, block in enumerate((plus2, other2)):
        stage_columns(block, mass, at, core, centered, column_feature)


def early_kernel(
    flags, mass_ref, other3, plus4, minus3, minus4, first_centered, first_feature, _, __,
    out, weighted, row_feature, centered, column_feature,
):
    core = flags[2]
    mass = mass_ref[...].astype(jnp.float32)
    order = (2, 3, 7)
    for at, block in enumerate((plus4, minus3, other3)):
        stage_columns(block, mass, at, core, centered, column_feature)
    for at, block in ((0, minus3), (2, minus4), (3, plus4)):
        stage_rows(block, mass, at, core, weighted, row_feature)
    put_groups(out, EARLY, (1, 5), core, weighted, first_centered, row_feature, first_feature)
    put_groups(out, EARLY, order, core, weighted, centered, row_feature, column_feature)

    @pl.when(flags[1] == 1)
    def _():
        stage_columns(minus4, mass, 3, core, centered, column_feature)
        p, q, last = STACK.index(4), STACK.index(2), order.index(2)
        upper = product(weighted[p * 3 * ROWS : (p + 1) * 3 * ROWS], centered[3])
        lower = product(weighted[q * 3 * ROWS : (q + 1) * 3 * ROWS], centered[last])
        i, j = iota((3 * ROWS, 256), 0) % ROWS, iota((3 * ROWS, 256), 1) % ROWS
        at = iota((ROWS, 256), 1)
        on = jnp.where((i == j) & (iota((3 * ROWS, 256), 1) < 3 * ROWS), lower, 0.0)
        lane = iota((ROWS, 128), 1)
        ends = row_feature[p] + column_feature[last]
        for c in range(3):
            mine = on[c * ROWS : (c + 1) * ROWS]
            for d in range(3):
                inside = (at >= d * ROWS) & (at < (d + 1) * ROWS)
                value = jnp.sum(jnp.where(inside, mine, 0.0), axis=1, keepdims=True)
                ends = jnp.where(lane == 66 + 3 * c + d, value, ends)
        put_pair(out, DIAGONAL, core, jnp.where(i <= j, upper, lower), ends)


def late_kernel(flags, mass_ref, weighted, row_feature, other4, sums, send, keep, last, centered, column_feature):
    core = flags[2]
    mass = mass_ref[...].astype(jnp.float32)
    stage_columns(other4, mass, 0, core, centered, column_feature)
    values = product(weighted[3 * ROWS :], centered[0])
    other = flags[0] == 1
    for n in range(2):
        rows = values[: 3 * ROWS] if n == 0 else jnp.where(other, values[3 * ROWS : 6 * ROWS], values[6 * ROWS :])
        feature = row_feature[1] if n == 0 else jnp.where(other, row_feature[2], row_feature[3])
        at = jnp.where(core == n, 0, 1)
        last[at, : 3 * ROWS] = rows[:, :128]
        last[at, 3 * ROWS :] = packed(rest_of(rows[:, 128:]) + feature + column_feature[0])
    keep[0] = last[0]
    send[CHIPS - 1] = last[1]
    send[: CHIPS - 1] = sums[CHIPS : 2 * CHIPS - 1]


def merge_kernel(sums, keep, taken, out):
    out[: CHIPS - 1] = sums[: CHIPS - 1] + taken[: CHIPS - 1]
    out[CHIPS - 1] = keep[0] + taken[CHIPS - 1]


def det_four(rows):
    a00, a01, a02, a03 = rows[0]
    a10, a11, a12, a13 = rows[1]
    a20, a21, a22, a23 = rows[2]
    a30, a31, a32, a33 = rows[3]
    s0 = a00 * a11 - a10 * a01
    s1 = a00 * a12 - a10 * a02
    s2 = a00 * a13 - a10 * a03
    s3 = a01 * a12 - a11 * a02
    s4 = a01 * a13 - a11 * a03
    s5 = a02 * a13 - a12 * a03
    t5 = a22 * a33 - a32 * a23
    t4 = a21 * a33 - a31 * a23
    t3 = a21 * a32 - a31 * a22
    t2 = a20 * a33 - a30 * a23
    t1 = a20 * a32 - a30 * a22
    t0 = a20 * a31 - a30 * a21
    return s0 * t5 - s1 * t4 + s2 * t3 + s3 * t2 - s4 * t1 + s5 * t0


def quaternion_fit(moment, spread_rows, spread_cols):
    sxx, sxy, sxz, syx, syy, syz, szx, szy, szz = moment
    coef_two = -2.0 * sum(m * m for m in moment)
    det_three = (
        sxx * (syy * szz - syz * szy)
        - sxy * (syx * szz - syz * szx)
        + sxz * (syx * szy - syy * szx)
    )
    coef_one = -8.0 * det_three
    rows = [
        [sxx + syy + szz, syz - szy, szx - sxz, sxy - syx],
        [syz - szy, sxx - syy - szz, sxy + syx, szx + sxz],
        [szx - sxz, sxy + syx, -sxx + syy - szz, syz + szy],
        [sxy - syx, szx + sxz, syz + szy, -sxx - syy + szz],
    ]
    coef_zero = det_four(rows)
    lam = 0.5 * (spread_rows + spread_cols)
    for turn in range(NEWTON):
        square = lam * lam
        value = (square + coef_two) * square + coef_one * lam + coef_zero
        slope = 4.0 * square * lam + 2.0 * coef_two * lam + coef_one
        lam = lam - value / slope
    return spread_rows + spread_cols - 2.0 * lam


def square_tile(x):
    return jnp.concatenate([x, jnp.zeros((128 - x.shape[0], 128), jnp.float32)], axis=0)


def fit_kernel(flags, parts, first, second):
    diagonal, swap = flags[1] == 1, flags[0] == 1
    total = parts[0]
    for a in range(1, CHIPS):
        total = total + parts[a]
    lane, row = iota((ROWS, 128), 1), iota((ROWS, 128), 0)
    rest = unpacked(total[3 * ROWS :])

    gathered = jnp.zeros((ROWS, 128), jnp.float32)
    for a in range(CHIPS):
        tile = jnp.where((lane >= 48) & (lane < 64), unpacked(parts[a, 3 * ROWS :]), 0.0)
        gathered = gathered + pltpu.roll(tile, (16 * a - 48) % 128, 1)

    sender = lane % 8 == 0

    def per_sender(which):
        return jnp.where(sender, pltpu.roll(gathered, (128 - which) % 128, 1), 0.0)

    mass = per_sender(3)
    whole = jnp.sum(mass, axis=1, keepdims=True)

    def offsets(base):
        out = []
        for c in range(3):
            mean = per_sender(base + c)
            centroid = jnp.sum(mass * mean, axis=1, keepdims=True) / whole
            out.append(jnp.where(sender, mean - centroid, 0.0))
        return out

    off_p, off_q = offsets(0), offsets(4)

    def spread(off, at):
        within = jnp.sum(jnp.where(lane == at, rest, 0.0), axis=1, keepdims=True)
        between = jnp.sum(mass * sum(o * o for o in off), axis=1, keepdims=True)
        return (within + between) / whole

    spread_p, spread_q = spread(off_p, 64), spread(off_q, 65)

    def as_row(column):
        return jnp.sum(jnp.where(row == lane, column, 0.0), axis=0, keepdims=True)

    upper = row <= lane
    corner = lane == ROWS
    row_p, row_q = as_row(spread_p), as_row(spread_q)
    spread_rows = jnp.where(upper, spread_p, jnp.where(diagonal, spread_q, spread_p))
    spread_cols = jnp.where(upper, jnp.where(diagonal, row_p, row_q), row_q)
    spread_rows = jnp.where(corner, spread_q, spread_rows)
    spread_cols = jnp.where(corner, spread_q, spread_cols)

    def parts_of(blocks, first):
        high, low = halves(jnp.concatenate(blocks, axis=0))
        return jnp.concatenate([high, high, low] if first else [high, low, high], axis=1)

    up_rows = parts_of([mass * p for p in off_p], True)
    low_rows = parts_of([mass * jnp.where(diagonal, q, p) for p, q in zip(off_p, off_q)], True)
    moment = []
    between = []
    for d in range(3):
        up = product(up_rows, parts_of([square_tile(jnp.where(diagonal, off_p[d], off_q[d]))], False))
        low = product(low_rows, parts_of([square_tile(off_q[d])], False))
        between.append((up, low))
    for c in range(3):
        main = total[c * ROWS : (c + 1) * ROWS]
        tail = pltpu.roll(rest, (32 - 16 * c) % 128, 1)
        shifted = [main, pltpu.roll(main, 128 - 48, 1), jnp.where(lane < 32, pltpu.roll(main, 128 - 96, 1), tail)]
        for d in range(3):
            up, low = (b[c * ROWS : (c + 1) * ROWS] for b in between[d])
            value = shifted[d] + jnp.where(upper, up, low)
            end = jnp.sum(jnp.where(lane == 66 + 3 * c + d, rest, 0.0), axis=1, keepdims=True)
            end = end + jnp.sum(mass * off_q[c] * off_q[d], axis=1, keepdims=True)
            moment.append(jnp.where(corner, end, value) / whole)
    msd = quaternion_fit(moment, spread_rows, spread_cols)
    corner_value = jnp.sum(jnp.where(corner, msd, 0.0), axis=1, keepdims=True)
    msd = jnp.where(lane < ROWS, msd, 0.0)
    turned = square_tile(msd).T[:ROWS]
    plain_a = jnp.where(diagonal, jnp.where(upper, msd, turned), msd)
    mirrored = jnp.where(row > lane, msd, jnp.where(row == lane, corner_value, turned))
    plain_b = jnp.where(diagonal, mirrored, turned)
    for out, here, there in ((first, plain_a, plain_b), (second, plain_b, plain_a)):
        value = jnp.where(swap, there, here)
        out[...] = value[: ROWS // 2] + pltpu.roll(value[ROWS // 2 :], 64, 1)


def on_device(coords, weights):
    orders, first, second, table = routes()
    frame, atom = lax.axis_index("frame"), lax.axis_index("atom")
    build_flags = jnp.stack([frame // SIDE, two_diagonals(frame % SIDE), atom % 2]).astype(jnp.int32)
    mine = jnp.asarray(np.array(table), jnp.int32)[frame * SIDE + atom]
    fit_flags = jnp.stack([mine & 1, mine >> 2])
    mass = weights[None, :]

    def along(block, distance):
        route = [
            (c * SIDE + (k + distance) % SIDE, c * SIDE + k) for c in range(2) for k in range(SIDE)
        ]
        return lax.ppermute(block, "frame", route)

    def across(block):
        return lax.ppermute(block, "frame", [((f + SIDE) % (2 * SIDE), f) for f in range(2 * SIDE)])

    own = coords.reshape(3 * ROWS, coords.shape[2])
    plus2 = along(own, 2)
    minus3 = along(own, -3)
    plus4 = along(plus2, 2)
    minus4 = along(minus3, -1)
    other2 = across(plus2)
    other3 = across(minus3)
    other4 = across(plus4)

    atoms = own.shape[1]
    smem = pl.BlockSpec(memory_space=pltpu.SMEM)
    vmem = pl.BlockSpec(memory_space=pltpu.VMEM)
    params = pltpu.CompilerParams(vmem_limit_bytes=VMEM_LIMIT)

    def columns_scratch(n):
        return [pltpu.VMEM((n, 256, 3 * atoms), jnp.bfloat16), pltpu.VMEM((n, ROWS, 128), jnp.float32)]

    def cost(pairs):
        return pl.CostEstimate(flops=pairs * 2 * 3 * ROWS * 256 * atoms * 3, bytes_accessed=4_000_000, transcendentals=0)

    def sums_of(n):
        return jax.ShapeDtypeStruct((n, SUM_ROWS, 128), jnp.float32)

    staged = [
        jax.ShapeDtypeStruct((len(STACK) * 3 * ROWS, 3 * atoms), jnp.bfloat16),
        jax.ShapeDtypeStruct((len(STACK), ROWS, 128), jnp.float32),
    ]
    columns = [
        jax.ShapeDtypeStruct((2, 256, 3 * atoms), jnp.bfloat16),
        jax.ShapeDtypeStruct((2, ROWS, 128), jnp.float32),
    ]
    weighted, row_feature, centered, column_feature = pl.pallas_call(
        first_kernel,
        out_shape=staged + columns,
        in_specs=[smem] + [vmem] * 4,
        out_specs=[vmem] * 4,
        compiler_params=params,
        cost_estimate=cost(len(EARLY)),
    )(build_flags, mass, own, plus2, other2)
    sums, weighted, row_feature = pl.pallas_call(
        early_kernel,
        out_shape=[sums_of(2 * CHIPS)] + staged,
        in_specs=[smem] + [vmem] * 9,
        out_specs=[vmem] * 3,
        scratch_shapes=columns_scratch(4),
        input_output_aliases={8: 1, 9: 2},
        compiler_params=params,
        cost_estimate=cost(len(EARLY) + 1),
    )(build_flags, mass, other3, plus4, minus3, minus4, centered, column_feature, weighted, row_feature)
    send, keep = pl.pallas_call(
        late_kernel,
        out_shape=[sums_of(CHIPS), sums_of(1)],
        in_specs=[smem] + [vmem] * 5,
        out_specs=[vmem] * 2,
        scratch_shapes=[pltpu.VMEM((2, SUM_ROWS, 128), jnp.float32)] + columns_scratch(1),
        compiler_params=params,
        cost_estimate=cost(len(LATE) + 1),
    )(build_flags, mass, weighted, row_feature, other4, sums)
    taken = lax.ppermute(send, "atom", [(a, a ^ 1) for a in range(SIDE)])
    merged = pl.pallas_call(
        merge_kernel,
        out_shape=sums_of(CHIPS),
        in_specs=[vmem] * 3,
        out_specs=vmem,
        compiler_params=params,
    )(sums, keep, taken)
    groups = [[f * SIDE + 2 * chip + c for chip in orders[f]] for f in range(2 * SIDE) for c in range(2)]
    parts = lax.all_to_all(merged, ("frame", "atom"), 0, 0, axis_index_groups=groups, tiled=True)

    block = jax.ShapeDtypeStruct((ROWS // 2, 128), jnp.float32)
    one, two = pl.pallas_call(
        fit_kernel,
        out_shape=(block, block),
        in_specs=[smem, vmem],
        out_specs=(vmem, vmem),
        compiler_params=params,
    )(fit_flags, parts)
    one = lax.ppermute(one, ("frame", "atom"), list(enumerate(first)))
    two = lax.ppermute(two, ("frame", "atom"), list(enumerate(second)))
    left = jnp.where(mine >> 1 & 1, two, one)
    right = jnp.where(mine >> 1 & 1, one, two)
    upper = jnp.concatenate([left[:, :ROWS], right[:, :ROWS]], axis=1)
    lower = jnp.concatenate([left[:, 64 : 64 + ROWS], right[:, 64 : 64 + ROWS]], axis=1)
    return jnp.concatenate([upper, lower], axis=0)


def solution(mesh):
    placed = (P(None, "frame", "atom"), P("atom"))
    return jax.shard_map(
        on_device, mesh=mesh, in_specs=placed, out_specs=P("frame", "atom"), check_vma=False
    )
```

```python
import functools

import jax
import jax.numpy as jnp
import numpy as np
from jax import lax
from jax.experimental import pallas as pl
from jax.experimental.pallas import tpu as pltpu
from jax.sharding import PartitionSpec as P

NEWTON = 3
ROWS = 48
SIDE = 16
EXACT = lax.Precision.HIGHEST
VMEM_LIMIT = 40 * 1024 * 1024

OWN = (0, 2, 4, -3, -4)
OTHER = (2, 4, -3)
STACK = (3, 0, 2, 4)
EARLY = (
    (3, 1), (0, 1),
    (3, 2), (0, 2),
    (0, 3),
    (3, 5), (0, 5),
    (0, 7), (2, 7),
)
NEXT = ((4, 1), (4, 2), (4, 3), (4, 5), (4, 7))
LATE = ((0, 6), (2, 6))
PAIRS = EARLY + NEXT + LATE
DIAGONAL = PAIRS.index((4, 2))
POSITION = (8, 6, 10, 2, 5, 12, 7, 3, 13, 11, 9, 0, 4, 1, 14, 15)
CHIPS = SIDE // 2
SUM_ROWS = 3 * ROWS + 32


def frame_block(column, z, index):
    if index < len(OWN):
        return column * SIDE + (z + OWN[index]) % SIDE
    return (1 - column) * SIDE + (z + OTHER[index - len(OWN)]) % SIDE


def two_diagonals(z):
    return (z + SIDE - 2) % SIDE < SIDE // 2


def ends_of(column, z, pair):
    p, q = PAIRS[pair]
    if pair == len(PAIRS) - 1 and column == 1:
        p = 4
    a, b = frame_block(column, z, p), frame_block(column, z, q)
    if pair == DIAGONAL and two_diagonals(z):
        return ((a, a), (b, b))
    return ((a, b), (b, a))


def around(a, b, n):
    return min((a - b) % n, (b - a) % n)


def distance(column, z, chip, end):
    to_column, to_z = divmod(end[0], SIDE)
    to_chip = end[1] // 4
    x, to_x = 2 * (chip % 2) + column, 2 * (to_chip % 2) + to_column
    return around(z, to_z, SIDE) + around(chip // 2, to_chip // 2, 4) + around(x, to_x, 4)


def order_of_chips(column, z):
    cost = [[0] * CHIPS for _ in range(CHIPS)]
    for k in range(CHIPS):
        for chip in range(CHIPS):
            for pair in POSITION[2 * k : 2 * k + 2]:
                far = [distance(column, z, chip, end) for end in ends_of(column, z, pair)]
                cost[k][chip] += 2 ** sum(far) + 2 * 4 ** max(far)
    best = {0: (0, ())}
    for k in range(CHIPS):
        later = {}
        for taken, (value, order) in best.items():
            for chip in range(CHIPS):
                if not taken >> chip & 1:
                    entry = (value + cost[k][chip], order + (chip,))
                    key = taken | 1 << chip
                    later[key] = min(later.get(key, entry), entry)
        best = later
    return best[(1 << CHIPS) - 1][1]


def routes():
    orders, ends, diagonal = [], [], []
    for column in range(2):
        for z in range(SIDE):
            order = order_of_chips(column, z)
            orders.append(order)
            for device in range(SIDE):
                pair = POSITION[2 * order.index(device // 2) + device % 2]
                ends.append(ends_of(column, z, pair))
                diagonal.append(int(pair == DIAGONAL and two_diagonals(z)))
    place = lambda end: end[0] * SIDE + end[1] // 2
    at = {}
    for device, pair in enumerate(ends):
        for which, end in enumerate(pair):
            at.setdefault(place(end), []).append((device, which))
    assert len(at) == len(ends) and all(len(v) == 2 for v in at.values())
    swapped = [None] * len(ends)
    for seed in range(len(ends)):
        device, enter = seed, 0
        while swapped[device] is None:
            swapped[device] = enter
            node = place(ends[device][1 - enter])
            device, enter = [e for e in at[node] if e != (device, 1 - enter)][0]
    first = [place(ends[d][swapped[d]]) for d in range(len(ends))]
    second = [place(ends[d][1 - swapped[d]]) for d in range(len(ends))]
    assert len(set(first)) == len(set(second)) == len(ends)
    half = [0] * len(ends)
    for d in range(len(ends)):
        half[first[d]] = ends[d][swapped[d]][1] % 2
    table = [a + 2 * b + 4 * c for a, b, c in zip(swapped, half, diagonal)]
    return orders, first, second, table


def lookup(step, values):
    out = jnp.int32(values[0])
    for k, value in enumerate(values):
        out = jnp.where(step == k, jnp.int32(value), out)
    return out


def iota(shape, axis):
    return lax.broadcasted_iota(jnp.int32, shape, axis)


def dot_t(a, b):
    return lax.dot_general(a, b, (((1,), (1,)), ((), ())), precision=EXACT, preferred_element_type=jnp.float32)


def product(a, b):
    return lax.dot_general(a, b, (((1,), (1,)), ((), ())), preferred_element_type=jnp.float32)


def halves(x):
    high = x.astype(jnp.bfloat16)
    return high, (x - high.astype(jnp.float32)).astype(jnp.bfloat16)


def stage(x, mass):
    local = jnp.sum(mass)
    mean = jnp.sum(x * mass, axis=1, keepdims=True) / local
    x = x - mean
    wx = x * mass
    square = jnp.sum(wx * x, axis=1, keepdims=True)
    return x, wx, mean, square[:ROWS] + square[ROWS : 2 * ROWS] + square[2 * ROWS :], local


def stage_rows(block, mass, at, core, weighted, feature):
    atoms = block.shape[1]
    _, wx, mean, square, local = stage(block[...], mass)
    high, low = halves(wx)
    for k, part in enumerate((high, high, low)):
        weighted[at * 3 * ROWS : (at + 1) * 3 * ROWS, k * atoms : (k + 1) * atoms] = part
    lane = iota((ROWS, 128), 1) - 8 * core
    out = jnp.where(lane == 51, local, jnp.where(lane == 64 - 8 * core, square, 0.0))
    for c in range(3):
        out = jnp.where(lane == 48 + c, mean[c * ROWS : (c + 1) * ROWS], out)
    feature[at] = out


def stage_columns(block, mass, at, core, centered, feature):
    atoms = block.shape[1]
    x, _, mean, square, _ = stage(block[...], mass)
    high, low = halves(x)
    for k, part in enumerate((high, low, high)):
        centered[at, : 3 * ROWS, k * atoms : (k + 1) * atoms] = part
    lane = iota((ROWS, 128), 1) - 8 * core
    out = jnp.where(lane == 65 - 8 * core, square, 0.0)
    for c in range(3):
        out = jnp.where(lane == 52 + c, mean[c * ROWS : (c + 1) * ROWS], out)
    feature[at] = out


def rest_of(tail):
    tail = jnp.where(iota((3 * ROWS, 128), 1) < 16, tail, 0.0)
    return tail[:ROWS] + pltpu.roll(tail[ROWS : 2 * ROWS], 16, 1) + pltpu.roll(tail[2 * ROWS :], 32, 1)


def packed(rest):
    lane, tail = iota((16, 128), 1), rest[32:]
    low = pltpu.roll(jnp.where(lane < 48, tail, 0.0), 80, 1)
    high = pltpu.roll(jnp.where(lane < 48, 0.0, tail), 32, 1)
    return rest[:32] + jnp.concatenate([low, high], axis=0)


def unpacked(rows):
    tail = jnp.where(iota((16, 128), 1) < 48, pltpu.roll(rows[:16], 48, 1), pltpu.roll(rows[16:], 96, 1))
    return jnp.concatenate([rows, tail], axis=0)


def put_pair(out, pair, core, value, feature):
    k, owner = divmod(POSITION.index(pair), 2)
    at = jnp.where(core == owner, k, CHIPS + k)
    out[at, : 3 * ROWS] = value[:, :128]
    out[at, 3 * ROWS :] = packed(rest_of(value[:, 128:]) + feature)


def put_groups(out, pairs, order, core, weighted, centered, row_feature, column_feature):
    for at, k in enumerate(order):
        group = [pair for pair in pairs if pair[1] == k]
        start = STACK.index(group[0][0])
        assert STACK[start : start + len(group)] == tuple(p for p, _ in group)
        values = product(weighted[start * 3 * ROWS : (start + len(group)) * 3 * ROWS], centered[at])
        for n, pair in enumerate(group):
            value = values[n * 3 * ROWS : (n + 1) * 3 * ROWS]
            put_pair(out, PAIRS.index(pair), core, value, row_feature[start + n] + column_feature[at])


def first_kernel(flags, mass_ref, own, plus2, other2, weighted, row_feature, centered, column_feature):
    core = flags[2]
    mass = mass_ref[...].astype(jnp.float32)
    stage_rows(own, mass, STACK.index(0), core, weighted, row_feature)
    for at, block in enumerate((plus2, other2)):
        stage_columns(block, mass, at, core, centered, column_feature)


def early_kernel(
    flags, mass_ref, other3, plus4, minus3, first_centered, first_feature, _, __,
    out, weighted, row_feature, centered, column_feature,
):
    core = flags[2]
    mass = mass_ref[...].astype(jnp.float32)
    for at, block in enumerate((plus4, minus3, other3)):
        stage_columns(block, mass, at, core, centered, column_feature)
    for k, block in ((3, minus3), (2, plus4)):
        stage_rows(block, mass, STACK.index(k), core, weighted, row_feature)
    put_groups(out, EARLY, (1, 5), core, weighted, first_centered, row_feature, first_feature)
    put_groups(out, EARLY, (2, 3, 7), core, weighted, centered, row_feature, column_feature)


def next_kernel(
    flags, mass_ref, minus4, first_centered, first_feature, centered, column_feature, _, __, ___,
    out, weighted, row_feature, own_centered, own_feature,
):
    core = flags[2]
    mass = mass_ref[...].astype(jnp.float32)
    stage_rows(minus4, mass, STACK.index(4), core, weighted, row_feature)
    put_groups(out, NEXT, (1, 5), core, weighted, first_centered, row_feature, first_feature)
    put_groups(out, NEXT, (2, 3, 7), core, weighted, centered, row_feature, column_feature)

    @pl.when(flags[1] == 1)
    def _():
        stage_columns(minus4, mass, 0, core, own_centered, own_feature)
        p, q, last = STACK.index(4), STACK.index(2), 0
        upper = product(weighted[p * 3 * ROWS : (p + 1) * 3 * ROWS], own_centered[0])
        lower = product(weighted[q * 3 * ROWS : (q + 1) * 3 * ROWS], centered[last])
        i, j = iota((3 * ROWS, 256), 0) % ROWS, iota((3 * ROWS, 256), 1) % ROWS
        at = iota((ROWS, 256), 1)
        on = jnp.where((i == j) & (iota((3 * ROWS, 256), 1) < 3 * ROWS), lower, 0.0)
        lane = iota((ROWS, 128), 1)
        ends = row_feature[p] + column_feature[last]
        for c in range(3):
            mine = on[c * ROWS : (c + 1) * ROWS]
            for d in range(3):
                inside = (at >= d * ROWS) & (at < (d + 1) * ROWS)
                value = jnp.sum(jnp.where(inside, mine, 0.0), axis=1, keepdims=True)
                ends = jnp.where(lane == 66 + 3 * c + d, value, ends)
        put_pair(out, DIAGONAL, core, jnp.where(i <= j, upper, lower), ends)


def late_kernel(flags, mass_ref, weighted, row_feature, other4, sums, send, keep, last, centered, column_feature):
    core = flags[2]
    mass = mass_ref[...].astype(jnp.float32)
    stage_columns(other4, mass, 0, core, centered, column_feature)
    values = product(weighted[3 * ROWS :], centered[0])
    other = flags[0] == 1
    for n in range(2):
        rows = values[: 3 * ROWS] if n == 0 else jnp.where(other, values[6 * ROWS :], values[3 * ROWS : 6 * ROWS])
        feature = row_feature[1] if n == 0 else jnp.where(other, row_feature[3], row_feature[2])
        at = jnp.where(core == n, 0, 1)
        last[at, : 3 * ROWS] = rows[:, :128]
        last[at, 3 * ROWS :] = packed(rest_of(rows[:, 128:]) + feature + column_feature[0])
    keep[0] = last[0]
    send[CHIPS - 1] = last[1]
    send[: CHIPS - 1] = sums[CHIPS : 2 * CHIPS - 1]


def merge_kernel(sums, keep, taken, out):
    out[: CHIPS - 1] = sums[: CHIPS - 1] + taken[: CHIPS - 1]
    out[CHIPS - 1] = keep[0] + taken[CHIPS - 1]


def det_four(rows):
    a00, a01, a02, a03 = rows[0]
    a10, a11, a12, a13 = rows[1]
    a20, a21, a22, a23 = rows[2]
    a30, a31, a32, a33 = rows[3]
    s0 = a00 * a11 - a10 * a01
    s1 = a00 * a12 - a10 * a02
    s2 = a00 * a13 - a10 * a03
    s3 = a01 * a12 - a11 * a02
    s4 = a01 * a13 - a11 * a03
    s5 = a02 * a13 - a12 * a03
    t5 = a22 * a33 - a32 * a23
    t4 = a21 * a33 - a31 * a23
    t3 = a21 * a32 - a31 * a22
    t2 = a20 * a33 - a30 * a23
    t1 = a20 * a32 - a30 * a22
    t0 = a20 * a31 - a30 * a21
    return s0 * t5 - s1 * t4 + s2 * t3 + s3 * t2 - s4 * t1 + s5 * t0


def quaternion_fit(moment, spread_rows, spread_cols):
    sxx, sxy, sxz, syx, syy, syz, szx, szy, szz = moment
    coef_two = -2.0 * sum(m * m for m in moment)
    det_three = (
        sxx * (syy * szz - syz * szy)
        - sxy * (syx * szz - syz * szx)
        + sxz * (syx * szy - syy * szx)
    )
    coef_one = -8.0 * det_three
    rows = [
        [sxx + syy + szz, syz - szy, szx - sxz, sxy - syx],
        [syz - szy, sxx - syy - szz, sxy + syx, szx + sxz],
        [szx - sxz, sxy + syx, -sxx + syy - szz, syz + szy],
        [sxy - syx, szx + sxz, syz + szy, -sxx - syy + szz],
    ]
    coef_zero = det_four(rows)
    lam = 0.5 * (spread_rows + spread_cols)
    for turn in range(NEWTON):
        square = lam * lam
        value = (square + coef_two) * square + coef_one * lam + coef_zero
        slope = 4.0 * square * lam + 2.0 * coef_two * lam + coef_one
        lam = lam - value / slope
    return spread_rows + spread_cols - 2.0 * lam


def square_tile(x):
    return jnp.concatenate([x, jnp.zeros((128 - x.shape[0], 128), jnp.float32)], axis=0)


def fit_kernel(flags, parts, first, second):
    diagonal, swap = flags[1] == 1, flags[0] == 1
    total = parts[0]
    for a in range(1, CHIPS):
        total = total + parts[a]
    lane, row = iota((ROWS, 128), 1), iota((ROWS, 128), 0)
    rest = unpacked(total[3 * ROWS :])

    gathered = jnp.zeros((ROWS, 128), jnp.float32)
    for a in range(CHIPS):
        tile = jnp.where((lane >= 48) & (lane < 64), unpacked(parts[a, 3 * ROWS :]), 0.0)
        gathered = gathered + pltpu.roll(tile, (16 * a - 48) % 128, 1)

    sender = lane % 8 == 0

    def per_sender(which):
        return jnp.where(sender, pltpu.roll(gathered, (128 - which) % 128, 1), 0.0)

    mass = per_sender(3)
    whole = jnp.sum(mass, axis=1, keepdims=True)

    def offsets(base):
        out = []
        for c in range(3):
            mean = per_sender(base + c)
            centroid = jnp.sum(mass * mean, axis=1, keepdims=True) / whole
            out.append(jnp.where(sender, mean - centroid, 0.0))
        return out

    off_p, off_q = offsets(0), offsets(4)

    def spread(off, at):
        within = jnp.sum(jnp.where(lane == at, rest, 0.0), axis=1, keepdims=True)
        between = jnp.sum(mass * sum(o * o for o in off), axis=1, keepdims=True)
        return (within + between) / whole

    spread_p, spread_q = spread(off_p, 64), spread(off_q, 65)

    def as_row(column):
        return jnp.sum(jnp.where(row == lane, column, 0.0), axis=0, keepdims=True)

    upper = row <= lane
    corner = lane == ROWS
    row_p, row_q = as_row(spread_p), as_row(spread_q)
    spread_rows = jnp.where(upper, spread_p, jnp.where(diagonal, spread_q, spread_p))
    spread_cols = jnp.where(upper, jnp.where(diagonal, row_p, row_q), row_q)
    spread_rows = jnp.where(corner, spread_q, spread_rows)
    spread_cols = jnp.where(corner, spread_q, spread_cols)

    def parts_of(blocks, first):
        high, low = halves(jnp.concatenate(blocks, axis=0))
        return jnp.concatenate([high, high, low] if first else [high, low, high], axis=1)

    up_rows = parts_of([mass * p for p in off_p], True)
    low_rows = parts_of([mass * jnp.where(diagonal, q, p) for p, q in zip(off_p, off_q)], True)
    moment = []
    between = []
    for d in range(3):
        up = product(up_rows, parts_of([square_tile(jnp.where(diagonal, off_p[d], off_q[d]))], False))
        low = product(low_rows, parts_of([square_tile(off_q[d])], False))
        between.append((up, low))
    for c in range(3):
        main = total[c * ROWS : (c + 1) * ROWS]
        tail = pltpu.roll(rest, (32 - 16 * c) % 128, 1)
        shifted = [main, pltpu.roll(main, 128 - 48, 1), jnp.where(lane < 32, pltpu.roll(main, 128 - 96, 1), tail)]
        for d in range(3):
            up, low = (b[c * ROWS : (c + 1) * ROWS] for b in between[d])
            value = shifted[d] + jnp.where(upper, up, low)
            end = jnp.sum(jnp.where(lane == 66 + 3 * c + d, rest, 0.0), axis=1, keepdims=True)
            end = end + jnp.sum(mass * off_q[c] * off_q[d], axis=1, keepdims=True)
            moment.append(jnp.where(corner, end, value) / whole)
    msd = quaternion_fit(moment, spread_rows, spread_cols)
    corner_value = jnp.sum(jnp.where(corner, msd, 0.0), axis=1, keepdims=True)
    msd = jnp.where(lane < ROWS, msd, 0.0)
    turned = square_tile(msd).T[:ROWS]
    plain_a = jnp.where(diagonal, jnp.where(upper, msd, turned), msd)
    mirrored = jnp.where(row > lane, msd, jnp.where(row == lane, corner_value, turned))
    plain_b = jnp.where(diagonal, mirrored, turned)
    for out, here, there in ((first, plain_a, plain_b), (second, plain_b, plain_a)):
        value = jnp.where(swap, there, here)
        out[...] = value[: ROWS // 2] + pltpu.roll(value[ROWS // 2 :], 64, 1)


def on_device(coords, weights):
    orders, first, second, table = routes()
    frame, atom = lax.axis_index("frame"), lax.axis_index("atom")
    build_flags = jnp.stack([frame // SIDE, two_diagonals(frame % SIDE), atom % 2]).astype(jnp.int32)
    mine = jnp.asarray(np.array(table), jnp.int32)[frame * SIDE + atom]
    fit_flags = jnp.stack([mine & 1, mine >> 2])
    mass = weights[None, :]

    def along(block, distance):
        route = [
            (c * SIDE + (k + distance) % SIDE, c * SIDE + k) for c in range(2) for k in range(SIDE)
        ]
        return lax.ppermute(block, "frame", route)

    def across(block):
        return lax.ppermute(block, "frame", [((f + SIDE) % (2 * SIDE), f) for f in range(2 * SIDE)])

    own = coords.reshape(3 * ROWS, coords.shape[2])
    plus2 = along(own, 2)
    minus3 = along(own, -3)
    plus4 = along(plus2, 2)
    minus4 = along(minus3, -1)
    other2 = across(plus2)
    other3 = across(minus3)
    other4 = across(plus4)

    atoms = own.shape[1]
    smem = pl.BlockSpec(memory_space=pltpu.SMEM)
    vmem = pl.BlockSpec(memory_space=pltpu.VMEM)
    params = pltpu.CompilerParams(vmem_limit_bytes=VMEM_LIMIT)

    def columns_scratch(n):
        return [pltpu.VMEM((n, 256, 3 * atoms), jnp.bfloat16), pltpu.VMEM((n, ROWS, 128), jnp.float32)]

    def cost(pairs):
        return pl.CostEstimate(flops=pairs * 2 * 3 * ROWS * 256 * atoms * 3, bytes_accessed=4_000_000, transcendentals=0)

    def sums_of(n):
        return jax.ShapeDtypeStruct((n, SUM_ROWS, 128), jnp.float32)

    staged = [
        jax.ShapeDtypeStruct((len(STACK) * 3 * ROWS, 3 * atoms), jnp.bfloat16),
        jax.ShapeDtypeStruct((len(STACK), ROWS, 128), jnp.float32),
    ]
    columns = [
        jax.ShapeDtypeStruct((2, 256, 3 * atoms), jnp.bfloat16),
        jax.ShapeDtypeStruct((2, ROWS, 128), jnp.float32),
    ]
    weighted, row_feature, centered, column_feature = pl.pallas_call(
        first_kernel,
        out_shape=staged + columns,
        in_specs=[smem] + [vmem] * 4,
        out_specs=[vmem] * 4,
        compiler_params=params,
        cost_estimate=cost(len(EARLY)),
    )(build_flags, mass, own, plus2, other2)
    more = [
        jax.ShapeDtypeStruct((3, 256, 3 * atoms), jnp.bfloat16),
        jax.ShapeDtypeStruct((3, ROWS, 128), jnp.float32),
    ]
    sums, weighted, row_feature, more_centered, more_feature = pl.pallas_call(
        early_kernel,
        out_shape=[sums_of(2 * CHIPS)] + staged + more,
        in_specs=[smem] + [vmem] * 8,
        out_specs=[vmem] * 5,
        input_output_aliases={7: 1, 8: 2},
        compiler_params=params,
        cost_estimate=cost(len(EARLY)),
    )(build_flags, mass, other3, plus4, minus3, centered, column_feature, weighted, row_feature)
    sums, weighted, row_feature = pl.pallas_call(
        next_kernel,
        out_shape=[sums_of(2 * CHIPS)] + staged,
        in_specs=[smem] + [vmem] * 9,
        out_specs=[vmem] * 3,
        scratch_shapes=columns_scratch(1),
        input_output_aliases={7: 0, 8: 1, 9: 2},
        compiler_params=params,
        cost_estimate=cost(len(NEXT) + 1),
    )(
        build_flags, mass, minus4, centered, column_feature, more_centered, more_feature, sums, weighted, row_feature
    )
    send, keep = pl.pallas_call(
        late_kernel,
        out_shape=[sums_of(CHIPS), sums_of(1)],
        in_specs=[smem] + [vmem] * 5,
        out_specs=[vmem] * 2,
        scratch_shapes=[pltpu.VMEM((2, SUM_ROWS, 128), jnp.float32)] + columns_scratch(1),
        compiler_params=params,
        cost_estimate=cost(len(LATE) + 1),
    )(build_flags, mass, weighted, row_feature, other4, sums)
    taken = lax.ppermute(send, "atom", [(a, a ^ 1) for a in range(SIDE)])
    merged = pl.pallas_call(
        merge_kernel,
        out_shape=sums_of(CHIPS),
        in_specs=[vmem] * 3,
        out_specs=vmem,
        compiler_params=params,
    )(sums, keep, taken)
    groups = [[f * SIDE + 2 * chip + c for chip in orders[f]] for f in range(2 * SIDE) for c in range(2)]
    parts = lax.all_to_all(merged, ("frame", "atom"), 0, 0, axis_index_groups=groups, tiled=True)

    block = jax.ShapeDtypeStruct((ROWS // 2, 128), jnp.float32)
    one, two = pl.pallas_call(
        fit_kernel,
        out_shape=(block, block),
        in_specs=[smem, vmem],
        out_specs=(vmem, vmem),
        compiler_params=params,
    )(fit_flags, parts)
    one = lax.ppermute(one, ("frame", "atom"), list(enumerate(first)))
    two = lax.ppermute(two, ("frame", "atom"), list(enumerate(second)))
    left = jnp.where(mine >> 1 & 1, two, one)
    right = jnp.where(mine >> 1 & 1, one, two)
    upper = jnp.concatenate([left[:, :ROWS], right[:, :ROWS]], axis=1)
    lower = jnp.concatenate([left[:, 64 : 64 + ROWS], right[:, 64 : 64 + ROWS]], axis=1)
    return jnp.concatenate([upper, lower], axis=0)


def solution(mesh):
    placed = (P(None, "frame", "atom"), P("atom"))
    return jax.shard_map(
        on_device, mesh=mesh, in_specs=placed, out_specs=P("frame", "atom"), check_vma=False
    )
```

```python
import functools

import jax
import jax.numpy as jnp
import numpy as np
from jax import lax
from jax.experimental import pallas as pl
from jax.experimental.pallas import tpu as pltpu
from jax.sharding import PartitionSpec as P

NEWTON = 3
ROWS = 48
SIDE = 16
EXACT = lax.Precision.HIGHEST
VMEM_LIMIT = 40 * 1024 * 1024

OWN = (0, 2, 4, -3, -4)
OTHER = (2, 4, -3)
STACK = (3, 0, 2, 4)
EARLY = (
    (3, 1), (0, 1),
    (3, 2), (0, 2),
    (0, 3),
    (3, 5), (0, 5),
    (0, 7), (2, 7),
)
NEXT = ((4, 1), (4, 2), (4, 3), (4, 5), (4, 7))
LATE = ((0, 6), (2, 6))
PAIRS = EARLY + NEXT + LATE
DIAGONAL = PAIRS.index((4, 2))
POSITION = (8, 6, 10, 2, 5, 12, 7, 3, 13, 11, 9, 0, 4, 1, 14, 15)
CHIPS = SIDE // 2
SUM_ROWS = 3 * ROWS + 32


def frame_block(column, z, index):
    if index < len(OWN):
        return column * SIDE + (z + OWN[index]) % SIDE
    return (1 - column) * SIDE + (z + OTHER[index - len(OWN)]) % SIDE


def two_diagonals(z):
    return (z + SIDE - 2) % SIDE < SIDE // 2


def ends_of(column, z, pair):
    p, q = PAIRS[pair]
    if pair == len(PAIRS) - 1 and column == 1:
        p = 4
    a, b = frame_block(column, z, p), frame_block(column, z, q)
    if pair == DIAGONAL and two_diagonals(z):
        return ((a, a), (b, b))
    return ((a, b), (b, a))


def around(a, b, n):
    return min((a - b) % n, (b - a) % n)


def distance(column, z, chip, end):
    to_column, to_z = divmod(end[0], SIDE)
    to_chip = end[1] // 4
    x, to_x = 2 * (chip % 2) + column, 2 * (to_chip % 2) + to_column
    return around(z, to_z, SIDE) + around(chip // 2, to_chip // 2, 4) + around(x, to_x, 4)


def order_of_chips(column, z):
    cost = [[0] * CHIPS for _ in range(CHIPS)]
    for k in range(CHIPS):
        for chip in range(CHIPS):
            for pair in POSITION[2 * k : 2 * k + 2]:
                far = [distance(column, z, chip, end) for end in ends_of(column, z, pair)]
                cost[k][chip] += 2 ** sum(far) + 2 * 4 ** max(far)
    best = {0: (0, ())}
    for k in range(CHIPS):
        later = {}
        for taken, (value, order) in best.items():
            for chip in range(CHIPS):
                if not taken >> chip & 1:
                    entry = (value + cost[k][chip], order + (chip,))
                    key = taken | 1 << chip
                    later[key] = min(later.get(key, entry), entry)
        best = later
    return best[(1 << CHIPS) - 1][1]


def routes():
    orders, ends, diagonal = [], [], []
    for column in range(2):
        for z in range(SIDE):
            order = order_of_chips(column, z)
            orders.append(order)
            for device in range(SIDE):
                pair = POSITION[2 * order.index(device // 2) + device % 2]
                ends.append(ends_of(column, z, pair))
                diagonal.append(int(pair == DIAGONAL and two_diagonals(z)))
    place = lambda end: end[0] * SIDE + end[1] // 2
    at = {}
    for device, pair in enumerate(ends):
        for which, end in enumerate(pair):
            at.setdefault(place(end), []).append((device, which))
    assert len(at) == len(ends) and all(len(v) == 2 for v in at.values())
    swapped = [None] * len(ends)
    for seed in range(len(ends)):
        device, enter = seed, 0
        while swapped[device] is None:
            swapped[device] = enter
            node = place(ends[device][1 - enter])
            device, enter = [e for e in at[node] if e != (device, 1 - enter)][0]
    first = [place(ends[d][swapped[d]]) for d in range(len(ends))]
    second = [place(ends[d][1 - swapped[d]]) for d in range(len(ends))]
    assert len(set(first)) == len(set(second)) == len(ends)
    half = [0] * len(ends)
    for d in range(len(ends)):
        half[first[d]] = ends[d][swapped[d]][1] % 2
    table = [a + 2 * b + 4 * c for a, b, c in zip(swapped, half, diagonal)]
    return orders, first, second, table


def lookup(step, values):
    out = jnp.int32(values[0])
    for k, value in enumerate(values):
        out = jnp.where(step == k, jnp.int32(value), out)
    return out


def iota(shape, axis):
    return lax.broadcasted_iota(jnp.int32, shape, axis)


def dot_t(a, b):
    return lax.dot_general(a, b, (((1,), (1,)), ((), ())), precision=EXACT, preferred_element_type=jnp.float32)


def product(a, b):
    return lax.dot_general(a, b, (((1,), (1,)), ((), ())), preferred_element_type=jnp.float32)


def halves(x):
    high = x.astype(jnp.bfloat16)
    return high, (x - high.astype(jnp.float32)).astype(jnp.bfloat16)


def stage(x, mass):
    local = jnp.sum(mass)
    mean = jnp.sum(x * mass, axis=1, keepdims=True) / local
    x = x - mean
    wx = x * mass
    square = jnp.sum(wx * x, axis=1, keepdims=True)
    return x, wx, mean, square[:ROWS] + square[ROWS : 2 * ROWS] + square[2 * ROWS :], local


def stage_rows(block, mass, at, core, weighted, feature):
    atoms = block.shape[1]
    _, wx, mean, square, local = stage(block[...], mass)
    high, low = halves(wx)
    for k, part in enumerate((high, high, low)):
        weighted[at * 3 * ROWS : (at + 1) * 3 * ROWS, k * atoms : (k + 1) * atoms] = part
    lane = iota((ROWS, 128), 1) - 8 * core
    out = jnp.where(lane == 51, local, jnp.where(lane == 64 - 8 * core, square, 0.0))
    for c in range(3):
        out = jnp.where(lane == 48 + c, mean[c * ROWS : (c + 1) * ROWS], out)
    feature[at] = out


def stage_columns(block, mass, at, core, centered, feature):
    atoms = block.shape[1]
    x, _, mean, square, _ = stage(block[...], mass)
    high, low = halves(x)
    for k, part in enumerate((high, low, high)):
        centered[at, : 3 * ROWS, k * atoms : (k + 1) * atoms] = part
    lane = iota((ROWS, 128), 1) - 8 * core
    out = jnp.where(lane == 65 - 8 * core, square, 0.0)
    for c in range(3):
        out = jnp.where(lane == 52 + c, mean[c * ROWS : (c + 1) * ROWS], out)
    feature[at] = out


def rest_of(tail):
    tail = jnp.where(iota((3 * ROWS, 128), 1) < 16, tail, 0.0)
    return tail[:ROWS] + pltpu.roll(tail[ROWS : 2 * ROWS], 16, 1) + pltpu.roll(tail[2 * ROWS :], 32, 1)


def packed(rest):
    lane, tail = iota((16, 128), 1), rest[32:]
    low = pltpu.roll(jnp.where(lane < 48, tail, 0.0), 80, 1)
    high = pltpu.roll(jnp.where(lane < 48, 0.0, tail), 32, 1)
    return rest[:32] + jnp.concatenate([low, high], axis=0)


def unpacked(rows):
    tail = jnp.where(iota((16, 128), 1) < 48, pltpu.roll(rows[:16], 48, 1), pltpu.roll(rows[16:], 96, 1))
    return jnp.concatenate([rows, tail], axis=0)


def put_pair(out, pair, core, value, feature):
    k, owner = divmod(POSITION.index(pair), 2)
    at = jnp.where(core == owner, k, CHIPS + k)
    out[at, : 3 * ROWS] = value[:, :128]
    out[at, 3 * ROWS :] = packed(rest_of(value[:, 128:]) + feature)


def put_groups(out, pairs, order, core, weighted, centered, row_feature, column_feature):
    for at, k in enumerate(order):
        group = [pair for pair in pairs if pair[1] == k]
        start = STACK.index(group[0][0])
        assert STACK[start : start + len(group)] == tuple(p for p, _ in group)
        values = product(weighted[start * 3 * ROWS : (start + len(group)) * 3 * ROWS], centered[at])
        for n, pair in enumerate(group):
            value = values[n * 3 * ROWS : (n + 1) * 3 * ROWS]
            put_pair(out, PAIRS.index(pair), core, value, row_feature[start + n] + column_feature[at])


def first_kernel(flags, mass_ref, own, plus2, other2, weighted, row_feature, centered, column_feature):
    core = flags[2]
    mass = mass_ref[...].astype(jnp.float32)
    stage_rows(own, mass, STACK.index(0), core, weighted, row_feature)
    for at, block in enumerate((plus2, other2)):
        stage_columns(block, mass, at, core, centered, column_feature)


def early_kernel(
    flags, mass_ref, other3, plus4, minus3, first_centered, first_feature, _, __,
    out, weighted, row_feature, centered, column_feature,
):
    core = flags[2]
    mass = mass_ref[...].astype(jnp.float32)
    for at, block in enumerate((plus4, minus3, other3)):
        stage_columns(block, mass, at, core, centered, column_feature)
    for k, block in ((3, minus3), (2, plus4)):
        stage_rows(block, mass, STACK.index(k), core, weighted, row_feature)
    put_groups(out, EARLY, (1, 5), core, weighted, first_centered, row_feature, first_feature)
    put_groups(out, EARLY, (2, 3, 7), core, weighted, centered, row_feature, column_feature)


def next_kernel(
    flags, mass_ref, minus4, first_centered, first_feature, centered, column_feature, _, __, ___,
    out, weighted, row_feature, own_centered, own_feature,
):
    core = flags[2]
    mass = mass_ref[...].astype(jnp.float32)
    stage_rows(minus4, mass, STACK.index(4), core, weighted, row_feature)
    put_groups(out, NEXT, (1, 5), core, weighted, first_centered, row_feature, first_feature)
    put_groups(out, NEXT, (2, 3, 7), core, weighted, centered, row_feature, column_feature)

    @pl.when(flags[1] == 1)
    def _():
        stage_columns(minus4, mass, 0, core, own_centered, own_feature)
        p, q, last = STACK.index(4), STACK.index(2), 0
        upper = product(weighted[p * 3 * ROWS : (p + 1) * 3 * ROWS], own_centered[0])
        lower = product(weighted[q * 3 * ROWS : (q + 1) * 3 * ROWS], centered[last])
        i, j = iota((3 * ROWS, 256), 0) % ROWS, iota((3 * ROWS, 256), 1) % ROWS
        at = iota((ROWS, 256), 1)
        on = jnp.where((i == j) & (iota((3 * ROWS, 256), 1) < 3 * ROWS), lower, 0.0)
        lane = iota((ROWS, 128), 1)
        ends = row_feature[p] + column_feature[last]
        for c in range(3):
            mine = on[c * ROWS : (c + 1) * ROWS]
            for d in range(3):
                inside = (at >= d * ROWS) & (at < (d + 1) * ROWS)
                value = jnp.sum(jnp.where(inside, mine, 0.0), axis=1, keepdims=True)
                ends = jnp.where(lane == 66 + 3 * c + d, value, ends)
        put_pair(out, DIAGONAL, core, jnp.where(i <= j, upper, lower), ends)


def late_kernel(flags, mass_ref, weighted, row_feature, other4, sums, send, keep, last, centered, column_feature):
    core = flags[2]
    mass = mass_ref[...].astype(jnp.float32)
    stage_columns(other4, mass, 0, core, centered, column_feature)
    values = product(weighted[3 * ROWS :], centered[0])
    other = flags[0] == 1
    for n in range(2):
        rows = values[: 3 * ROWS] if n == 0 else jnp.where(other, values[6 * ROWS :], values[3 * ROWS : 6 * ROWS])
        feature = row_feature[1] if n == 0 else jnp.where(other, row_feature[3], row_feature[2])
        at = jnp.where(core == n, 0, 1)
        last[at, : 3 * ROWS] = rows[:, :128]
        last[at, 3 * ROWS :] = packed(rest_of(rows[:, 128:]) + feature + column_feature[0])
    keep[0] = last[0]
    send[CHIPS - 1] = last[1]
    send[: CHIPS - 1] = sums[CHIPS : 2 * CHIPS - 1]


def merge_kernel(sums, keep, taken, out):
    out[: CHIPS - 1] = sums[: CHIPS - 1] + taken[: CHIPS - 1]
    out[CHIPS - 1] = keep[0] + taken[CHIPS - 1]


def det_four(rows):
    a00, a01, a02, a03 = rows[0]
    a10, a11, a12, a13 = rows[1]
    a20, a21, a22, a23 = rows[2]
    a30, a31, a32, a33 = rows[3]
    s0 = a00 * a11 - a10 * a01
    s1 = a00 * a12 - a10 * a02
    s2 = a00 * a13 - a10 * a03
    s3 = a01 * a12 - a11 * a02
    s4 = a01 * a13 - a11 * a03
    s5 = a02 * a13 - a12 * a03
    t5 = a22 * a33 - a32 * a23
    t4 = a21 * a33 - a31 * a23
    t3 = a21 * a32 - a31 * a22
    t2 = a20 * a33 - a30 * a23
    t1 = a20 * a32 - a30 * a22
    t0 = a20 * a31 - a30 * a21
    return s0 * t5 - s1 * t4 + s2 * t3 + s3 * t2 - s4 * t1 + s5 * t0


def quaternion_fit(moment, spread_rows, spread_cols):
    sxx, sxy, sxz, syx, syy, syz, szx, szy, szz = moment
    coef_two = -2.0 * sum(m * m for m in moment)
    det_three = (
        sxx * (syy * szz - syz * szy)
        - sxy * (syx * szz - syz * szx)
        + sxz * (syx * szy - syy * szx)
    )
    coef_one = -8.0 * det_three
    rows = [
        [sxx + syy + szz, syz - szy, szx - sxz, sxy - syx],
        [syz - szy, sxx - syy - szz, sxy + syx, szx + sxz],
        [szx - sxz, sxy + syx, -sxx + syy - szz, syz + szy],
        [sxy - syx, szx + sxz, syz + szy, -sxx - syy + szz],
    ]
    coef_zero = det_four(rows)
    lam = 0.5 * (spread_rows + spread_cols)
    for turn in range(NEWTON):
        square = lam * lam
        value = (square + coef_two) * square + coef_one * lam + coef_zero
        slope = 4.0 * square * lam + 2.0 * coef_two * lam + coef_one
        lam = lam - value / slope
    return spread_rows + spread_cols - 2.0 * lam


def square_tile(x):
    return jnp.concatenate([x, jnp.zeros((128 - x.shape[0], 128), jnp.float32)], axis=0)


def fit_kernel(flags, parts, first, second, lower):
    diagonal, swap = flags[1] == 1, flags[0] == 1
    total = parts[0]
    for a in range(1, CHIPS):
        total = total + parts[a]
    lane, row = iota((ROWS, 128), 1), iota((ROWS, 128), 0)
    rest = unpacked(total[3 * ROWS :])

    gathered = jnp.zeros((ROWS, 128), jnp.float32)
    for a in range(CHIPS):
        tile = jnp.where((lane >= 48) & (lane < 64), unpacked(parts[a, 3 * ROWS :]), 0.0)
        gathered = gathered + pltpu.roll(tile, (16 * a - 48) % 128, 1)

    sender = lane % 8 == 0

    def per_sender(which):
        return jnp.where(sender, pltpu.roll(gathered, (128 - which) % 128, 1), 0.0)

    mass = per_sender(3)
    whole = jnp.sum(mass, axis=1, keepdims=True)

    def offsets(base):
        out = []
        for c in range(3):
            mean = per_sender(base + c)
            centroid = jnp.sum(mass * mean, axis=1, keepdims=True) / whole
            out.append(jnp.where(sender, mean - centroid, 0.0))
        return out

    off_p, off_q = offsets(0), offsets(4)

    def spread(off, at):
        within = jnp.sum(jnp.where(lane == at, rest, 0.0), axis=1, keepdims=True)
        between = jnp.sum(mass * sum(o * o for o in off), axis=1, keepdims=True)
        return (within + between) / whole

    spread_p, spread_q = spread(off_p, 64), spread(off_q, 65)

    def as_row(column):
        return jnp.sum(jnp.where(row == lane, column, 0.0), axis=0, keepdims=True)

    upper = row <= lane
    corner = lane == ROWS
    row_p, row_q = as_row(spread_p), as_row(spread_q)
    spread_rows = jnp.where(upper, spread_p, jnp.where(diagonal, spread_q, spread_p))
    spread_cols = jnp.where(upper, jnp.where(diagonal, row_p, row_q), row_q)
    spread_rows = jnp.where(corner, spread_q, spread_rows)
    spread_cols = jnp.where(corner, spread_q, spread_cols)

    def parts_of(blocks, first):
        high, low = halves(jnp.concatenate(blocks, axis=0))
        return jnp.concatenate([high, high, low] if first else [high, low, high], axis=1)

    up_rows = parts_of([mass * p for p in off_p], True)
    moment = []
    between = []
    for d in range(3):
        up = product(up_rows, parts_of([square_tile(jnp.where(diagonal, off_p[d], off_q[d]))], False))
        lower[d] = up
        between.append(up)

    @pl.when(diagonal)
    def _():
        low_rows = parts_of([mass * q for q in off_q], True)
        for d in range(3):
            lower[d] = product(low_rows, parts_of([square_tile(off_q[d])], False))

    for c in range(3):
        main = total[c * ROWS : (c + 1) * ROWS]
        tail = pltpu.roll(rest, (32 - 16 * c) % 128, 1)
        shifted = [main, pltpu.roll(main, 128 - 48, 1), jnp.where(lane < 32, pltpu.roll(main, 128 - 96, 1), tail)]
        for d in range(3):
            up, low = between[d][c * ROWS : (c + 1) * ROWS], lower[d, c * ROWS : (c + 1) * ROWS]
            value = shifted[d] + jnp.where(upper, up, low)
            end = jnp.sum(jnp.where(lane == 66 + 3 * c + d, rest, 0.0), axis=1, keepdims=True)
            end = end + jnp.sum(mass * off_q[c] * off_q[d], axis=1, keepdims=True)
            moment.append(jnp.where(corner, end, value) / whole)
    msd = quaternion_fit(moment, spread_rows, spread_cols)
    corner_value = jnp.sum(jnp.where(corner, msd, 0.0), axis=1, keepdims=True)
    msd = jnp.where(lane < ROWS, msd, 0.0)
    turned = square_tile(msd).T[:ROWS]
    plain_a = jnp.where(diagonal, jnp.where(upper, msd, turned), msd)
    mirrored = jnp.where(row > lane, msd, jnp.where(row == lane, corner_value, turned))
    plain_b = jnp.where(diagonal, mirrored, turned)
    for out, here, there in ((first, plain_a, plain_b), (second, plain_b, plain_a)):
        value = jnp.where(swap, there, here)
        out[...] = value[: ROWS // 2] + pltpu.roll(value[ROWS // 2 :], 64, 1)


def on_device(coords, weights):
    orders, first, second, table = routes()
    frame, atom = lax.axis_index("frame"), lax.axis_index("atom")
    build_flags = jnp.stack([frame // SIDE, two_diagonals(frame % SIDE), atom % 2]).astype(jnp.int32)
    mine = jnp.asarray(np.array(table), jnp.int32)[frame * SIDE + atom]
    fit_flags = jnp.stack([mine & 1, mine >> 2])
    mass = weights[None, :]

    def along(block, distance):
        route = [
            (c * SIDE + (k + distance) % SIDE, c * SIDE + k) for c in range(2) for k in range(SIDE)
        ]
        return lax.ppermute(block, "frame", route)

    def across(block):
        return lax.ppermute(block, "frame", [((f + SIDE) % (2 * SIDE), f) for f in range(2 * SIDE)])

    own = coords.reshape(3 * ROWS, coords.shape[2])
    plus2 = along(own, 2)
    minus3 = along(own, -3)
    plus4 = along(plus2, 2)
    minus4 = along(minus3, -1)
    other2 = across(plus2)
    other3 = across(minus3)
    other4 = across(plus4)

    atoms = own.shape[1]
    smem = pl.BlockSpec(memory_space=pltpu.SMEM)
    vmem = pl.BlockSpec(memory_space=pltpu.VMEM)
    params = pltpu.CompilerParams(vmem_limit_bytes=VMEM_LIMIT)

    def columns_scratch(n):
        return [pltpu.VMEM((n, 256, 3 * atoms), jnp.bfloat16), pltpu.VMEM((n, ROWS, 128), jnp.float32)]

    def cost(pairs):
        return pl.CostEstimate(flops=pairs * 2 * 3 * ROWS * 256 * atoms * 3, bytes_accessed=4_000_000, transcendentals=0)

    def sums_of(n):
        return jax.ShapeDtypeStruct((n, SUM_ROWS, 128), jnp.float32)

    staged = [
        jax.ShapeDtypeStruct((len(STACK) * 3 * ROWS, 3 * atoms), jnp.bfloat16),
        jax.ShapeDtypeStruct((len(STACK), ROWS, 128), jnp.float32),
    ]
    columns = [
        jax.ShapeDtypeStruct((2, 256, 3 * atoms), jnp.bfloat16),
        jax.ShapeDtypeStruct((2, ROWS, 128), jnp.float32),
    ]
    weighted, row_feature, centered, column_feature = pl.pallas_call(
        first_kernel,
        out_shape=staged + columns,
        in_specs=[smem] + [vmem] * 4,
        out_specs=[vmem] * 4,
        compiler_params=params,
        cost_estimate=cost(len(EARLY)),
    )(build_flags, mass, own, plus2, other2)
    more = [
        jax.ShapeDtypeStruct((3, 256, 3 * atoms), jnp.bfloat16),
        jax.ShapeDtypeStruct((3, ROWS, 128), jnp.float32),
    ]
    sums, weighted, row_feature, more_centered, more_feature = pl.pallas_call(
        early_kernel,
        out_shape=[sums_of(2 * CHIPS)] + staged + more,
        in_specs=[smem] + [vmem] * 8,
        out_specs=[vmem] * 5,
        input_output_aliases={7: 1, 8: 2},
        compiler_params=params,
        cost_estimate=cost(len(EARLY)),
    )(build_flags, mass, other3, plus4, minus3, centered, column_feature, weighted, row_feature)
    sums, weighted, row_feature = pl.pallas_call(
        next_kernel,
        out_shape=[sums_of(2 * CHIPS)] + staged,
        in_specs=[smem] + [vmem] * 9,
        out_specs=[vmem] * 3,
        scratch_shapes=columns_scratch(1),
        input_output_aliases={7: 0, 8: 1, 9: 2},
        compiler_params=params,
        cost_estimate=cost(len(NEXT) + 1),
    )(
        build_flags, mass, minus4, centered, column_feature, more_centered, more_feature, sums, weighted, row_feature
    )
    send, keep = pl.pallas_call(
        late_kernel,
        out_shape=[sums_of(CHIPS), sums_of(1)],
        in_specs=[smem] + [vmem] * 5,
        out_specs=[vmem] * 2,
        scratch_shapes=[pltpu.VMEM((2, SUM_ROWS, 128), jnp.float32)] + columns_scratch(1),
        compiler_params=params,
        cost_estimate=cost(len(LATE) + 1),
    )(build_flags, mass, weighted, row_feature, other4, sums)
    taken = lax.ppermute(send, "atom", [(a, a ^ 1) for a in range(SIDE)])
    merged = pl.pallas_call(
        merge_kernel,
        out_shape=sums_of(CHIPS),
        in_specs=[vmem] * 3,
        out_specs=vmem,
        compiler_params=params,
    )(sums, keep, taken)
    groups = [[f * SIDE + 2 * chip + c for chip in orders[f]] for f in range(2 * SIDE) for c in range(2)]
    parts = lax.all_to_all(merged, ("frame", "atom"), 0, 0, axis_index_groups=groups, tiled=True)

    block = jax.ShapeDtypeStruct((ROWS // 2, 128), jnp.float32)
    one, two = pl.pallas_call(
        fit_kernel,
        out_shape=(block, block),
        in_specs=[smem, vmem],
        out_specs=(vmem, vmem),
        scratch_shapes=[pltpu.VMEM((3, 3 * ROWS, 128), jnp.float32)],
        compiler_params=params,
    )(fit_flags, parts)
    one = lax.ppermute(one, ("frame", "atom"), list(enumerate(first)))
    two = lax.ppermute(two, ("frame", "atom"), list(enumerate(second)))
    left = jnp.where(mine >> 1 & 1, two, one)
    right = jnp.where(mine >> 1 & 1, one, two)
    upper = jnp.concatenate([left[:, :ROWS], right[:, :ROWS]], axis=1)
    lower = jnp.concatenate([left[:, 64 : 64 + ROWS], right[:, 64 : 64 + ROWS]], axis=1)
    return jnp.concatenate([upper, lower], axis=0)


def solution(mesh):
    placed = (P(None, "frame", "atom"), P("atom"))
    return jax.shard_map(
        on_device, mesh=mesh, in_specs=placed, out_specs=P("frame", "atom"), check_vma=False
    )
```

```python
import functools

import jax
import jax.numpy as jnp
import numpy as np
from jax import lax
from jax.experimental import pallas as pl
from jax.experimental.pallas import tpu as pltpu
from jax.sharding import PartitionSpec as P

NEWTON = 3
ROWS = 48
SIDE = 16
EXACT = lax.Precision.HIGHEST
VMEM_LIMIT = 40 * 1024 * 1024

OWN = (0, 2, 4, -3, -4)
OTHER = (2, 4, -3)
STACK = (3, 0, 2, 4)
EARLY = (
    (3, 1), (0, 1),
    (3, 2), (0, 2),
    (0, 3),
    (3, 5), (0, 5),
    (0, 7), (2, 7),
)
NEXT = ((4, 1), (4, 2), (4, 3), (4, 5), (4, 7))
LATE = ((0, 6), (2, 6))
PAIRS = EARLY + NEXT + LATE
DIAGONAL = PAIRS.index((4, 2))
POSITION = (8, 6, 10, 2, 5, 12, 7, 3, 13, 11, 9, 0, 4, 1, 14, 15)
CHIPS = SIDE // 2
SUM_ROWS = 3 * ROWS + 32


def frame_block(column, z, index):
    if index < len(OWN):
        return column * SIDE + (z + OWN[index]) % SIDE
    return (1 - column) * SIDE + (z + OTHER[index - len(OWN)]) % SIDE


def two_diagonals(z):
    return (z + SIDE - 2) % SIDE < SIDE // 2


def ends_of(column, z, pair):
    p, q = PAIRS[pair]
    if pair == len(PAIRS) - 1 and column == 1:
        p = 4
    a, b = frame_block(column, z, p), frame_block(column, z, q)
    if pair == DIAGONAL and two_diagonals(z):
        return ((a, a), (b, b))
    return ((a, b), (b, a))


def around(a, b, n):
    return min((a - b) % n, (b - a) % n)


def distance(column, z, chip, end):
    to_column, to_z = divmod(end[0], SIDE)
    to_chip = end[1] // 4
    x, to_x = 2 * (chip % 2) + column, 2 * (to_chip % 2) + to_column
    return around(z, to_z, SIDE) + around(chip // 2, to_chip // 2, 4) + around(x, to_x, 4)


def order_of_chips(column, z):
    cost = [[0] * CHIPS for _ in range(CHIPS)]
    for k in range(CHIPS):
        for chip in range(CHIPS):
            for pair in POSITION[2 * k : 2 * k + 2]:
                far = [distance(column, z, chip, end) for end in ends_of(column, z, pair)]
                cost[k][chip] += 2 ** sum(far) + 2 * 4 ** max(far)
    best = {0: (0, ())}
    for k in range(CHIPS):
        later = {}
        for taken, (value, order) in best.items():
            for chip in range(CHIPS):
                if not taken >> chip & 1:
                    entry = (value + cost[k][chip], order + (chip,))
                    key = taken | 1 << chip
                    later[key] = min(later.get(key, entry), entry)
        best = later
    return best[(1 << CHIPS) - 1][1]


def routes():
    orders, ends, diagonal = [], [], []
    for column in range(2):
        for z in range(SIDE):
            order = order_of_chips(column, z)
            orders.append(order)
            for device in range(SIDE):
                pair = POSITION[2 * order.index(device // 2) + device % 2]
                ends.append(ends_of(column, z, pair))
                diagonal.append(int(pair == DIAGONAL and two_diagonals(z)))
    place = lambda end: end[0] * SIDE + end[1] // 2
    at = {}
    for device, pair in enumerate(ends):
        for which, end in enumerate(pair):
            at.setdefault(place(end), []).append((device, which))
    assert len(at) == len(ends) and all(len(v) == 2 for v in at.values())
    swapped = [None] * len(ends)
    for seed in range(len(ends)):
        device, enter = seed, 0
        while swapped[device] is None:
            swapped[device] = enter
            node = place(ends[device][1 - enter])
            device, enter = [e for e in at[node] if e != (device, 1 - enter)][0]
    first = [place(ends[d][swapped[d]]) for d in range(len(ends))]
    second = [place(ends[d][1 - swapped[d]]) for d in range(len(ends))]
    assert len(set(first)) == len(set(second)) == len(ends)
    half = [0] * len(ends)
    for d in range(len(ends)):
        half[first[d]] = ends[d][swapped[d]][1] % 2
    table = [a + 2 * b + 4 * c for a, b, c in zip(swapped, half, diagonal)]
    return orders, first, second, table


def lookup(step, values):
    out = jnp.int32(values[0])
    for k, value in enumerate(values):
        out = jnp.where(step == k, jnp.int32(value), out)
    return out


def iota(shape, axis):
    return lax.broadcasted_iota(jnp.int32, shape, axis)


def dot_t(a, b):
    return lax.dot_general(a, b, (((1,), (1,)), ((), ())), precision=EXACT, preferred_element_type=jnp.float32)


def product(a, b):
    return lax.dot_general(a, b, (((1,), (1,)), ((), ())), preferred_element_type=jnp.float32)


def halves(x):
    high = x.astype(jnp.bfloat16)
    return high, (x - high.astype(jnp.float32)).astype(jnp.bfloat16)


def stage(x, mass):
    local = jnp.sum(mass)
    mean = jnp.sum(x * mass, axis=1, keepdims=True) / local
    x = x - mean
    wx = x * mass
    square = jnp.sum(wx * x, axis=1, keepdims=True)
    return x, wx, mean, square[:ROWS] + square[ROWS : 2 * ROWS] + square[2 * ROWS :], local


def stage_rows(block, mass, at, core, weighted, feature):
    atoms = block.shape[1]
    _, wx, mean, square, local = stage(block[...], mass)
    high, low = halves(wx)
    for k, part in enumerate((high, high, low)):
        weighted[at * 3 * ROWS : (at + 1) * 3 * ROWS, k * atoms : (k + 1) * atoms] = part
    lane = iota((ROWS, 128), 1) - 8 * core
    out = jnp.where(lane == 51, local, jnp.where(lane == 64 - 8 * core, square, 0.0))
    for c in range(3):
        out = jnp.where(lane == 48 + c, mean[c * ROWS : (c + 1) * ROWS], out)
    feature[at] = out


def stage_columns(block, mass, at, core, centered, feature):
    atoms = block.shape[1]
    x, _, mean, square, _ = stage(block[...], mass)
    high, low = halves(x)
    for k, part in enumerate((high, low, high)):
        centered[at, : 3 * ROWS, k * atoms : (k + 1) * atoms] = part
    lane = iota((ROWS, 128), 1) - 8 * core
    out = jnp.where(lane == 65 - 8 * core, square, 0.0)
    for c in range(3):
        out = jnp.where(lane == 52 + c, mean[c * ROWS : (c + 1) * ROWS], out)
    feature[at] = out


def rest_of(tail):
    tail = jnp.where(iota((3 * ROWS, 128), 1) < 16, tail, 0.0)
    return tail[:ROWS] + pltpu.roll(tail[ROWS : 2 * ROWS], 16, 1) + pltpu.roll(tail[2 * ROWS :], 32, 1)


def packed(rest):
    lane, tail = iota((16, 128), 1), rest[32:]
    low = pltpu.roll(jnp.where(lane < 48, tail, 0.0), 80, 1)
    high = pltpu.roll(jnp.where(lane < 48, 0.0, tail), 32, 1)
    return rest[:32] + jnp.concatenate([low, high], axis=0)


def unpacked(rows):
    tail = jnp.where(iota((16, 128), 1) < 48, pltpu.roll(rows[:16], 48, 1), pltpu.roll(rows[16:], 96, 1))
    return jnp.concatenate([rows, tail], axis=0)


def put_pair(out, pair, core, value, feature):
    k, owner = divmod(POSITION.index(pair), 2)
    at = jnp.where(core == owner, k, CHIPS + k)
    out[at, : 3 * ROWS] = value[:, :128]
    out[at, 3 * ROWS :] = packed(rest_of(value[:, 128:]) + feature)


def put_groups(out, pairs, order, core, weighted, centered, row_feature, column_feature):
    for at, k in enumerate(order):
        group = [pair for pair in pairs if pair[1] == k]
        start = STACK.index(group[0][0])
        assert STACK[start : start + len(group)] == tuple(p for p, _ in group)
        values = product(weighted[start * 3 * ROWS : (start + len(group)) * 3 * ROWS], centered[at])
        for n, pair in enumerate(group):
            value = values[n * 3 * ROWS : (n + 1) * 3 * ROWS]
            put_pair(out, PAIRS.index(pair), core, value, row_feature[start + n] + column_feature[at])


def first_kernel(flags, mass_ref, own, plus2, other2, weighted, row_feature, centered, column_feature):
    core = flags[2]
    mass = mass_ref[...].astype(jnp.float32)
    stage_rows(own, mass, STACK.index(0), core, weighted, row_feature)
    for at, block in enumerate((plus2, other2)):
        stage_columns(block, mass, at, core, centered, column_feature)


def early_kernel(
    flags, mass_ref, other3, plus4, minus3, first_centered, first_feature, _, __,
    out, weighted, row_feature, centered, column_feature,
):
    core = flags[2]
    mass = mass_ref[...].astype(jnp.float32)
    for at, block in enumerate((plus4, minus3, other3)):
        stage_columns(block, mass, at, core, centered, column_feature)
    for k, block in ((3, minus3), (2, plus4)):
        stage_rows(block, mass, STACK.index(k), core, weighted, row_feature)
    put_groups(out, EARLY, (1, 5), core, weighted, first_centered, row_feature, first_feature)
    put_groups(out, EARLY, (2, 3, 7), core, weighted, centered, row_feature, column_feature)


def next_kernel(
    flags, mass_ref, minus4, first_centered, first_feature, centered, column_feature, _, __, ___,
    out, weighted, row_feature, own_centered, own_feature,
):
    core = flags[2]
    mass = mass_ref[...].astype(jnp.float32)
    stage_rows(minus4, mass, STACK.index(4), core, weighted, row_feature)
    put_groups(out, NEXT, (1, 5), core, weighted, first_centered, row_feature, first_feature)
    put_groups(out, NEXT, (2, 3, 7), core, weighted, centered, row_feature, column_feature)

    @pl.when(flags[1] == 1)
    def _():
        stage_columns(minus4, mass, 0, core, own_centered, own_feature)
        p, q, last = STACK.index(4), STACK.index(2), 0
        upper = product(weighted[p * 3 * ROWS : (p + 1) * 3 * ROWS], own_centered[0])
        lower = product(weighted[q * 3 * ROWS : (q + 1) * 3 * ROWS], centered[last])
        i, j = iota((3 * ROWS, 256), 0) % ROWS, iota((3 * ROWS, 256), 1) % ROWS
        at = iota((ROWS, 256), 1)
        on = jnp.where((i == j) & (iota((3 * ROWS, 256), 1) < 3 * ROWS), lower, 0.0)
        lane = iota((ROWS, 128), 1)
        ends = row_feature[p] + column_feature[last]
        for c in range(3):
            mine = on[c * ROWS : (c + 1) * ROWS]
            for d in range(3):
                inside = (at >= d * ROWS) & (at < (d + 1) * ROWS)
                value = jnp.sum(jnp.where(inside, mine, 0.0), axis=1, keepdims=True)
                ends = jnp.where(lane == 66 + 3 * c + d, value, ends)
        put_pair(out, DIAGONAL, core, jnp.where(i <= j, upper, lower), ends)


def late_kernel(flags, mass_ref, weighted, row_feature, other4, sums, send, keep, last, centered, column_feature):
    core = flags[2]
    mass = mass_ref[...].astype(jnp.float32)
    stage_columns(other4, mass, 0, core, centered, column_feature)
    values = product(weighted[3 * ROWS :], centered[0])
    other = flags[0] == 1
    for n in range(2):
        rows = values[: 3 * ROWS] if n == 0 else jnp.where(other, values[6 * ROWS :], values[3 * ROWS : 6 * ROWS])
        feature = row_feature[1] if n == 0 else jnp.where(other, row_feature[3], row_feature[2])
        at = jnp.where(core == n, 0, 1)
        last[at, : 3 * ROWS] = rows[:, :128]
        last[at, 3 * ROWS :] = packed(rest_of(rows[:, 128:]) + feature + column_feature[0])
    keep[0] = last[0]
    send[CHIPS - 1] = last[1]
    send[: CHIPS - 1] = sums[CHIPS : 2 * CHIPS - 1]


def merge_kernel(sums, keep, taken, out):
    out[: CHIPS - 1] = sums[: CHIPS - 1] + taken[: CHIPS - 1]
    out[CHIPS - 1] = keep[0] + taken[CHIPS - 1]


def det_four(rows):
    a00, a01, a02, a03 = rows[0]
    a10, a11, a12, a13 = rows[1]
    a20, a21, a22, a23 = rows[2]
    a30, a31, a32, a33 = rows[3]
    s0 = a00 * a11 - a10 * a01
    s1 = a00 * a12 - a10 * a02
    s2 = a00 * a13 - a10 * a03
    s3 = a01 * a12 - a11 * a02
    s4 = a01 * a13 - a11 * a03
    s5 = a02 * a13 - a12 * a03
    t5 = a22 * a33 - a32 * a23
    t4 = a21 * a33 - a31 * a23
    t3 = a21 * a32 - a31 * a22
    t2 = a20 * a33 - a30 * a23
    t1 = a20 * a32 - a30 * a22
    t0 = a20 * a31 - a30 * a21
    return s0 * t5 - s1 * t4 + s2 * t3 + s3 * t2 - s4 * t1 + s5 * t0


def quaternion_fit(moment, spread_rows, spread_cols):
    sxx, sxy, sxz, syx, syy, syz, szx, szy, szz = moment
    coef_two = -2.0 * sum(m * m for m in moment)
    det_three = (
        sxx * (syy * szz - syz * szy)
        - sxy * (syx * szz - syz * szx)
        + sxz * (syx * szy - syy * szx)
    )
    coef_one = -8.0 * det_three
    rows = [
        [sxx + syy + szz, syz - szy, szx - sxz, sxy - syx],
        [syz - szy, sxx - syy - szz, sxy + syx, szx + sxz],
        [szx - sxz, sxy + syx, -sxx + syy - szz, syz + szy],
        [sxy - syx, szx + sxz, syz + szy, -sxx - syy + szz],
    ]
    coef_zero = det_four(rows)
    lam = 0.5 * (spread_rows + spread_cols)
    for turn in range(NEWTON):
        square = lam * lam
        value = (square + coef_two) * square + coef_one * lam + coef_zero
        slope = 4.0 * square * lam + 2.0 * coef_two * lam + coef_one
        lam = lam - value / slope
    return spread_rows + spread_cols - 2.0 * lam


def square_tile(x):
    return jnp.concatenate([x, jnp.zeros((128 - x.shape[0], 128), jnp.float32)], axis=0)


def fit_kernel(flags, parts, first, second):
    diagonal, swap = flags[1] == 1, flags[0] == 1
    total = parts[0]
    for a in range(1, CHIPS):
        total = total + parts[a]
    lane, row = iota((ROWS, 128), 1), iota((ROWS, 128), 0)
    rest = unpacked(total[3 * ROWS :])

    gathered = jnp.zeros((ROWS, 128), jnp.float32)
    for a in range(CHIPS):
        tile = jnp.where((lane >= 48) & (lane < 64), unpacked(parts[a, 3 * ROWS :]), 0.0)
        gathered = gathered + pltpu.roll(tile, (16 * a - 48) % 128, 1)

    sender = lane % 8 == 0

    def per_sender(which):
        return jnp.where(sender, pltpu.roll(gathered, (128 - which) % 128, 1), 0.0)

    mass = per_sender(3)
    whole = jnp.sum(mass, axis=1, keepdims=True)

    def offsets(base):
        out = []
        for c in range(3):
            mean = per_sender(base + c)
            centroid = jnp.sum(mass * mean, axis=1, keepdims=True) / whole
            out.append(jnp.where(sender, mean - centroid, 0.0))
        return out

    off_p, off_q = offsets(0), offsets(4)

    def spread(off, at):
        within = jnp.sum(jnp.where(lane == at, rest, 0.0), axis=1, keepdims=True)
        between = jnp.sum(mass * sum(o * o for o in off), axis=1, keepdims=True)
        return (within + between) / whole

    spread_p, spread_q = spread(off_p, 64), spread(off_q, 65)

    def as_row(column):
        return jnp.sum(jnp.where(row == lane, column, 0.0), axis=0, keepdims=True)

    upper = row <= lane
    corner = lane == ROWS
    row_p, row_q = as_row(spread_p), as_row(spread_q)
    spread_rows = jnp.where(upper, spread_p, jnp.where(diagonal, spread_q, spread_p))
    spread_cols = jnp.where(upper, jnp.where(diagonal, row_p, row_q), row_q)
    spread_rows = jnp.where(corner, spread_q, spread_rows)
    spread_cols = jnp.where(corner, spread_q, spread_cols)

    def parts_of(blocks, first):
        high, low = halves(jnp.concatenate(blocks, axis=0))
        return jnp.concatenate([high, high, low] if first else [high, low, high], axis=1)

    up_rows = parts_of([mass * p for p in off_p], True)
    low_rows = parts_of([mass * jnp.where(diagonal, q, p) for p, q in zip(off_p, off_q)], True)
    blank = jnp.zeros((256 - 3 * ROWS, 128), jnp.float32)
    up_columns = parts_of([jnp.where(diagonal, p, q) for p, q in zip(off_p, off_q)] + [blank], False)
    low_columns = parts_of(off_q + [blank], False)
    above = iota((3 * ROWS, 256), 0) % ROWS <= iota((3 * ROWS, 256), 1) % ROWS
    between = jnp.where(above, product(up_rows, up_columns), product(low_rows, low_columns))
    sums = total[: 3 * ROWS] + between[:, :128]
    narrow = rest + rest_of(between[:, 128:])
    moment = []
    for c in range(3):
        main = sums[c * ROWS : (c + 1) * ROWS]
        tail = pltpu.roll(narrow, (32 - 16 * c) % 128, 1)
        shifted = [main, pltpu.roll(main, 128 - 48, 1), jnp.where(lane < 32, pltpu.roll(main, 128 - 96, 1), tail)]
        for d in range(3):
            value = shifted[d]
            end = jnp.sum(jnp.where(lane == 66 + 3 * c + d, rest, 0.0), axis=1, keepdims=True)
            end = end + jnp.sum(mass * off_q[c] * off_q[d], axis=1, keepdims=True)
            moment.append(jnp.where(corner, end, value) / whole)
    msd = quaternion_fit(moment, spread_rows, spread_cols)
    corner_value = jnp.sum(jnp.where(corner, msd, 0.0), axis=1, keepdims=True)
    msd = jnp.where(lane < ROWS, msd, 0.0)
    turned = square_tile(msd).T[:ROWS]
    plain_a = jnp.where(diagonal, jnp.where(upper, msd, turned), msd)
    mirrored = jnp.where(row > lane, msd, jnp.where(row == lane, corner_value, turned))
    plain_b = jnp.where(diagonal, mirrored, turned)
    for out, here, there in ((first, plain_a, plain_b), (second, plain_b, plain_a)):
        value = jnp.where(swap, there, here)
        out[...] = value[: ROWS // 2] + pltpu.roll(value[ROWS // 2 :], 64, 1)


def on_device(coords, weights):
    orders, first, second, table = routes()
    frame, atom = lax.axis_index("frame"), lax.axis_index("atom")
    build_flags = jnp.stack([frame // SIDE, two_diagonals(frame % SIDE), atom % 2]).astype(jnp.int32)
    mine = jnp.asarray(np.array(table), jnp.int32)[frame * SIDE + atom]
    fit_flags = jnp.stack([mine & 1, mine >> 2])
    mass = weights[None, :]

    def along(block, distance):
        route = [
            (c * SIDE + (k + distance) % SIDE, c * SIDE + k) for c in range(2) for k in range(SIDE)
        ]
        return lax.ppermute(block, "frame", route)

    def across(block):
        return lax.ppermute(block, "frame", [((f + SIDE) % (2 * SIDE), f) for f in range(2 * SIDE)])

    own = coords.reshape(3 * ROWS, coords.shape[2])
    plus2 = along(own, 2)
    minus3 = along(own, -3)
    plus4 = along(plus2, 2)
    minus4 = along(minus3, -1)
    other2 = across(plus2)
    other3 = across(minus3)
    other4 = across(plus4)

    atoms = own.shape[1]
    smem = pl.BlockSpec(memory_space=pltpu.SMEM)
    vmem = pl.BlockSpec(memory_space=pltpu.VMEM)
    params = pltpu.CompilerParams(vmem_limit_bytes=VMEM_LIMIT)

    def columns_scratch(n):
        return [pltpu.VMEM((n, 256, 3 * atoms), jnp.bfloat16), pltpu.VMEM((n, ROWS, 128), jnp.float32)]

    def cost(pairs):
        return pl.CostEstimate(flops=pairs * 2 * 3 * ROWS * 256 * atoms * 3, bytes_accessed=4_000_000, transcendentals=0)

    def sums_of(n):
        return jax.ShapeDtypeStruct((n, SUM_ROWS, 128), jnp.float32)

    staged = [
        jax.ShapeDtypeStruct((len(STACK) * 3 * ROWS, 3 * atoms), jnp.bfloat16),
        jax.ShapeDtypeStruct((len(STACK), ROWS, 128), jnp.float32),
    ]
    columns = [
        jax.ShapeDtypeStruct((2, 256, 3 * atoms), jnp.bfloat16),
        jax.ShapeDtypeStruct((2, ROWS, 128), jnp.float32),
    ]
    weighted, row_feature, centered, column_feature = pl.pallas_call(
        first_kernel,
        out_shape=staged + columns,
        in_specs=[smem] + [vmem] * 4,
        out_specs=[vmem] * 4,
        compiler_params=params,
        cost_estimate=cost(len(EARLY)),
    )(build_flags, mass, own, plus2, other2)
    more = [
        jax.ShapeDtypeStruct((3, 256, 3 * atoms), jnp.bfloat16),
        jax.ShapeDtypeStruct((3, ROWS, 128), jnp.float32),
    ]
    sums, weighted, row_feature, more_centered, more_feature = pl.pallas_call(
        early_kernel,
        out_shape=[sums_of(2 * CHIPS)] + staged + more,
        in_specs=[smem] + [vmem] * 8,
        out_specs=[vmem] * 5,
        input_output_aliases={7: 1, 8: 2},
        compiler_params=params,
        cost_estimate=cost(len(EARLY)),
    )(build_flags, mass, other3, plus4, minus3, centered, column_feature, weighted, row_feature)
    sums, weighted, row_feature = pl.pallas_call(
        next_kernel,
        out_shape=[sums_of(2 * CHIPS)] + staged,
        in_specs=[smem] + [vmem] * 9,
        out_specs=[vmem] * 3,
        scratch_shapes=columns_scratch(1),
        input_output_aliases={7: 0, 8: 1, 9: 2},
        compiler_params=params,
        cost_estimate=cost(len(NEXT) + 1),
    )(
        build_flags, mass, minus4, centered, column_feature, more_centered, more_feature, sums, weighted, row_feature
    )
    send, keep = pl.pallas_call(
        late_kernel,
        out_shape=[sums_of(CHIPS), sums_of(1)],
        in_specs=[smem] + [vmem] * 5,
        out_specs=[vmem] * 2,
        scratch_shapes=[pltpu.VMEM((2, SUM_ROWS, 128), jnp.float32)] + columns_scratch(1),
        compiler_params=params,
        cost_estimate=cost(len(LATE) + 1),
    )(build_flags, mass, weighted, row_feature, other4, sums)
    taken = lax.ppermute(send, "atom", [(a, a ^ 1) for a in range(SIDE)])
    merged = pl.pallas_call(
        merge_kernel,
        out_shape=sums_of(CHIPS),
        in_specs=[vmem] * 3,
        out_specs=vmem,
        compiler_params=params,
    )(sums, keep, taken)
    groups = [[f * SIDE + 2 * chip + c for chip in orders[f]] for f in range(2 * SIDE) for c in range(2)]
    parts = lax.all_to_all(merged, ("frame", "atom"), 0, 0, axis_index_groups=groups, tiled=True)

    block = jax.ShapeDtypeStruct((ROWS // 2, 128), jnp.float32)
    one, two = pl.pallas_call(
        fit_kernel,
        out_shape=(block, block),
        in_specs=[smem, vmem],
        out_specs=(vmem, vmem),
        compiler_params=params,
    )(fit_flags, parts)
    one = lax.ppermute(one, ("frame", "atom"), list(enumerate(first)))
    two = lax.ppermute(two, ("frame", "atom"), list(enumerate(second)))
    left = jnp.where(mine >> 1 & 1, two, one)
    right = jnp.where(mine >> 1 & 1, one, two)
    upper = jnp.concatenate([left[:, :ROWS], right[:, :ROWS]], axis=1)
    lower = jnp.concatenate([left[:, 64 : 64 + ROWS], right[:, 64 : 64 + ROWS]], axis=1)
    return jnp.concatenate([upper, lower], axis=0)


def solution(mesh):
    placed = (P(None, "frame", "atom"), P("atom"))
    return jax.shard_map(
        on_device, mesh=mesh, in_specs=placed, out_specs=P("frame", "atom"), check_vma=False
    )
```

```python
import functools

import jax
import jax.numpy as jnp
import numpy as np
from jax import lax
from jax.experimental import pallas as pl
from jax.experimental.pallas import tpu as pltpu
from jax.sharding import PartitionSpec as P

NEWTON = 3
ROWS = 48
SIDE = 16
EXACT = lax.Precision.HIGHEST
VMEM_LIMIT = 40 * 1024 * 1024

OWN = (0, 2, 4, -3, -4)
OTHER = (2, 4, -3)
STACK = (3, 0, 2, 4)
EARLY = (
    (3, 1), (0, 1),
    (3, 2), (0, 2),
    (0, 3),
    (3, 5), (0, 5),
    (0, 7), (2, 7),
)
NEXT = ((4, 1), (4, 2), (4, 3), (4, 5), (4, 7))
LATE = ((0, 6), (2, 6))
PAIRS = EARLY + NEXT + LATE
DIAGONAL = PAIRS.index((4, 2))
POSITION = (8, 6, 10, 2, 5, 12, 7, 3, 13, 11, 9, 0, 4, 1, 14, 15)
CHIPS = SIDE // 2
SUM_ROWS = 3 * ROWS + 32


def frame_block(column, z, index):
    if index < len(OWN):
        return column * SIDE + (z + OWN[index]) % SIDE
    return (1 - column) * SIDE + (z + OTHER[index - len(OWN)]) % SIDE


def two_diagonals(z):
    return (z + SIDE - 2) % SIDE < SIDE // 2


def ends_of(column, z, pair):
    p, q = PAIRS[pair]
    if pair == len(PAIRS) - 1 and column == 1:
        p = 4
    a, b = frame_block(column, z, p), frame_block(column, z, q)
    if pair == DIAGONAL and two_diagonals(z):
        return ((a, a), (b, b))
    return ((a, b), (b, a))


def around(a, b, n):
    return min((a - b) % n, (b - a) % n)


def distance(column, z, chip, end):
    to_column, to_z = divmod(end[0], SIDE)
    to_chip = end[1] // 4
    x, to_x = 2 * (chip % 2) + column, 2 * (to_chip % 2) + to_column
    return around(z, to_z, SIDE) + around(chip // 2, to_chip // 2, 4) + around(x, to_x, 4)


def order_of_chips(column, z):
    cost = [[0] * CHIPS for _ in range(CHIPS)]
    for k in range(CHIPS):
        for chip in range(CHIPS):
            for pair in POSITION[2 * k : 2 * k + 2]:
                far = [distance(column, z, chip, end) for end in ends_of(column, z, pair)]
                cost[k][chip] += 2 ** sum(far) + 2 * 4 ** max(far)
    best = {0: (0, ())}
    for k in range(CHIPS):
        later = {}
        for taken, (value, order) in best.items():
            for chip in range(CHIPS):
                if not taken >> chip & 1:
                    entry = (value + cost[k][chip], order + (chip,))
                    key = taken | 1 << chip
                    later[key] = min(later.get(key, entry), entry)
        best = later
    return best[(1 << CHIPS) - 1][1]


def routes():
    orders, ends, diagonal = [], [], []
    for column in range(2):
        for z in range(SIDE):
            order = order_of_chips(column, z)
            orders.append(order)
            for device in range(SIDE):
                pair = POSITION[2 * order.index(device // 2) + device % 2]
                ends.append(ends_of(column, z, pair))
                diagonal.append(int(pair == DIAGONAL and two_diagonals(z)))
    place = lambda end: end[0] * SIDE + end[1] // 2
    at = {}
    for device, pair in enumerate(ends):
        for which, end in enumerate(pair):
            at.setdefault(place(end), []).append((device, which))
    assert len(at) == len(ends) and all(len(v) == 2 for v in at.values())
    swapped = [None] * len(ends)
    for seed in range(len(ends)):
        ring, device, enter = [], seed, 0
        while swapped[device] is None:
            swapped[device] = enter
            ring.append(device)
            node = place(ends[device][1 - enter])
            device, enter = [e for e in at[node] if e != (device, 1 - enter)][0]
        cost = [0, 0]
        for d in ring:
            column, z = divmod(d // SIDE, SIDE)
            far = [distance(column, z, d % SIDE // 2, ends[d][e]) for e in (swapped[d], 1 - swapped[d])]
            cost[0] += 2 ** (2 * far[0] + far[1])
            cost[1] += 2 ** (2 * far[1] + far[0])
        if cost[1] < cost[0]:
            for d in ring:
                swapped[d] = 1 - swapped[d]
    first = [place(ends[d][swapped[d]]) for d in range(len(ends))]
    second = [place(ends[d][1 - swapped[d]]) for d in range(len(ends))]
    assert len(set(first)) == len(set(second)) == len(ends)
    half = [0] * len(ends)
    for d in range(len(ends)):
        half[first[d]] = ends[d][swapped[d]][1] % 2
    table = [a + 2 * b + 4 * c for a, b, c in zip(swapped, half, diagonal)]
    return orders, first, second, table


def lookup(step, values):
    out = jnp.int32(values[0])
    for k, value in enumerate(values):
        out = jnp.where(step == k, jnp.int32(value), out)
    return out


def iota(shape, axis):
    return lax.broadcasted_iota(jnp.int32, shape, axis)


def dot_t(a, b):
    return lax.dot_general(a, b, (((1,), (1,)), ((), ())), precision=EXACT, preferred_element_type=jnp.float32)


def product(a, b):
    return lax.dot_general(a, b, (((1,), (1,)), ((), ())), preferred_element_type=jnp.float32)


def halves(x):
    high = x.astype(jnp.bfloat16)
    return high, (x - high.astype(jnp.float32)).astype(jnp.bfloat16)


def stage(x, mass):
    local = jnp.sum(mass)
    mean = jnp.sum(x * mass, axis=1, keepdims=True) / local
    x = x - mean
    wx = x * mass
    square = jnp.sum(wx * x, axis=1, keepdims=True)
    return x, wx, mean, square[:ROWS] + square[ROWS : 2 * ROWS] + square[2 * ROWS :], local


def stage_rows(block, mass, at, core, weighted, feature):
    atoms = block.shape[1]
    _, wx, mean, square, local = stage(block[...], mass)
    high, low = halves(wx)
    for k, part in enumerate((high, high, low)):
        weighted[at * 3 * ROWS : (at + 1) * 3 * ROWS, k * atoms : (k + 1) * atoms] = part
    lane = iota((ROWS, 128), 1) - 8 * core
    out = jnp.where(lane == 51, local, jnp.where(lane == 64 - 8 * core, square, 0.0))
    for c in range(3):
        out = jnp.where(lane == 48 + c, mean[c * ROWS : (c + 1) * ROWS], out)
    feature[at] = out


def stage_columns(block, mass, at, core, centered, feature):
    atoms = block.shape[1]
    x, _, mean, square, _ = stage(block[...], mass)
    high, low = halves(x)
    for k, part in enumerate((high, low, high)):
        centered[at, : 3 * ROWS, k * atoms : (k + 1) * atoms] = part
    lane = iota((ROWS, 128), 1) - 8 * core
    out = jnp.where(lane == 65 - 8 * core, square, 0.0)
    for c in range(3):
        out = jnp.where(lane == 52 + c, mean[c * ROWS : (c + 1) * ROWS], out)
    feature[at] = out


def rest_of(tail):
    tail = jnp.where(iota((3 * ROWS, 128), 1) < 16, tail, 0.0)
    return tail[:ROWS] + pltpu.roll(tail[ROWS : 2 * ROWS], 16, 1) + pltpu.roll(tail[2 * ROWS :], 32, 1)


def packed(rest):
    lane, tail = iota((16, 128), 1), rest[32:]
    low = pltpu.roll(jnp.where(lane < 48, tail, 0.0), 80, 1)
    high = pltpu.roll(jnp.where(lane < 48, 0.0, tail), 32, 1)
    return rest[:32] + jnp.concatenate([low, high], axis=0)


def unpacked(rows):
    tail = jnp.where(iota((16, 128), 1) < 48, pltpu.roll(rows[:16], 48, 1), pltpu.roll(rows[16:], 96, 1))
    return jnp.concatenate([rows, tail], axis=0)


def put_pair(out, pair, core, value, feature):
    k, owner = divmod(POSITION.index(pair), 2)
    at = jnp.where(core == owner, k, CHIPS + k)
    out[at, : 3 * ROWS] = value[:, :128]
    out[at, 3 * ROWS :] = packed(rest_of(value[:, 128:]) + feature)


def put_groups(out, pairs, order, core, weighted, centered, row_feature, column_feature):
    for at, k in enumerate(order):
        group = [pair for pair in pairs if pair[1] == k]
        start = STACK.index(group[0][0])
        assert STACK[start : start + len(group)] == tuple(p for p, _ in group)
        values = product(weighted[start * 3 * ROWS : (start + len(group)) * 3 * ROWS], centered[at])
        for n, pair in enumerate(group):
            value = values[n * 3 * ROWS : (n + 1) * 3 * ROWS]
            put_pair(out, PAIRS.index(pair), core, value, row_feature[start + n] + column_feature[at])


def first_kernel(flags, mass_ref, own, plus2, other2, weighted, row_feature, centered, column_feature):
    core = flags[2]
    mass = mass_ref[...].astype(jnp.float32)
    stage_rows(own, mass, STACK.index(0), core, weighted, row_feature)
    for at, block in enumerate((plus2, other2)):
        stage_columns(block, mass, at, core, centered, column_feature)


def early_kernel(
    flags, mass_ref, other3, plus4, minus3, first_centered, first_feature, _, __,
    out, weighted, row_feature, centered, column_feature,
):
    core = flags[2]
    mass = mass_ref[...].astype(jnp.float32)
    for at, block in enumerate((plus4, minus3, other3)):
        stage_columns(block, mass, at, core, centered, column_feature)
    for k, block in ((3, minus3), (2, plus4)):
        stage_rows(block, mass, STACK.index(k), core, weighted, row_feature)
    put_groups(out, EARLY, (1, 5), core, weighted, first_centered, row_feature, first_feature)
    put_groups(out, EARLY, (2, 3, 7), core, weighted, centered, row_feature, column_feature)


def next_kernel(
    flags, mass_ref, minus4, first_centered, first_feature, centered, column_feature, _, __, ___,
    out, weighted, row_feature, own_centered, own_feature,
):
    core = flags[2]
    mass = mass_ref[...].astype(jnp.float32)
    stage_rows(minus4, mass, STACK.index(4), core, weighted, row_feature)
    put_groups(out, NEXT, (1, 5), core, weighted, first_centered, row_feature, first_feature)
    put_groups(out, NEXT, (2, 3, 7), core, weighted, centered, row_feature, column_feature)

    @pl.when(flags[1] == 1)
    def _():
        stage_columns(minus4, mass, 0, core, own_centered, own_feature)
        p, q, last = STACK.index(4), STACK.index(2), 0
        upper = product(weighted[p * 3 * ROWS : (p + 1) * 3 * ROWS], own_centered[0])
        lower = product(weighted[q * 3 * ROWS : (q + 1) * 3 * ROWS], centered[last])
        i, j = iota((3 * ROWS, 256), 0) % ROWS, iota((3 * ROWS, 256), 1) % ROWS
        at = iota((ROWS, 256), 1)
        on = jnp.where((i == j) & (iota((3 * ROWS, 256), 1) < 3 * ROWS), lower, 0.0)
        lane = iota((ROWS, 128), 1)
        ends = row_feature[p] + column_feature[last]
        for c in range(3):
            mine = on[c * ROWS : (c + 1) * ROWS]
            for d in range(3):
                inside = (at >= d * ROWS) & (at < (d + 1) * ROWS)
                value = jnp.sum(jnp.where(inside, mine, 0.0), axis=1, keepdims=True)
                ends = jnp.where(lane == 66 + 3 * c + d, value, ends)
        put_pair(out, DIAGONAL, core, jnp.where(i <= j, upper, lower), ends)


def late_kernel(flags, mass_ref, weighted, row_feature, other4, sums, send, keep, last, centered, column_feature):
    core = flags[2]
    mass = mass_ref[...].astype(jnp.float32)
    stage_columns(other4, mass, 0, core, centered, column_feature)
    values = product(weighted[3 * ROWS :], centered[0])
    other = flags[0] == 1
    for n in range(2):
        rows = values[: 3 * ROWS] if n == 0 else jnp.where(other, values[6 * ROWS :], values[3 * ROWS : 6 * ROWS])
        feature = row_feature[1] if n == 0 else jnp.where(other, row_feature[3], row_feature[2])
        at = jnp.where(core == n, 0, 1)
        last[at, : 3 * ROWS] = rows[:, :128]
        last[at, 3 * ROWS :] = packed(rest_of(rows[:, 128:]) + feature + column_feature[0])
    keep[0] = last[0]
    send[CHIPS - 1] = last[1]
    send[: CHIPS - 1] = sums[CHIPS : 2 * CHIPS - 1]


def merge_kernel(sums, keep, taken, out):
    out[: CHIPS - 1] = sums[: CHIPS - 1] + taken[: CHIPS - 1]
    out[CHIPS - 1] = keep[0] + taken[CHIPS - 1]


def det_four(rows):
    a00, a01, a02, a03 = rows[0]
    a10, a11, a12, a13 = rows[1]
    a20, a21, a22, a23 = rows[2]
    a30, a31, a32, a33 = rows[3]
    s0 = a00 * a11 - a10 * a01
    s1 = a00 * a12 - a10 * a02
    s2 = a00 * a13 - a10 * a03
    s3 = a01 * a12 - a11 * a02
    s4 = a01 * a13 - a11 * a03
    s5 = a02 * a13 - a12 * a03
    t5 = a22 * a33 - a32 * a23
    t4 = a21 * a33 - a31 * a23
    t3 = a21 * a32 - a31 * a22
    t2 = a20 * a33 - a30 * a23
    t1 = a20 * a32 - a30 * a22
    t0 = a20 * a31 - a30 * a21
    return s0 * t5 - s1 * t4 + s2 * t3 + s3 * t2 - s4 * t1 + s5 * t0


def quaternion_fit(moment, spread_rows, spread_cols):
    sxx, sxy, sxz, syx, syy, syz, szx, szy, szz = moment
    coef_two = -2.0 * sum(m * m for m in moment)
    det_three = (
        sxx * (syy * szz - syz * szy)
        - sxy * (syx * szz - syz * szx)
        + sxz * (syx * szy - syy * szx)
    )
    coef_one = -8.0 * det_three
    rows = [
        [sxx + syy + szz, syz - szy, szx - sxz, sxy - syx],
        [syz - szy, sxx - syy - szz, sxy + syx, szx + sxz],
        [szx - sxz, sxy + syx, -sxx + syy - szz, syz + szy],
        [sxy - syx, szx + sxz, syz + szy, -sxx - syy + szz],
    ]
    coef_zero = det_four(rows)
    lam = 0.5 * (spread_rows + spread_cols)
    for turn in range(NEWTON):
        square = lam * lam
        value = (square + coef_two) * square + coef_one * lam + coef_zero
        slope = 4.0 * square * lam + 2.0 * coef_two * lam + coef_one
        lam = lam - value / slope
    return spread_rows + spread_cols - 2.0 * lam


def square_tile(x):
    return jnp.concatenate([x, jnp.zeros((128 - x.shape[0], 128), jnp.float32)], axis=0)


def fit_kernel(flags, parts, first, second):
    diagonal, swap = flags[1] == 1, flags[0] == 1
    total = parts[0]
    for a in range(1, CHIPS):
        total = total + parts[a]
    lane, row = iota((ROWS, 128), 1), iota((ROWS, 128), 0)
    rest = unpacked(total[3 * ROWS :])

    gathered = jnp.zeros((ROWS, 128), jnp.float32)
    for a in range(CHIPS):
        tile = jnp.where((lane >= 48) & (lane < 64), unpacked(parts[a, 3 * ROWS :]), 0.0)
        gathered = gathered + pltpu.roll(tile, (16 * a - 48) % 128, 1)

    sender = lane % 8 == 0

    def per_sender(which):
        return jnp.where(sender, pltpu.roll(gathered, (128 - which) % 128, 1), 0.0)

    mass = per_sender(3)
    whole = jnp.sum(mass, axis=1, keepdims=True)

    def offsets(base):
        out = []
        for c in range(3):
            mean = per_sender(base + c)
            centroid = jnp.sum(mass * mean, axis=1, keepdims=True) / whole
            out.append(jnp.where(sender, mean - centroid, 0.0))
        return out

    off_p, off_q = offsets(0), offsets(4)

    def spread(off, at):
        within = jnp.sum(jnp.where(lane == at, rest, 0.0), axis=1, keepdims=True)
        between = jnp.sum(mass * sum(o * o for o in off), axis=1, keepdims=True)
        return (within + between) / whole

    spread_p, spread_q = spread(off_p, 64), spread(off_q, 65)

    def as_row(column):
        return jnp.sum(jnp.where(row == lane, column, 0.0), axis=0, keepdims=True)

    upper = row <= lane
    corner = lane == ROWS
    row_p, row_q = as_row(spread_p), as_row(spread_q)
    spread_rows = jnp.where(upper, spread_p, jnp.where(diagonal, spread_q, spread_p))
    spread_cols = jnp.where(upper, jnp.where(diagonal, row_p, row_q), row_q)
    spread_rows = jnp.where(corner, spread_q, spread_rows)
    spread_cols = jnp.where(corner, spread_q, spread_cols)

    def parts_of(blocks, first):
        high, low = halves(jnp.concatenate(blocks, axis=0))
        return jnp.concatenate([high, high, low] if first else [high, low, high], axis=1)

    up_rows = parts_of([mass * p for p in off_p], True)
    low_rows = parts_of([mass * jnp.where(diagonal, q, p) for p, q in zip(off_p, off_q)], True)
    moment = []
    between = []
    for d in range(3):
        up = product(up_rows, parts_of([square_tile(jnp.where(diagonal, off_p[d], off_q[d]))], False))
        low = product(low_rows, parts_of([square_tile(off_q[d])], False))
        between.append((up, low))
    for c in range(3):
        main = total[c * ROWS : (c + 1) * ROWS]
        tail = pltpu.roll(rest, (32 - 16 * c) % 128, 1)
        shifted = [main, pltpu.roll(main, 128 - 48, 1), jnp.where(lane < 32, pltpu.roll(main, 128 - 96, 1), tail)]
        for d in range(3):
            up, low = (b[c * ROWS : (c + 1) * ROWS] for b in between[d])
            value = shifted[d] + jnp.where(upper, up, low)
            end = jnp.sum(jnp.where(lane == 66 + 3 * c + d, rest, 0.0), axis=1, keepdims=True)
            end = end + jnp.sum(mass * off_q[c] * off_q[d], axis=1, keepdims=True)
            moment.append(jnp.where(corner, end, value) / whole)
    msd = quaternion_fit(moment, spread_rows, spread_cols)
    corner_value = jnp.sum(jnp.where(corner, msd, 0.0), axis=1, keepdims=True)
    msd = jnp.where(lane < ROWS, msd, 0.0)
    turned = square_tile(msd).T[:ROWS]
    plain_a = jnp.where(diagonal, jnp.where(upper, msd, turned), msd)
    mirrored = jnp.where(row > lane, msd, jnp.where(row == lane, corner_value, turned))
    plain_b = jnp.where(diagonal, mirrored, turned)
    for out, here, there in ((first, plain_a, plain_b), (second, plain_b, plain_a)):
        value = jnp.where(swap, there, here)
        out[...] = value[: ROWS // 2] + pltpu.roll(value[ROWS // 2 :], 64, 1)


def on_device(coords, weights):
    orders, first, second, table = routes()
    frame, atom = lax.axis_index("frame"), lax.axis_index("atom")
    build_flags = jnp.stack([frame // SIDE, two_diagonals(frame % SIDE), atom % 2]).astype(jnp.int32)
    mine = jnp.asarray(np.array(table), jnp.int32)[frame * SIDE + atom]
    fit_flags = jnp.stack([mine & 1, mine >> 2])
    mass = weights[None, :]

    def along(block, distance):
        route = [
            (c * SIDE + (k + distance) % SIDE, c * SIDE + k) for c in range(2) for k in range(SIDE)
        ]
        return lax.ppermute(block, "frame", route)

    def across(block):
        return lax.ppermute(block, "frame", [((f + SIDE) % (2 * SIDE), f) for f in range(2 * SIDE)])

    own = coords.reshape(3 * ROWS, coords.shape[2])
    plus2 = along(own, 2)
    minus3 = along(own, -3)
    plus4 = along(plus2, 2)
    minus4 = along(minus3, -1)
    other2 = across(plus2)
    other3 = across(minus3)
    other4 = across(plus4)

    atoms = own.shape[1]
    smem = pl.BlockSpec(memory_space=pltpu.SMEM)
    vmem = pl.BlockSpec(memory_space=pltpu.VMEM)
    params = pltpu.CompilerParams(vmem_limit_bytes=VMEM_LIMIT)

    def columns_scratch(n):
        return [pltpu.VMEM((n, 256, 3 * atoms), jnp.bfloat16), pltpu.VMEM((n, ROWS, 128), jnp.float32)]

    def cost(pairs):
        return pl.CostEstimate(flops=pairs * 2 * 3 * ROWS * 256 * atoms * 3, bytes_accessed=4_000_000, transcendentals=0)

    def sums_of(n):
        return jax.ShapeDtypeStruct((n, SUM_ROWS, 128), jnp.float32)

    staged = [
        jax.ShapeDtypeStruct((len(STACK) * 3 * ROWS, 3 * atoms), jnp.bfloat16),
        jax.ShapeDtypeStruct((len(STACK), ROWS, 128), jnp.float32),
    ]
    columns = [
        jax.ShapeDtypeStruct((2, 256, 3 * atoms), jnp.bfloat16),
        jax.ShapeDtypeStruct((2, ROWS, 128), jnp.float32),
    ]
    weighted, row_feature, centered, column_feature = pl.pallas_call(
        first_kernel,
        out_shape=staged + columns,
        in_specs=[smem] + [vmem] * 4,
        out_specs=[vmem] * 4,
        compiler_params=params,
        cost_estimate=cost(len(EARLY)),
    )(build_flags, mass, own, plus2, other2)
    more = [
        jax.ShapeDtypeStruct((3, 256, 3 * atoms), jnp.bfloat16),
        jax.ShapeDtypeStruct((3, ROWS, 128), jnp.float32),
    ]
    sums, weighted, row_feature, more_centered, more_feature = pl.pallas_call(
        early_kernel,
        out_shape=[sums_of(2 * CHIPS)] + staged + more,
        in_specs=[smem] + [vmem] * 8,
        out_specs=[vmem] * 5,
        input_output_aliases={7: 1, 8: 2},
        compiler_params=params,
        cost_estimate=cost(len(EARLY)),
    )(build_flags, mass, other3, plus4, minus3, centered, column_feature, weighted, row_feature)
    sums, weighted, row_feature = pl.pallas_call(
        next_kernel,
        out_shape=[sums_of(2 * CHIPS)] + staged,
        in_specs=[smem] + [vmem] * 9,
        out_specs=[vmem] * 3,
        scratch_shapes=columns_scratch(1),
        input_output_aliases={7: 0, 8: 1, 9: 2},
        compiler_params=params,
        cost_estimate=cost(len(NEXT) + 1),
    )(
        build_flags, mass, minus4, centered, column_feature, more_centered, more_feature, sums, weighted, row_feature
    )
    send, keep = pl.pallas_call(
        late_kernel,
        out_shape=[sums_of(CHIPS), sums_of(1)],
        in_specs=[smem] + [vmem] * 5,
        out_specs=[vmem] * 2,
        scratch_shapes=[pltpu.VMEM((2, SUM_ROWS, 128), jnp.float32)] + columns_scratch(1),
        compiler_params=params,
        cost_estimate=cost(len(LATE) + 1),
    )(build_flags, mass, weighted, row_feature, other4, sums)
    taken = lax.ppermute(send, "atom", [(a, a ^ 1) for a in range(SIDE)])
    merged = pl.pallas_call(
        merge_kernel,
        out_shape=sums_of(CHIPS),
        in_specs=[vmem] * 3,
        out_specs=vmem,
        compiler_params=params,
    )(sums, keep, taken)
    groups = [[f * SIDE + 2 * chip + c for chip in orders[f]] for f in range(2 * SIDE) for c in range(2)]
    parts = lax.all_to_all(merged, ("frame", "atom"), 0, 0, axis_index_groups=groups, tiled=True)

    block = jax.ShapeDtypeStruct((ROWS // 2, 128), jnp.float32)
    one, two = pl.pallas_call(
        fit_kernel,
        out_shape=(block, block),
        in_specs=[smem, vmem],
        out_specs=(vmem, vmem),
        compiler_params=params,
    )(fit_flags, parts)
    one = lax.ppermute(one, ("frame", "atom"), list(enumerate(first)))
    two = lax.ppermute(two, ("frame", "atom"), list(enumerate(second)))
    left = jnp.where(mine >> 1 & 1, two, one)
    right = jnp.where(mine >> 1 & 1, one, two)
    upper = jnp.concatenate([left[:, :ROWS], right[:, :ROWS]], axis=1)
    lower = jnp.concatenate([left[:, 64 : 64 + ROWS], right[:, 64 : 64 + ROWS]], axis=1)
    return jnp.concatenate([upper, lower], axis=0)


def solution(mesh):
    placed = (P(None, "frame", "atom"), P("atom"))
    return jax.shard_map(
        on_device, mesh=mesh, in_specs=placed, out_specs=P("frame", "atom"), check_vma=False
    )
```

```python
import functools

import jax
import jax.numpy as jnp
import numpy as np
from jax import lax
from jax.experimental import pallas as pl
from jax.experimental.pallas import tpu as pltpu
from jax.sharding import PartitionSpec as P

NEWTON = 3
ROWS = 48
SIDE = 16
EXACT = lax.Precision.HIGHEST
VMEM_LIMIT = 40 * 1024 * 1024

OWN = (0, 2, 4, -3, -4)
OTHER = (2, 4, -3)
STACK = (3, 0, 2, 4)
EARLY = (
    (3, 1), (0, 1),
    (3, 2), (0, 2),
    (0, 3),
    (3, 5), (0, 5),
    (0, 7), (2, 7),
)
NEXT = ((4, 1), (4, 2), (4, 3), (4, 5), (4, 7))
LATE = ((0, 6), (2, 6))
PAIRS = EARLY + NEXT + LATE
DIAGONAL = PAIRS.index((4, 2))
POSITION = (8, 6, 10, 2, 5, 12, 7, 3, 13, 11, 9, 0, 4, 1, 14, 15)
CHIPS = SIDE // 2
SUM_ROWS = 3 * ROWS + 32


def frame_block(column, z, index):
    if index < len(OWN):
        return column * SIDE + (z + OWN[index]) % SIDE
    return (1 - column) * SIDE + (z + OTHER[index - len(OWN)]) % SIDE


def two_diagonals(z):
    return (z + SIDE - 2) % SIDE < SIDE // 2


def ends_of(column, z, pair):
    p, q = PAIRS[pair]
    if pair == len(PAIRS) - 1 and column == 1:
        p = 4
    a, b = frame_block(column, z, p), frame_block(column, z, q)
    if pair == DIAGONAL and two_diagonals(z):
        return ((a, a), (b, b))
    return ((a, b), (b, a))


def around(a, b, n):
    return min((a - b) % n, (b - a) % n)


def distance(column, z, chip, end):
    to_column, to_z = divmod(end[0], SIDE)
    to_chip = end[1] // 4
    x, to_x = 2 * (chip % 2) + column, 2 * (to_chip % 2) + to_column
    return around(z, to_z, SIDE) + around(chip // 2, to_chip // 2, 4) + around(x, to_x, 4)


def order_of_chips(column, z):
    cost = [[0] * CHIPS for _ in range(CHIPS)]
    for k in range(CHIPS):
        for chip in range(CHIPS):
            for pair in POSITION[2 * k : 2 * k + 2]:
                far = [distance(column, z, chip, end) for end in ends_of(column, z, pair)]
                cost[k][chip] += 2 ** sum(far) + 2 * 4 ** max(far)
    best = {0: (0, ())}
    for k in range(CHIPS):
        later = {}
        for taken, (value, order) in best.items():
            for chip in range(CHIPS):
                if not taken >> chip & 1:
                    entry = (value + cost[k][chip], order + (chip,))
                    key = taken | 1 << chip
                    later[key] = min(later.get(key, entry), entry)
        best = later
    return best[(1 << CHIPS) - 1][1]


def routes():
    orders, ends, diagonal = [], [], []
    for column in range(2):
        for z in range(SIDE):
            order = order_of_chips(column, z)
            orders.append(order)
            for device in range(SIDE):
                pair = POSITION[2 * order.index(device // 2) + device % 2]
                ends.append(ends_of(column, z, pair))
                diagonal.append(int(pair == DIAGONAL and two_diagonals(z)))
    place = lambda end: end[0] * SIDE + end[1] // 2
    at = {}
    for device, pair in enumerate(ends):
        for which, end in enumerate(pair):
            at.setdefault(place(end), []).append((device, which))
    assert len(at) == len(ends) and all(len(v) == 2 for v in at.values())
    swapped = [None] * len(ends)
    for seed in range(len(ends)):
        ring, device, enter = [], seed, 0
        while swapped[device] is None:
            swapped[device] = enter
            ring.append(device)
            node = place(ends[device][1 - enter])
            device, enter = [e for e in at[node] if e != (device, 1 - enter)][0]
        cost = [0, 0]
        for d in ring:
            column, z = divmod(d // SIDE, SIDE)
            far = [distance(column, z, d % SIDE // 2, ends[d][e]) for e in (swapped[d], 1 - swapped[d])]
            cost[0] += 2 ** (far[0] + 2 * far[1])
            cost[1] += 2 ** (far[1] + 2 * far[0])
        if cost[1] < cost[0]:
            for d in ring:
                swapped[d] = 1 - swapped[d]
    first = [place(ends[d][swapped[d]]) for d in range(len(ends))]
    second = [place(ends[d][1 - swapped[d]]) for d in range(len(ends))]
    assert len(set(first)) == len(set(second)) == len(ends)
    half = [0] * len(ends)
    for d in range(len(ends)):
        half[first[d]] = ends[d][swapped[d]][1] % 2
    table = [a + 2 * b + 4 * c for a, b, c in zip(swapped, half, diagonal)]
    return orders, first, second, table


def lookup(step, values):
    out = jnp.int32(values[0])
    for k, value in enumerate(values):
        out = jnp.where(step == k, jnp.int32(value), out)
    return out


def iota(shape, axis):
    return lax.broadcasted_iota(jnp.int32, shape, axis)


def dot_t(a, b):
    return lax.dot_general(a, b, (((1,), (1,)), ((), ())), precision=EXACT, preferred_element_type=jnp.float32)


def product(a, b):
    return lax.dot_general(a, b, (((1,), (1,)), ((), ())), preferred_element_type=jnp.float32)


def halves(x):
    high = x.astype(jnp.bfloat16)
    return high, (x - high.astype(jnp.float32)).astype(jnp.bfloat16)


def stage(x, mass):
    local = jnp.sum(mass)
    mean = jnp.sum(x * mass, axis=1, keepdims=True) / local
    x = x - mean
    wx = x * mass
    square = jnp.sum(wx * x, axis=1, keepdims=True)
    return x, wx, mean, square[:ROWS] + square[ROWS : 2 * ROWS] + square[2 * ROWS :], local


def stage_rows(block, mass, at, core, weighted, feature):
    atoms = block.shape[1]
    _, wx, mean, square, local = stage(block[...], mass)
    high, low = halves(wx)
    for k, part in enumerate((high, high, low)):
        weighted[at * 3 * ROWS : (at + 1) * 3 * ROWS, k * atoms : (k + 1) * atoms] = part
    lane = iota((ROWS, 128), 1) - 8 * core
    out = jnp.where(lane == 51, local, jnp.where(lane == 64 - 8 * core, square, 0.0))
    for c in range(3):
        out = jnp.where(lane == 48 + c, mean[c * ROWS : (c + 1) * ROWS], out)
    feature[at] = out


def stage_columns(block, mass, at, core, centered, feature):
    atoms = block.shape[1]
    x, _, mean, square, _ = stage(block[...], mass)
    high, low = halves(x)
    for k, part in enumerate((high, low, high)):
        centered[at, : 3 * ROWS, k * atoms : (k + 1) * atoms] = part
    lane = iota((ROWS, 128), 1) - 8 * core
    out = jnp.where(lane == 65 - 8 * core, square, 0.0)
    for c in range(3):
        out = jnp.where(lane == 52 + c, mean[c * ROWS : (c + 1) * ROWS], out)
    feature[at] = out


def rest_of(tail):
    tail = jnp.where(iota((3 * ROWS, 128), 1) < 16, tail, 0.0)
    return tail[:ROWS] + pltpu.roll(tail[ROWS : 2 * ROWS], 16, 1) + pltpu.roll(tail[2 * ROWS :], 32, 1)


def packed(rest):
    lane, tail = iota((16, 128), 1), rest[32:]
    low = pltpu.roll(jnp.where(lane < 48, tail, 0.0), 80, 1)
    high = pltpu.roll(jnp.where(lane < 48, 0.0, tail), 32, 1)
    return rest[:32] + jnp.concatenate([low, high], axis=0)


def unpacked(rows):
    tail = jnp.where(iota((16, 128), 1) < 48, pltpu.roll(rows[:16], 48, 1), pltpu.roll(rows[16:], 96, 1))
    return jnp.concatenate([rows, tail], axis=0)


def put_pair(out, pair, core, value, feature):
    k, owner = divmod(POSITION.index(pair), 2)
    at = jnp.where(core == owner, k, CHIPS + k)
    out[at, : 3 * ROWS] = value[:, :128]
    out[at, 3 * ROWS :] = packed(rest_of(value[:, 128:]) + feature)


def put_groups(out, pairs, order, core, weighted, centered, row_feature, column_feature):
    for at, k in enumerate(order):
        group = [pair for pair in pairs if pair[1] == k]
        start = STACK.index(group[0][0])
        assert STACK[start : start + len(group)] == tuple(p for p, _ in group)
        values = product(weighted[start * 3 * ROWS : (start + len(group)) * 3 * ROWS], centered[at])
        for n, pair in enumerate(group):
            value = values[n * 3 * ROWS : (n + 1) * 3 * ROWS]
            put_pair(out, PAIRS.index(pair), core, value, row_feature[start + n] + column_feature[at])


def first_kernel(flags, mass_ref, own, plus2, other2, weighted, row_feature, centered, column_feature):
    core = flags[2]
    mass = mass_ref[...].astype(jnp.float32)
    stage_rows(own, mass, STACK.index(0), core, weighted, row_feature)
    for at, block in enumerate((plus2, other2)):
        stage_columns(block, mass, at, core, centered, column_feature)


def early_kernel(
    flags, mass_ref, other3, plus4, minus3, first_centered, first_feature, _, __,
    out, weighted, row_feature, centered, column_feature,
):
    core = flags[2]
    mass = mass_ref[...].astype(jnp.float32)
    for at, block in enumerate((plus4, minus3, other3)):
        stage_columns(block, mass, at, core, centered, column_feature)
    for k, block in ((3, minus3), (2, plus4)):
        stage_rows(block, mass, STACK.index(k), core, weighted, row_feature)
    put_groups(out, EARLY, (1, 5), core, weighted, first_centered, row_feature, first_feature)
    put_groups(out, EARLY, (2, 3, 7), core, weighted, centered, row_feature, column_feature)


def next_kernel(
    flags, mass_ref, minus4, first_centered, first_feature, centered, column_feature, _, __, ___,
    out, weighted, row_feature, own_centered, own_feature,
):
    core = flags[2]
    mass = mass_ref[...].astype(jnp.float32)
    stage_rows(minus4, mass, STACK.index(4), core, weighted, row_feature)
    put_groups(out, NEXT, (1, 5), core, weighted, first_centered, row_feature, first_feature)
    put_groups(out, NEXT, (2, 3, 7), core, weighted, centered, row_feature, column_feature)

    @pl.when(flags[1] == 1)
    def _():
        stage_columns(minus4, mass, 0, core, own_centered, own_feature)
        p, q, last = STACK.index(4), STACK.index(2), 0
        upper = product(weighted[p * 3 * ROWS : (p + 1) * 3 * ROWS], own_centered[0])
        lower = product(weighted[q * 3 * ROWS : (q + 1) * 3 * ROWS], centered[last])
        i, j = iota((3 * ROWS, 256), 0) % ROWS, iota((3 * ROWS, 256), 1) % ROWS
        at = iota((ROWS, 256), 1)
        on = jnp.where((i == j) & (iota((3 * ROWS, 256), 1) < 3 * ROWS), lower, 0.0)
        lane = iota((ROWS, 128), 1)
        ends = row_feature[p] + column_feature[last]
        for c in range(3):
            mine = on[c * ROWS : (c + 1) * ROWS]
            for d in range(3):
                inside = (at >= d * ROWS) & (at < (d + 1) * ROWS)
                value = jnp.sum(jnp.where(inside, mine, 0.0), axis=1, keepdims=True)
                ends = jnp.where(lane == 66 + 3 * c + d, value, ends)
        put_pair(out, DIAGONAL, core, jnp.where(i <= j, upper, lower), ends)


def late_kernel(flags, mass_ref, weighted, row_feature, other4, sums, send, keep, last, centered, column_feature):
    core = flags[2]
    mass = mass_ref[...].astype(jnp.float32)
    stage_columns(other4, mass, 0, core, centered, column_feature)
    values = product(weighted[3 * ROWS :], centered[0])
    other = flags[0] == 1
    for n in range(2):
        rows = values[: 3 * ROWS] if n == 0 else jnp.where(other, values[6 * ROWS :], values[3 * ROWS : 6 * ROWS])
        feature = row_feature[1] if n == 0 else jnp.where(other, row_feature[3], row_feature[2])
        at = jnp.where(core == n, 0, 1)
        last[at, : 3 * ROWS] = rows[:, :128]
        last[at, 3 * ROWS :] = packed(rest_of(rows[:, 128:]) + feature + column_feature[0])
    keep[0] = last[0]
    send[CHIPS - 1] = last[1]
    send[: CHIPS - 1] = sums[CHIPS : 2 * CHIPS - 1]


def merge_kernel(sums, keep, taken, out):
    out[: CHIPS - 1] = sums[: CHIPS - 1] + taken[: CHIPS - 1]
    out[CHIPS - 1] = keep[0] + taken[CHIPS - 1]


def det_four(rows):
    a00, a01, a02, a03 = rows[0]
    a10, a11, a12, a13 = rows[1]
    a20, a21, a22, a23 = rows[2]
    a30, a31, a32, a33 = rows[3]
    s0 = a00 * a11 - a10 * a01
    s1 = a00 * a12 - a10 * a02
    s2 = a00 * a13 - a10 * a03
    s3 = a01 * a12 - a11 * a02
    s4 = a01 * a13 - a11 * a03
    s5 = a02 * a13 - a12 * a03
    t5 = a22 * a33 - a32 * a23
    t4 = a21 * a33 - a31 * a23
    t3 = a21 * a32 - a31 * a22
    t2 = a20 * a33 - a30 * a23
    t1 = a20 * a32 - a30 * a22
    t0 = a20 * a31 - a30 * a21
    return s0 * t5 - s1 * t4 + s2 * t3 + s3 * t2 - s4 * t1 + s5 * t0


def quaternion_fit(moment, spread_rows, spread_cols):
    sxx, sxy, sxz, syx, syy, syz, szx, szy, szz = moment
    coef_two = -2.0 * sum(m * m for m in moment)
    det_three = (
        sxx * (syy * szz - syz * szy)
        - sxy * (syx * szz - syz * szx)
        + sxz * (syx * szy - syy * szx)
    )
    coef_one = -8.0 * det_three
    rows = [
        [sxx + syy + szz, syz - szy, szx - sxz, sxy - syx],
        [syz - szy, sxx - syy - szz, sxy + syx, szx + sxz],
        [szx - sxz, sxy + syx, -sxx + syy - szz, syz + szy],
        [sxy - syx, szx + sxz, syz + szy, -sxx - syy + szz],
    ]
    coef_zero = det_four(rows)
    lam = 0.5 * (spread_rows + spread_cols)
    for turn in range(NEWTON):
        square = lam * lam
        value = (square + coef_two) * square + coef_one * lam + coef_zero
        slope = 4.0 * square * lam + 2.0 * coef_two * lam + coef_one
        lam = lam - value / slope
    return spread_rows + spread_cols - 2.0 * lam


def square_tile(x):
    return jnp.concatenate([x, jnp.zeros((128 - x.shape[0], 128), jnp.float32)], axis=0)


def fit_kernel(flags, parts, first, second):
    diagonal, swap = flags[1] == 1, flags[0] == 1
    total = parts[0]
    for a in range(1, CHIPS):
        total = total + parts[a]
    lane, row = iota((ROWS, 128), 1), iota((ROWS, 128), 0)
    rest = unpacked(total[3 * ROWS :])

    gathered = jnp.zeros((ROWS, 128), jnp.float32)
    for a in range(CHIPS):
        tile = jnp.where((lane >= 48) & (lane < 64), unpacked(parts[a, 3 * ROWS :]), 0.0)
        gathered = gathered + pltpu.roll(tile, (16 * a - 48) % 128, 1)

    sender = lane % 8 == 0

    def per_sender(which):
        return jnp.where(sender, pltpu.roll(gathered, (128 - which) % 128, 1), 0.0)

    mass = per_sender(3)
    whole = jnp.sum(mass, axis=1, keepdims=True)

    def offsets(base):
        out = []
        for c in range(3):
            mean = per_sender(base + c)
            centroid = jnp.sum(mass * mean, axis=1, keepdims=True) / whole
            out.append(jnp.where(sender, mean - centroid, 0.0))
        return out

    off_p, off_q = offsets(0), offsets(4)

    def spread(off, at):
        within = jnp.sum(jnp.where(lane == at, rest, 0.0), axis=1, keepdims=True)
        between = jnp.sum(mass * sum(o * o for o in off), axis=1, keepdims=True)
        return (within + between) / whole

    spread_p, spread_q = spread(off_p, 64), spread(off_q, 65)

    def as_row(column):
        return jnp.sum(jnp.where(row == lane, column, 0.0), axis=0, keepdims=True)

    upper = row <= lane
    corner = lane == ROWS
    row_p, row_q = as_row(spread_p), as_row(spread_q)
    spread_rows = jnp.where(upper, spread_p, jnp.where(diagonal, spread_q, spread_p))
    spread_cols = jnp.where(upper, jnp.where(diagonal, row_p, row_q), row_q)
    spread_rows = jnp.where(corner, spread_q, spread_rows)
    spread_cols = jnp.where(corner, spread_q, spread_cols)

    def parts_of(blocks, first):
        high, low = halves(jnp.concatenate(blocks, axis=0))
        return jnp.concatenate([high, high, low] if first else [high, low, high], axis=1)

    up_rows = parts_of([mass * p for p in off_p], True)
    low_rows = parts_of([mass * jnp.where(diagonal, q, p) for p, q in zip(off_p, off_q)], True)
    moment = []
    between = []
    for d in range(3):
        up = product(up_rows, parts_of([square_tile(jnp.where(diagonal, off_p[d], off_q[d]))], False))
        low = product(low_rows, parts_of([square_tile(off_q[d])], False))
        between.append((up, low))
    for c in range(3):
        main = total[c * ROWS : (c + 1) * ROWS]
        tail = pltpu.roll(rest, (32 - 16 * c) % 128, 1)
        shifted = [main, pltpu.roll(main, 128 - 48, 1), jnp.where(lane < 32, pltpu.roll(main, 128 - 96, 1), tail)]
        for d in range(3):
            up, low = (b[c * ROWS : (c + 1) * ROWS] for b in between[d])
            value = shifted[d] + jnp.where(upper, up, low)
            end = jnp.sum(jnp.where(lane == 66 + 3 * c + d, rest, 0.0), axis=1, keepdims=True)
            end = end + jnp.sum(mass * off_q[c] * off_q[d], axis=1, keepdims=True)
            moment.append(jnp.where(corner, end, value) / whole)
    msd = quaternion_fit(moment, spread_rows, spread_cols)
    corner_value = jnp.sum(jnp.where(corner, msd, 0.0), axis=1, keepdims=True)
    msd = jnp.where(lane < ROWS, msd, 0.0)
    turned = square_tile(msd).T[:ROWS]
    plain_a = jnp.where(diagonal, jnp.where(upper, msd, turned), msd)
    mirrored = jnp.where(row > lane, msd, jnp.where(row == lane, corner_value, turned))
    plain_b = jnp.where(diagonal, mirrored, turned)
    for out, here, there in ((first, plain_a, plain_b), (second, plain_b, plain_a)):
        value = jnp.where(swap, there, here)
        out[...] = value[: ROWS // 2] + pltpu.roll(value[ROWS // 2 :], 64, 1)


def on_device(coords, weights):
    orders, first, second, table = routes()
    frame, atom = lax.axis_index("frame"), lax.axis_index("atom")
    build_flags = jnp.stack([frame // SIDE, two_diagonals(frame % SIDE), atom % 2]).astype(jnp.int32)
    mine = jnp.asarray(np.array(table), jnp.int32)[frame * SIDE + atom]
    fit_flags = jnp.stack([mine & 1, mine >> 2])
    mass = weights[None, :]

    def along(block, distance):
        route = [
            (c * SIDE + (k + distance) % SIDE, c * SIDE + k) for c in range(2) for k in range(SIDE)
        ]
        return lax.ppermute(block, "frame", route)

    def across(block):
        return lax.ppermute(block, "frame", [((f + SIDE) % (2 * SIDE), f) for f in range(2 * SIDE)])

    own = coords.reshape(3 * ROWS, coords.shape[2])
    plus2 = along(own, 2)
    minus3 = along(own, -3)
    plus4 = along(plus2, 2)
    minus4 = along(minus3, -1)
    other2 = across(plus2)
    other3 = across(minus3)
    other4 = across(plus4)

    atoms = own.shape[1]
    smem = pl.BlockSpec(memory_space=pltpu.SMEM)
    vmem = pl.BlockSpec(memory_space=pltpu.VMEM)
    params = pltpu.CompilerParams(vmem_limit_bytes=VMEM_LIMIT)

    def columns_scratch(n):
        return [pltpu.VMEM((n, 256, 3 * atoms), jnp.bfloat16), pltpu.VMEM((n, ROWS, 128), jnp.float32)]

    def cost(pairs):
        return pl.CostEstimate(flops=pairs * 2 * 3 * ROWS * 256 * atoms * 3, bytes_accessed=4_000_000, transcendentals=0)

    def sums_of(n):
        return jax.ShapeDtypeStruct((n, SUM_ROWS, 128), jnp.float32)

    staged = [
        jax.ShapeDtypeStruct((len(STACK) * 3 * ROWS, 3 * atoms), jnp.bfloat16),
        jax.ShapeDtypeStruct((len(STACK), ROWS, 128), jnp.float32),
    ]
    columns = [
        jax.ShapeDtypeStruct((2, 256, 3 * atoms), jnp.bfloat16),
        jax.ShapeDtypeStruct((2, ROWS, 128), jnp.float32),
    ]
    weighted, row_feature, centered, column_feature = pl.pallas_call(
        first_kernel,
        out_shape=staged + columns,
        in_specs=[smem] + [vmem] * 4,
        out_specs=[vmem] * 4,
        compiler_params=params,
        cost_estimate=cost(len(EARLY)),
    )(build_flags, mass, own, plus2, other2)
    more = [
        jax.ShapeDtypeStruct((3, 256, 3 * atoms), jnp.bfloat16),
        jax.ShapeDtypeStruct((3, ROWS, 128), jnp.float32),
    ]
    sums, weighted, row_feature, more_centered, more_feature = pl.pallas_call(
        early_kernel,
        out_shape=[sums_of(2 * CHIPS)] + staged + more,
        in_specs=[smem] + [vmem] * 8,
        out_specs=[vmem] * 5,
        input_output_aliases={7: 1, 8: 2},
        compiler_params=params,
        cost_estimate=cost(len(EARLY)),
    )(build_flags, mass, other3, plus4, minus3, centered, column_feature, weighted, row_feature)
    sums, weighted, row_feature = pl.pallas_call(
        next_kernel,
        out_shape=[sums_of(2 * CHIPS)] + staged,
        in_specs=[smem] + [vmem] * 9,
        out_specs=[vmem] * 3,
        scratch_shapes=columns_scratch(1),
        input_output_aliases={7: 0, 8: 1, 9: 2},
        compiler_params=params,
        cost_estimate=cost(len(NEXT) + 1),
    )(
        build_flags, mass, minus4, centered, column_feature, more_centered, more_feature, sums, weighted, row_feature
    )
    send, keep = pl.pallas_call(
        late_kernel,
        out_shape=[sums_of(CHIPS), sums_of(1)],
        in_specs=[smem] + [vmem] * 5,
        out_specs=[vmem] * 2,
        scratch_shapes=[pltpu.VMEM((2, SUM_ROWS, 128), jnp.float32)] + columns_scratch(1),
        compiler_params=params,
        cost_estimate=cost(len(LATE) + 1),
    )(build_flags, mass, weighted, row_feature, other4, sums)
    taken = lax.ppermute(send, "atom", [(a, a ^ 1) for a in range(SIDE)])
    merged = pl.pallas_call(
        merge_kernel,
        out_shape=sums_of(CHIPS),
        in_specs=[vmem] * 3,
        out_specs=vmem,
        compiler_params=params,
    )(sums, keep, taken)
    groups = [[f * SIDE + 2 * chip + c for chip in orders[f]] for f in range(2 * SIDE) for c in range(2)]
    parts = lax.all_to_all(merged, ("frame", "atom"), 0, 0, axis_index_groups=groups, tiled=True)

    block = jax.ShapeDtypeStruct((ROWS // 2, 128), jnp.float32)
    one, two = pl.pallas_call(
        fit_kernel,
        out_shape=(block, block),
        in_specs=[smem, vmem],
        out_specs=(vmem, vmem),
        compiler_params=params,
    )(fit_flags, parts)
    one = lax.ppermute(one, ("frame", "atom"), list(enumerate(first)))
    two = lax.ppermute(two, ("frame", "atom"), list(enumerate(second)))
    left = jnp.where(mine >> 1 & 1, two, one)
    right = jnp.where(mine >> 1 & 1, one, two)
    upper = jnp.concatenate([left[:, :ROWS], right[:, :ROWS]], axis=1)
    lower = jnp.concatenate([left[:, 64 : 64 + ROWS], right[:, 64 : 64 + ROWS]], axis=1)
    return jnp.concatenate([upper, lower], axis=0)


def solution(mesh):
    placed = (P(None, "frame", "atom"), P("atom"))
    return jax.shard_map(
        on_device, mesh=mesh, in_specs=placed, out_specs=P("frame", "atom"), check_vma=False
    )
```
